32 devices in a mesh: tm: 16 (over z, x, core), space: 2 (over y).
Axes of the slice: x: 2, y: 2, z: 4, core: 2. Of those that a mesh axis runs over, the one named last changes fastest.
Arguments:
- observations: bfloat16 [4096, 16, 2, 512], P(None, 'tm', 'space'), may hold values from -6 to 6
- pod_basis: bfloat16 [16, 2, 512, 1024], P(None, 'space'), may hold values from -0.046875 to 0.046875
- decay: float32 [4096, 1024], P('tm', 'space'), may hold values from 0 to 1
- step_mask: int32 [4096], P('tm'), may hold values 0 or 1
- process_var: float32 [1024], P('space'), may hold values from 0.00024414062 to 1
- obs_var: float32 [1024], P('space'), may hold values from 1 to 256
- prior_mean: float32 [1024], P('space'), may hold values from -6 to 6
- prior_var: float32 [1024], P('space'), may hold values from 0.5 to 4
Outputs:
- coefficients: float32 [4096, 1024], P('tm', 'space')
- filtered_mean: float32 [4096, 1024], P('tm', 'space')
- smoothed_mean: float32 [4096, 1024], P('tm', 'space')
- log_variance: float32 [4096, 1024], P('tm', 'space')
The draws below stay inside these ranges and needn't reach their ends.
All inputs are finite; a program needn't handle non-finite values. No bound on the sum of `step_mask` on one device may be relied on, other than what follows from the above.
Results may differ from the reference program's by a relative error of at most 0.0003.
Values may be sent and summed in bfloat16 or wider, within the bound.
No kernel may reach another device: no remote copies, remote signals or barrier semaphores. Data moves between devices by JAX's collectives and lax.ppermute only.
A program may use at most 256 MiB of HBM per device.

```python
import math
import jax
import jax.numpy as jnp
from jax import lax

K = 1024
CB = 512
STEPS = 4096
GRID_T = 16
GRID_S = 2
CELLS = 16384


def draw_decay(key, part):
    key_rate, key_rough, key_place, key_loss = jax.random.split(key, 4)
    low_rate = math.log(0.5 / STEPS)
    high_rate = math.log(1.0 / 30.0)
    rates = jnp.exp(jax.random.uniform(key_rate, (K,), jnp.float32, low_rate, high_rate))
    rough = jnp.exp(jax.random.uniform(key_rough, (STEPS, K), jnp.float32, math.log(0.5), math.log(2.0)))
    places = jax.random.randint(key_place, (3,), 0, STEPS)
    struck = jnp.any(jnp.arange(STEPS)[:, None] == places[None, :], axis=1)
    losses = jax.random.uniform(key_loss, (STEPS, K), jnp.float32, 0.5, 0.8)
    factors = jnp.exp(-rates[None, :] * rough) * jnp.where(struck[:, None], losses, 1.0)
    return factors.astype(jnp.float32)


def touch_ends(drawn, stream_key, smallest, high):
    dims = drawn.shape
    place = [jax.random.randint(jax.random.fold_in(stream_key, axis), (), 0, dims[axis]) for axis in range(len(dims))]
    drawn = drawn.at[tuple(place)].set(smallest)
    longest = dims.index(max(dims))
    place[longest] = (place[longest] + 1) % dims[longest]
    return drawn.at[tuple(place)].set(high)


def spiked(entries, rng, source, target, parts, factor):
    def block_of(position):
        return (jnp.arange(entries.shape[position]) // (entries.shape[position] // parts)).reshape((-1,) + (1,) * (entries.ndim - 1 - position))

    near = jax.random.permutation(rng, parts)[block_of(target)]
    second = (block_of(target) + parts // 2) % parts
    return jnp.where((block_of(source) == near) | (block_of(source) == second), factor * entries, entries)


def block_levels(key, shape, cuts, low, top_value):
    gain, own = 1.0, jax.random.fold_in(key, 6)
    for dim, parts in cuts:
        steps = jnp.exp(jax.random.uniform(jax.random.fold_in(own, dim), (parts,), jnp.float32, low / len(cuts), top_value / len(cuts)))
        gain = gain * jnp.repeat(steps, shape[dim] // parts).reshape([-1 if axis == dim else 1 for axis in range(len(shape))])
    return gain


def bell_draw(stream_key, shape, deviation, limit, cuts=(), kind=jnp.bfloat16):
    array = deviation * jax.random.normal(stream_key, shape, jnp.float32)
    if cuts:
        array = array * block_levels(stream_key, shape, cuts, -0.22, 0.18)
    return jnp.clip(array, -limit, limit).astype(kind)


def gaussian_with(own_key, extent, spread, most, cuts, heavy, dtype=jnp.bfloat16):
    array = spread * jax.random.normal(own_key, extent, jnp.float32)
    if cuts:
        array = array * block_levels(own_key, extent, cuts, -0.22, 0.18)
    return jnp.clip(spiked(array, jax.random.fold_in(own_key, 3), *heavy), -most, most).astype(dtype)


def setup_inputs(seed: int = 0) -> dict:
    seeds = jax.random.split(jax.random.key(seed), 9)
    return {
        "observations": gaussian_with(seeds[0], (STEPS, GRID_T, GRID_S, CB), 1.0, 6.0, ((1, 16), (2, 2)), (1, 0, 16, 2.0)),
        "pod_basis": bell_draw(seeds[1], (GRID_T, GRID_S, CB, K), CELLS ** -0.5, 0.046875, ((1, 2),)),
        "decay": draw_decay(jax.random.fold_in(seeds[8], 71), 0),
        "step_mask": touch_ends((jax.random.randint(seeds[3], (STEPS,), 0, 2) < 1).astype(jnp.int32), jax.random.fold_in(seeds[3], 1), 0, 1),
        "process_var": jnp.clip(jnp.exp(math.log(1.0) - 8.317766 * jax.random.uniform(seeds[4], (K,), jnp.float32) ** block_levels(seeds[4], (K,), ((0, 2),), -0.2, 0.2)), 0.00024414062, 1.0),
        "obs_var": jnp.clip(jnp.exp(math.log(256.0) - 5.5451774 * jax.random.uniform(seeds[5], (K,), jnp.float32) ** block_levels(seeds[5], (K,), ((0, 2),), -0.2, 0.2)), 1.0, 256.0),
        "prior_mean": bell_draw(seeds[6], (K,), 1.0, 6.0, ((0, 2),), jnp.float32),
        "prior_var": jnp.clip(jnp.exp(math.log(4.0) - 2.0794415 * jax.random.uniform(seeds[7], (K,), jnp.float32) ** block_levels(seeds[7], (K,), ((0, 2),), -0.2, 0.2)), 0.5, 4.0),
    }


def reference(observations, pod_basis, decay, step_mask, process_var, obs_var, prior_mean, prior_var):
    flat_obs = observations.reshape(observations.shape[0], -1)
    flat_pod = pod_basis.reshape(-1, pod_basis.shape[-1])
    coefficients = jnp.dot(flat_obs, flat_pod, preferred_element_type=jnp.float32)
    observed = step_mask.astype(jnp.float32)

    def update(pred_mean, pred_var, target, flag):
        denominator = pred_var + obs_var
        kalman_gain = flag * pred_var / denominator
        retain = (obs_var + (1.0 - flag) * pred_var) / denominator
        return pred_mean + kalman_gain * (target - pred_mean), retain * pred_var

    start_mean, start_var = update(prior_mean, prior_var, coefficients[0], observed[0])

    def forward(carry, inputs):
        last_mean, last_var = carry
        factor, target, flag = inputs
        new_mean, new_var = update(factor * last_mean, factor * factor * last_var + process_var, target, flag)
        return (new_mean, new_var), (new_mean, new_var)

    _, (means, variances) = lax.scan(forward, (start_mean, start_var), (decay[1:], coefficients[1:], observed[1:]))
    filtered_mean = jnp.concatenate([start_mean[None], means], 0)
    filtered_var = jnp.concatenate([start_var[None], variances], 0)

    def backward(carry, inputs):
        later_mean, later_var = carry
        here_mean, here_var, factor = inputs
        predicted = factor * factor * here_var + process_var
        smoother_gain = here_var * factor / predicted
        new_mean = here_mean + smoother_gain * (later_mean - factor * here_mean)
        new_var = smoother_gain * smoother_gain * later_var + here_var * process_var / predicted
        return (new_mean, new_var), (new_mean, new_var)

    _, (smooth_means, smooth_vars) = lax.scan(backward, (filtered_mean[-1], filtered_var[-1]), (filtered_mean[:-1], filtered_var[:-1], decay[1:]), reverse=True)
    smoothed_mean = jnp.concatenate([smooth_means, filtered_mean[-1:]], 0)
    smoothed_var = jnp.concatenate([smooth_vars, filtered_var[-1:]], 0)
    return coefficients, filtered_mean, smoothed_mean, jnp.log(smoothed_var)
```

```python
import functools

import jax
import jax.numpy as jnp
from jax import lax
from jax.experimental import pallas as pl
from jax.experimental.pallas import tpu as pltpu
from jax.sharding import PartitionSpec as P

CHUNK = 16
LANES = 128
F32 = jnp.float32
LIMIT = 48 * 1024 * 1024


def rotate(block, axis, turn, count, group, outer):
    route = []
    for i in range(count):
        low, high = i % group, i // group
        if outer:
            target = ((high + turn) % (count // group)) * group + low
        else:
            target = high * group + (low + turn) % group
        route.append((i, target))
    return lax.ppermute(block, axis, route)


def inner_size(count):
    group = 1
    while group * group < count:
        group *= 2
    return group if count % group == 0 else count


def gather_rows(rows, axis):
    count = lax.axis_size(axis)
    group = inner_size(count)
    near = jnp.stack([rows] + [rotate(rows, axis, s, count, group, False) for s in range(1, group)])
    far = [near] + [rotate(near, axis, s, count, group, True) for s in range(1, count // group)]
    return jnp.concatenate(far, 0)


def place(me, j, count):
    group = inner_size(count)
    rounds = count // group
    high = lax.rem(me // group - j // group + rounds, rounds)
    low = lax.rem(lax.rem(me, group) - j % group + group, group)
    return high * group + low


def lanes(ref, strip_ref):
    for m in range(strip_ref.shape[0]):
        strip_ref[m] = ref[:, m * LANES : (m + 1) * LANES]


def unlanes(strip_ref, ref):
    for m in range(strip_ref.shape[0]):
        ref[:, m * LANES : (m + 1) * LANES] = strip_ref[m]


def chunk_rows(strip_ref, i, chunks):
    rows = pl.ds(i, chunks, stride=CHUNK)
    return jnp.concatenate([strip_ref[m, rows, :] for m in range(strip_ref.shape[0])], 1)


def put_rows(strip_ref, i, chunks, value):
    rows = pl.ds(i, chunks, stride=CHUNK)
    for m in range(strip_ref.shape[0]):
        strip_ref[m, rows, :] = value[:, m * LANES : (m + 1) * LANES]


def opened(me_ref, shape):
    rows = lax.broadcasted_iota(jnp.int32, shape, 0)
    return jnp.logical_and(rows == 0, me_ref[0] == 0)


def totals_kernel(me_ref, decay_in, seen_in, q_ref, r_ref, chunk_ref, block_ref, decay_ref, seen_ref):
    steps, modes = decay_in.shape
    lanes(decay_in, decay_ref)
    lanes(seen_in, seen_ref)
    chunks = steps // CHUNK
    shape = (chunks, modes)
    q = jnp.broadcast_to(q_ref[...], shape)
    r = jnp.broadcast_to(r_ref[...], shape)
    first = opened(me_ref, shape)
    lead = spread = weight = None
    for i in range(CHUNK):
        d = chunk_rows(decay_ref, i, chunks)
        seen = chunk_rows(seen_ref, i, chunks) > 0.5
        base = q
        if i == 0:
            d = jnp.where(first, 1.0, d)
            base = jnp.where(first, 0.0, q)
        inverse = 1.0 / (base + r)
        retain = jnp.where(seen, r * inverse, 1.0)
        step_lead = retain * d
        step_spread = retain * base
        step_weight = jnp.where(seen, d * d * inverse, 0.0)
        if i == 0:
            lead, spread, weight = step_lead, step_spread, step_weight
        else:
            factor = 1.0 / (1.0 + spread * step_weight)
            spread = step_lead * step_lead * factor * spread + step_spread
            weight = lead * lead * factor * step_weight + weight
            lead = step_lead * factor * lead
    chunk_ref[0] = lead
    chunk_ref[1] = spread
    chunk_ref[2] = weight
    lead, spread, weight = (chunk_ref[k, 0:1, :] for k in range(3))
    for c in range(1, chunks):
        step_lead, step_spread, step_weight = (chunk_ref[k, c : c + 1, :] for k in range(3))
        factor = 1.0 / (1.0 + spread * step_weight)
        spread = step_lead * step_lead * factor * spread + step_spread
        weight = lead * lead * factor * step_weight + weight
        lead = step_lead * factor * lead
    block_ref[0:1, :] = lead
    block_ref[1:2, :] = spread
    block_ref[2:3, :] = weight


def gains_kernel(
    count, me_ref, decay_in, next_ref, seen_in, q_ref, r_ref, prior_ref, chunk_ref, blocks_ref,
    a_ref, b_ref, g_ref, h_ref, whole_ref, edge_ref, block_ref, enter_ref, full_ref, var_ref, decay_ref, seen_ref,
):
    steps, modes = decay_in.shape
    lanes(decay_in, decay_ref)
    lanes(seen_in, seen_ref)
    chunks = steps // CHUNK
    shape = (chunks, modes)
    me = me_ref[0]
    q = jnp.broadcast_to(q_ref[...], shape)
    r = jnp.broadcast_to(r_ref[...], shape)
    first = opened(me_ref, shape)

    v = prior_ref[...]
    for j in range(count - 1):
        at = place(me, j, count)
        lead, spread, weight = (blocks_ref[at, k : k + 1, :] for k in range(3))
        longer = spread + lead * lead * v / (1.0 + weight * v)
        v = jnp.where(j < me, longer, v)
    for c in range(chunks):
        enter_ref[c : c + 1, :] = v
        lead, spread, weight = (chunk_ref[k, c : c + 1, :] for k in range(3))
        v = spread + lead * lead * v / (1.0 + weight * v)

    v = enter_ref[...]
    run = None
    for i in range(CHUNK):
        d = chunk_rows(decay_ref, i, chunks)
        seen = chunk_rows(seen_ref, i, chunks) > 0.5
        base = q
        if i == 0:
            d = jnp.where(first, 1.0, d)
            base = jnp.where(first, 0.0, q)
        ahead = d * d * v + base
        inverse = 1.0 / (ahead + r)
        retain = jnp.where(seen, r * inverse, 1.0)
        v = retain * ahead
        a = retain * d
        run = a if i == 0 else a * run
        a_ref[i] = a
        b_ref[i] = jnp.where(seen, ahead * inverse, 0.0)
        var_ref[i] = v
        full_ref[i] = run
    edge_ref[0] = run
    carry = jnp.ones((1, modes), F32)
    for c in range(chunks):
        enter_ref[c : c + 1, :] = carry
        carry = carry * edge_ref[0, c : c + 1, :]
    block_ref[0:1, :] = carry
    enter = enter_ref[...]

    enter_ref[chunks - 1 : chunks, :] = next_ref[...]
    if chunks > 1:
        for c in range(chunks - 1):
            enter_ref[c : c + 1, :] = decay_in[(c + 1) * CHUNK : (c + 1) * CHUNK + 1, :]
    last_next = enter_ref[...]
    gain_run = spread_run = reply_run = None
    for i in reversed(range(CHUNK)):
        n = last_next if i == CHUNK - 1 else chunk_rows(decay_ref, i + 1, chunks)
        v = var_ref[i]
        h = q / (n * n * v + q)
        g = v * n / (n * n * v + q)
        a_full = full_ref[i] * enter
        whole_ref[0, i] = a_full
        if i == CHUNK - 1:
            gain_run, spread_run, reply_run = g, v * h, h * a_full
        else:
            gain_run, spread_run, reply_run = (
                g * gain_run,
                g * g * spread_run + v * h,
                g * reply_run + h * a_full,
            )
        g_ref[i] = g
        h_ref[i] = h
        whole_ref[1, i] = gain_run
        whole_ref[2, i] = spread_run
        whole_ref[3, i] = reply_run
    edge_ref[1] = gain_run
    edge_ref[2] = spread_run
    edge_ref[3] = reply_run
    gain = jnp.ones((1, modes), F32)
    spread = jnp.zeros((1, modes), F32)
    reply = jnp.zeros((1, modes), F32)
    for c in reversed(range(chunks)):
        full_ref[0, c : c + 1, :] = gain
        full_ref[1, c : c + 1, :] = spread
        full_ref[2, c : c + 1, :] = reply
        step = edge_ref[1, c : c + 1, :]
        spread = edge_ref[2, c : c + 1, :] + step * step * spread
        reply = edge_ref[3, c : c + 1, :] + step * reply
        gain = step * gain
    block_ref[1:2, :] = gain
    block_ref[2:3, :] = spread
    block_ref[3:4, :] = reply
    gain = full_ref[0]
    spread = full_ref[1]
    reply = full_ref[2]
    for i in range(CHUNK):
        run = whole_ref[1, i]
        whole_ref[2, i] = whole_ref[2, i] + run * run * spread
        whole_ref[3, i] = whole_ref[3, i] + run * reply
        whole_ref[1, i] = run * gain


def variance_kernel(count, me_ref, whole_ref, blocks_ref, out_ref, strip_ref):
    steps, modes = out_ref.shape
    chunks = steps // CHUNK
    me = me_ref[0]
    later = jnp.zeros((1, modes), F32)
    for j in reversed(range(1, count)):
        at = place(me, j, count)
        gain = blocks_ref[at, 1:2, :]
        longer = blocks_ref[at, 2:3, :] + gain * gain * later
        later = jnp.where(j > me, longer, later)
    later = jnp.broadcast_to(later, (chunks, modes))
    for i in range(CHUNK):
        gain = whole_ref[1, i]
        put_rows(strip_ref, i, chunks, jnp.log(whole_ref[2, i] + gain * gain * later))
    unlanes(strip_ref, out_ref)


def means_kernel(parts, *refs):
    part_refs = refs[:parts]
    a_ref, b_ref, g_ref, h_ref, edge_ref = refs[parts : parts + 5]
    coef_ref, mean_ref, smooth_ref, block_ref, enter_ref, strip_ref = refs[parts + 5 :]
    steps, modes = coef_ref.shape
    chunks = steps // CHUNK
    c = part_refs[0][...]
    for ref in part_refs[1:]:
        c = c + ref[...]
    coef_ref[...] = c
    lanes(coef_ref, strip_ref)
    f = None
    for i in range(CHUNK):
        push = b_ref[i] * chunk_rows(strip_ref, i, chunks)
        mean_ref[i] = push
        f = push if i == 0 else a_ref[i] * f + push
    smooth_ref[0] = f
    carry = jnp.zeros((1, modes), F32)
    for c in range(chunks):
        enter_ref[c : c + 1, :] = carry
        carry = smooth_ref[0, c : c + 1, :] + edge_ref[0, c : c + 1, :] * carry
    block_ref[0:1, :] = carry
    f = enter_ref[...]
    for i in range(CHUNK):
        f = a_ref[i] * f + mean_ref[i]
        mean_ref[i] = f
    s = None
    for i in reversed(range(CHUNK)):
        push = h_ref[i] * mean_ref[i]
        s = push if i == CHUNK - 1 else g_ref[i] * s + push
    smooth_ref[0] = s
    carry = jnp.zeros((1, modes), F32)
    for c in reversed(range(chunks)):
        enter_ref[c : c + 1, :] = carry
        carry = smooth_ref[0, c : c + 1, :] + edge_ref[1, c : c + 1, :] * carry
    block_ref[1:2, :] = carry
    s = enter_ref[...]
    for i in reversed(range(CHUNK)):
        s = g_ref[i] * s + h_ref[i] * mean_ref[i]
        smooth_ref[i] = s


def finish_kernel(count, me_ref, prior_ref, whole_ref, edges_ref, blocks_ref, mean_ref, smooth_ref, out_mean_ref, out_smooth_ref, enter_ref, mean_strip_ref, smooth_strip_ref):
    steps, modes = out_mean_ref.shape
    chunks = steps // CHUNK
    me = me_ref[0]
    mean = prior_ref[...]
    mine = mean
    for j in range(count):
        enter_ref[j : j + 1, :] = mean
        mine = jnp.where(j == me, mean, mine)
        at = place(me, j, count)
        mean = blocks_ref[at, 0:1, :] + edges_ref[at, 0:1, :] * mean
    later = jnp.zeros((1, modes), F32)
    for j in reversed(range(1, count)):
        at = place(me, j, count)
        longer = (
            blocks_ref[at, 1:2, :]
            + edges_ref[at, 3:4, :] * enter_ref[j : j + 1, :]
            + edges_ref[at, 1:2, :] * later
        )
        later = jnp.where(j > me, longer, later)
    mine = jnp.broadcast_to(mine, (chunks, modes))
    later = jnp.broadcast_to(later, (chunks, modes))
    for i in range(CHUNK):
        put_rows(mean_strip_ref, i, chunks, mean_ref[i] + whole_ref[0, i] * mine)
        put_rows(smooth_strip_ref, i, chunks, smooth_ref[i] + whole_ref[3, i] * mine + whole_ref[1, i] * later)
    unlanes(mean_strip_ref, out_mean_ref)
    unlanes(smooth_strip_ref, out_smooth_ref)


def product_kernel(slab_ref, basis_ref, out_ref):
    @pl.when(pl.program_id(0) == 0)
    def _():
        out_ref[...] = jnp.zeros_like(out_ref)

    out_ref[...] += jnp.dot(slab_ref[0], basis_ref[0], preferred_element_type=F32)


def project(slabs, basis, part, modes):
    count, steps, cells = slabs.shape

    def inner(part_ref, *refs):
        product_kernel(*refs)

    return pl.pallas_call(
        inner,
        grid_spec=pltpu.PrefetchScalarGridSpec(
            num_scalar_prefetch=1,
            grid=(count,),
            in_specs=[
                pl.BlockSpec((1, steps, cells), lambda g, part_ref: (g, 0, 0)),
                pl.BlockSpec((1, cells, modes), lambda g, part_ref: (g, 0, part_ref[0])),
            ],
            out_specs=pl.BlockSpec((steps, modes), lambda g, part_ref: (0, 0)),
        ),
        out_shape=jax.ShapeDtypeStruct((steps, modes), F32),
        compiler_params=pltpu.CompilerParams(vmem_limit_bytes=LIMIT),
        cost_estimate=pl.CostEstimate(
            flops=2 * count * steps * cells * modes,
            bytes_accessed=2 * count * cells * (steps + modes) + 4 * steps * modes,
            transcendentals=0,
        ),
    )(part.reshape(1), slabs, basis)


def call(kernel, inputs, outputs, scratch, flops):
    smem = pl.BlockSpec(memory_space=pltpu.SMEM)
    vmem = pl.BlockSpec(memory_space=pltpu.VMEM)
    moved = sum(4 * x.size for x in inputs) + sum(4 * x.size for x in outputs)
    return pl.pallas_call(
        kernel,
        in_specs=[smem if x.dtype == jnp.int32 else vmem for x in inputs],
        out_specs=[vmem] * len(outputs),
        out_shape=outputs,
        scratch_shapes=scratch,
        compiler_params=pltpu.CompilerParams(vmem_limit_bytes=LIMIT),
        cost_estimate=pl.CostEstimate(flops=flops, bytes_accessed=moved, transcendentals=0),
    )(*inputs)


def body(observations, pod_basis, decay, step_mask, process_var, obs_var, prior_mean, prior_var):
    tm_count = lax.axis_size("tm")
    space_count = lax.axis_size("space")
    steps, modes = decay.shape
    chunks = steps // CHUNK
    me = lax.axis_index("tm").astype(jnp.int32).reshape(1)
    side = lax.axis_index("space").astype(jnp.int32)
    shape = functools.partial(jax.ShapeDtypeStruct, dtype=F32)
    area = pltpu.VMEM

    slabs = observations.reshape(tm_count, steps, observations.shape[3])
    slabs = lax.all_to_all(slabs, "tm", 0, 0, tiled=True)

    seen = jnp.broadcast_to(step_mask.astype(F32)[:, None], (steps, modes))
    q, r = process_var[None, :], obs_var[None, :]
    following = lax.ppermute(decay[:1], "tm", [(i + 1, i) for i in range(tm_count - 1)])
    flat = (chunks, modes)
    deep = (CHUNK, chunks, modes)
    strips = area((modes // LANES, steps, LANES), F32)
    chunk_totals, block_totals = call(
        totals_kernel, (me, decay, seen, q, r), [shape((3,) + flat), shape((3, modes))], [strips] * 2, 40 * steps * modes
    )
    blocks = gather_rows(block_totals, "tm")
    a, b, g, h, whole, edge, block = call(
        functools.partial(gains_kernel, tm_count),
        (me, decay, following, seen, q, r, prior_var[None, :], chunk_totals, blocks),
        [shape(deep)] * 4 + [shape((4,) + deep), shape((4,) + flat), shape((4, modes))],
        [area(flat, F32), area(deep, F32), area(deep, F32), strips, strips],
        80 * steps * modes,
    )
    edges = gather_rows(block, "tm")
    (log_variance,) = call(
        functools.partial(variance_kernel, tm_count), (me, whole, edges), [shape((steps, modes))], [strips], 30 * steps * modes
    )

    basis = pod_basis.reshape(tm_count, -1, pod_basis.shape[3])
    parts = []
    for turn in range(1, space_count):
        theirs = project(slabs, basis, lax.rem(side + turn, space_count), modes)
        parts.append(lax.ppermute(theirs, "space", [(i, (i + turn) % space_count) for i in range(space_count)]))
    parts.insert(0, project(slabs, basis, side, modes))

    coefficients, mean, smooth, ends = call(
        functools.partial(means_kernel, len(parts)),
        (*parts, a, b, g, h, edge),
        [shape((steps, modes)), shape(deep), shape(deep), shape((2, modes))],
        [area(flat, F32), strips],
        12 * steps * modes,
    )
    ends = gather_rows(ends, "tm")
    filtered, smoothed = call(
        functools.partial(finish_kernel, tm_count),
        (me, prior_mean[None, :], whole, edges, ends, mean, smooth),
        [shape((steps, modes))] * 2,
        [area((tm_count, modes), F32), strips, strips],
        8 * steps * modes,
    )
    return coefficients, filtered, smoothed, log_variance


def solution(mesh):
    return jax.shard_map(
        body,
        mesh=mesh,
        in_specs=(
            P(None, "tm", "space", None),
            P(None, "space", None, None),
            P("tm", "space"),
            P("tm"),
            P("space"),
            P("space"),
            P("space"),
            P("space"),
        ),
        out_specs=(P("tm", "space"), P("tm", "space"), P("tm", "space"), P("tm", "space")),
        check_vma=False,
    )
```

```python
import functools

import jax
import jax.numpy as jnp
from jax import lax
from jax.experimental import pallas as pl
from jax.experimental.pallas import tpu as pltpu
from jax.sharding import PartitionSpec as P

CHUNK = 16
LANES = 128
F32 = jnp.float32
LIMIT = 48 * 1024 * 1024


def rotate(block, axis, turn, count, group, outer):
    route = []
    for i in range(count):
        low, high = i % group, i // group
        if outer:
            target = ((high + turn) % (count // group)) * group + low
        else:
            target = high * group + (low + turn) % group
        route.append((i, target))
    return lax.ppermute(block, axis, route)


def inner_size(count):
    group = 1
    while group * group < count:
        group *= 2
    return group if count % group == 0 else count


def gather_rows(rows, axis):
    count = lax.axis_size(axis)
    group = inner_size(count)
    near = jnp.stack([rows] + [rotate(rows, axis, s, count, group, False) for s in range(1, group)])
    far = [near] + [rotate(near, axis, s, count, group, True) for s in range(1, count // group)]
    return jnp.concatenate(far, 0)


def place(me, j, count):
    group = inner_size(count)
    rounds = count // group
    high = lax.rem(me // group - j // group + rounds, rounds)
    low = lax.rem(lax.rem(me, group) - j % group + group, group)
    return high * group + low


def lanes(ref, strip_ref):
    for m in range(strip_ref.shape[0]):
        strip_ref[m] = ref[:, m * LANES : (m + 1) * LANES]


def unlanes(strip_ref, ref):
    for m in range(strip_ref.shape[0]):
        ref[:, m * LANES : (m + 1) * LANES] = strip_ref[m]


def chunk_rows(strip_ref, i, chunks):
    rows = pl.ds(i, chunks, stride=CHUNK)
    return jnp.concatenate([strip_ref[m, rows, :] for m in range(strip_ref.shape[0])], 1)


def put_rows(strip_ref, i, chunks, value):
    rows = pl.ds(i, chunks, stride=CHUNK)
    for m in range(strip_ref.shape[0]):
        strip_ref[m, rows, :] = value[:, m * LANES : (m + 1) * LANES]


def opened(me_ref, shape):
    rows = lax.broadcasted_iota(jnp.int32, shape, 0)
    return jnp.logical_and(rows == 0, me_ref[0] == 0)


def step_terms(i, chunks, first, q, r, decay_ref, seen_ref):
    d = chunk_rows(decay_ref, i, chunks)
    seen = chunk_rows(seen_ref, i, chunks) > 0.5
    base = q
    if i == 0:
        d = jnp.where(first, 1.0, d)
        base = jnp.where(first, 0.0, q)
    return d, seen, base


def element(d, seen, base, r):
    inverse = 1.0 / (base + r)
    retain = jnp.where(seen, r * inverse, 1.0)
    return retain * d, retain * base, jnp.where(seen, d * d * inverse, 0.0), inverse


def join(early, late):
    lead, spread, weight = early
    lead_late, spread_late, weight_late = late
    factor = 1.0 / (1.0 + spread * weight_late)
    return (
        lead_late * factor * lead,
        lead_late * lead_late * factor * spread + spread_late,
        lead * lead * factor * weight_late + weight,
    )


def totals_kernel(me_ref, decay_in, seen_in, q_ref, r_ref, chunk_ref, block_ref, decay_ref, seen_ref):
    steps, modes = decay_in.shape
    lanes(decay_in, decay_ref)
    lanes(seen_in, seen_ref)
    chunks = steps // CHUNK
    shape = (chunks, modes)
    q = jnp.broadcast_to(q_ref[...], shape)
    r = jnp.broadcast_to(r_ref[...], shape)
    first = opened(me_ref, shape)
    total = None
    for i in range(CHUNK):
        step = element(*step_terms(i, chunks, first, q, r, decay_ref, seen_ref), r)[:3]
        total = step if i == 0 else join(total, step)
    for k in range(3):
        chunk_ref[k] = total[k]
    total = tuple(chunk_ref[k, 0:1, :] for k in range(3))
    for c in range(1, chunks):
        total = join(total, tuple(chunk_ref[k, c : c + 1, :] for k in range(3)))
    for k in range(3):
        block_ref[k : k + 1, :] = total[k]


def gains_kernel(
    count, me_ref, decay_in, seen_in, q_ref, r_ref, prior_ref, chunk_ref, blocks_ref,
    a_ref, b_ref, alpha_ref, beta_ref, keep_ref, lift_ref, whole_ref, carry_ref, edge_ref, log_ref,
    enter_ref, var_ref, info_ref, decay_ref, seen_ref,
):
    steps, modes = decay_in.shape
    lanes(decay_in, decay_ref)
    lanes(seen_in, seen_ref)
    chunks = steps // CHUNK
    shape = (chunks, modes)
    me = me_ref[0]
    q = jnp.broadcast_to(q_ref[...], shape)
    r = jnp.broadcast_to(r_ref[...], shape)
    first = opened(me_ref, shape)

    v = prior_ref[...]
    mine = v
    for j in range(count):
        mine = jnp.where(j == me, v, mine)
        at = place(me, j, count)
        lead, spread, weight = (blocks_ref[at, k : k + 1, :] for k in range(3))
        along = lead / (1.0 + weight * v)
        edge_ref[0, j : j + 1, :] = along
        v = spread + lead * along * v
    v = mine
    for c in range(chunks):
        enter_ref[0, c : c + 1, :] = v
        lead, spread, weight = (chunk_ref[k, c : c + 1, :] for k in range(3))
        v = spread + lead * lead * v / (1.0 + weight * v)

    info = jnp.zeros((1, modes), F32)
    mine = info
    for j in reversed(range(count)):
        mine = jnp.where(j == me, info, mine)
        at = place(me, j, count)
        lead, spread, weight = (blocks_ref[at, k : k + 1, :] for k in range(3))
        along = lead / (1.0 + spread * info)
        edge_ref[1, j : j + 1, :] = along
        info = weight + lead * along * info
    info = mine
    for c in reversed(range(chunks)):
        enter_ref[1, c : c + 1, :] = info
        lead, spread, weight = (chunk_ref[k, c : c + 1, :] for k in range(3))
        info = weight + lead * lead * info / (1.0 + spread * info)

    v = enter_ref[0]
    run = None
    for i in range(CHUNK):
        d, seen, base = step_terms(i, chunks, first, q, r, decay_ref, seen_ref)
        ahead = d * d * v + base
        inverse = 1.0 / (ahead + r)
        retain = jnp.where(seen, r * inverse, 1.0)
        v = retain * ahead
        a = retain * d
        run = a if i == 0 else a * run
        a_ref[i] = a
        b_ref[i] = jnp.where(seen, ahead * inverse, 0.0)
        var_ref[i] = v
        whole_ref[0, i] = run
    carry_ref[0] = run

    info = enter_ref[1]
    run = jnp.ones(shape, F32)
    for i in reversed(range(CHUNK)):
        lead, spread, weight, inverse = element(*step_terms(i, chunks, first, q, r, decay_ref, seen_ref), r)
        d, seen, _ = step_terms(i, chunks, first, q, r, decay_ref, seen_ref)
        factor = 1.0 / (1.0 + spread * info)
        alpha = lead * factor
        info_ref[i] = info
        whole_ref[2, i] = run
        alpha_ref[i] = alpha
        beta_ref[i] = jnp.where(seen, d * inverse * factor, 0.0)
        info = weight + lead * alpha * info
        run = alpha * run
    carry_ref[1] = run

    along = jnp.ones((1, modes), F32)
    for c in range(chunks):
        enter_ref[0, c : c + 1, :] = along
        along = along * carry_ref[0, c : c + 1, :]
    along = jnp.ones((1, modes), F32)
    for c in reversed(range(chunks)):
        enter_ref[1, c : c + 1, :] = along
        along = along * carry_ref[1, c : c + 1, :]
    onward = enter_ref[0]
    back = enter_ref[1]
    for i in range(CHUNK):
        v = var_ref[i]
        keep = 1.0 / (1.0 + v * info_ref[i])
        lift = v * keep
        weight = whole_ref[0, i] * onward
        keep_ref[i] = keep
        lift_ref[i] = lift
        whole_ref[0, i] = weight
        whole_ref[1, i] = keep * weight
        whole_ref[2, i] = lift * (whole_ref[2, i] * back)
        put_rows(decay_ref, i, chunks, jnp.log(lift))
    unlanes(decay_ref, log_ref)


def means_kernel(parts, *refs):
    part_refs = refs[:parts]
    a_ref, b_ref, alpha_ref, beta_ref, keep_ref, lift_ref, carry_ref = refs[parts : parts + 7]
    coef_ref, mean_ref, smooth_ref, block_ref, enter_ref, strip_ref = refs[parts + 7 :]
    steps, modes = coef_ref.shape
    chunks = steps // CHUNK
    c = part_refs[0][...]
    for ref in part_refs[1:]:
        c = c + ref[...]
    coef_ref[...] = c
    lanes(coef_ref, strip_ref)
    f = e = jnp.zeros((chunks, modes), F32)
    for i in range(CHUNK):
        f = a_ref[i] * f + b_ref[i] * chunk_rows(strip_ref, i, chunks)
        k = CHUNK - 1 - i
        e = alpha_ref[k] * e + beta_ref[k] * chunk_rows(strip_ref, k, chunks)
    mean_ref[0] = f
    mean_ref[1] = e
    f = e = jnp.zeros((1, modes), F32)
    for c in range(chunks):
        k = chunks - 1 - c
        enter_ref[0, c : c + 1, :] = f
        enter_ref[1, k : k + 1, :] = e
        f = mean_ref[0, c : c + 1, :] + carry_ref[0, c : c + 1, :] * f
        e = mean_ref[1, k : k + 1, :] + carry_ref[1, k : k + 1, :] * e
    block_ref[0:1, :] = f
    block_ref[1:2, :] = e
    f = enter_ref[0]
    e = enter_ref[1]
    for i in range(CHUNK):
        f = a_ref[i] * f + b_ref[i] * chunk_rows(strip_ref, i, chunks)
        mean_ref[i] = f
    for i in reversed(range(CHUNK)):
        smooth_ref[i] = keep_ref[i] * mean_ref[i] + lift_ref[i] * e
        e = alpha_ref[i] * e + beta_ref[i] * chunk_rows(strip_ref, i, chunks)


def finish_kernel(count, me_ref, prior_ref, whole_ref, edge_ref, blocks_ref, mean_ref, smooth_ref, out_mean_ref, out_smooth_ref, mean_strip_ref, smooth_strip_ref):
    steps, modes = out_mean_ref.shape
    chunks = steps // CHUNK
    me = me_ref[0]
    f = prior_ref[...]
    e = jnp.zeros((1, modes), F32)
    for j in range(count - 1):
        at = place(me, j, count)
        f = jnp.where(j < me, blocks_ref[at, 0:1, :] + edge_ref[0, j : j + 1, :] * f, f)
        k = count - 1 - j
        at = place(me, k, count)
        e = jnp.where(k > me, blocks_ref[at, 1:2, :] + edge_ref[1, k : k + 1, :] * e, e)
    f = jnp.broadcast_to(f, (chunks, modes))
    e = jnp.broadcast_to(e, (chunks, modes))
    for i in range(CHUNK):
        put_rows(mean_strip_ref, i, chunks, mean_ref[i] + whole_ref[0, i] * f)
        put_rows(smooth_strip_ref, i, chunks, smooth_ref[i] + whole_ref[1, i] * f + whole_ref[2, i] * e)
    unlanes(mean_strip_ref, out_mean_ref)
    unlanes(smooth_strip_ref, out_smooth_ref)


def project_kernel(at_ref, slab_ref, basis_ref, out_ref, slab_area, basis_area, slab_sems, basis_sems):
    count = slab_ref.shape[0]
    owners, steps, modes = out_ref.shape
    copies = []
    for g in range(count):
        copies.append((
            pltpu.make_async_copy(slab_ref.at[g], slab_area.at[g], slab_sems.at[g]),
            pltpu.make_async_copy(basis_ref.at[at_ref[0] + g], basis_area.at[g], basis_sems.at[g]),
        ))
    for pair in copies:
        for copy in pair:
            copy.start()
    for g in range(count):
        for copy in copies[g]:
            copy.wait()
        for turn in range(owners):
            owner = lax.rem(at_ref[1] + turn, owners)
            columns = pl.ds(pl.multiple_of(owner * modes, LANES), modes)
            term = jnp.dot(slab_area[g], basis_area[g, :, columns], preferred_element_type=F32)
            out_ref[turn] = term if g == 0 else out_ref[turn] + term


def project(slabs, basis, first, side, owners):
    count, steps, cells = slabs.shape
    modes = basis.shape[2] // owners
    return pl.pallas_call(
        project_kernel,
        in_specs=[
            pl.BlockSpec(memory_space=pltpu.SMEM),
            pl.BlockSpec(memory_space=pl.ANY),
            pl.BlockSpec(memory_space=pl.ANY),
        ],
        out_specs=pl.BlockSpec(memory_space=pltpu.VMEM),
        out_shape=jax.ShapeDtypeStruct((owners, steps, modes), F32),
        scratch_shapes=[
            pltpu.VMEM(slabs.shape, slabs.dtype),
            pltpu.VMEM((count,) + basis.shape[1:], basis.dtype),
            pltpu.SemaphoreType.DMA((count,)),
            pltpu.SemaphoreType.DMA((count,)),
        ],
        compiler_params=pltpu.CompilerParams(vmem_limit_bytes=LIMIT),
        cost_estimate=pl.CostEstimate(
            flops=2 * count * steps * cells * modes * owners,
            bytes_accessed=2 * count * cells * (steps + modes * owners) + 4 * steps * modes * owners,
            transcendentals=0,
        ),
    )(jnp.stack([first, side]), slabs, basis)


def call(kernel, inputs, outputs, scratch, flops):
    smem = pl.BlockSpec(memory_space=pltpu.SMEM)
    vmem = pl.BlockSpec(memory_space=pltpu.VMEM)
    moved = sum(4 * x.size for x in inputs) + sum(4 * x.size for x in outputs)
    return pl.pallas_call(
        kernel,
        in_specs=[smem if x.dtype == jnp.int32 else vmem for x in inputs],
        out_specs=[vmem] * len(outputs),
        out_shape=outputs,
        scratch_shapes=scratch,
        compiler_params=pltpu.CompilerParams(vmem_limit_bytes=LIMIT),
        cost_estimate=pl.CostEstimate(flops=flops, bytes_accessed=moved, transcendentals=0),
    )(*inputs)


def swap_halves(block, axis):
    half = lax.axis_size(axis) // 2
    return lax.ppermute(block, axis, [(i, (i + half) % (2 * half)) for i in range(2 * half)])


def sum_over(terms, axis):
    count = lax.axis_size(axis)
    arrived = [
        lax.ppermute(terms[turn], axis, [(i, (i + turn) % count) for i in range(count)]) for turn in range(1, count)
    ]
    return [terms[0]] + arrived


def body(observations, pod_basis, decay, step_mask, process_var, obs_var, prior_mean, prior_var):
    tm_count = lax.axis_size("tm")
    space_count = lax.axis_size("space")
    steps, modes = decay.shape
    chunks = steps // CHUNK
    rank = lax.axis_index("tm").astype(jnp.int32)
    me = rank.reshape(1)
    side = lax.axis_index("space").astype(jnp.int32)
    shape = functools.partial(jax.ShapeDtypeStruct, dtype=F32)
    area = pltpu.VMEM
    group = tm_count // 2
    groups = [[half * group + i for i in range(group)] for half in range(2)]
    half = rank // group

    slabs = observations.reshape(2, group, steps, observations.shape[3])
    basis = pod_basis.reshape(tm_count, -1, pod_basis.shape[3])
    far = lax.dynamic_index_in_dim(slabs, 1 - half, 0, keepdims=False)
    far = lax.all_to_all(far, "tm", 0, 0, axis_index_groups=groups, tiled=True)
    near = lax.dynamic_index_in_dim(slabs, half, 0, keepdims=False)
    near = lax.all_to_all(near, "tm", 0, 0, axis_index_groups=groups, tiled=True)
    far = project(far, basis, half * group, side, space_count)
    crossing = swap_halves(sum(sum_over(far, "space")), "tm")
    near = project(near, basis, half * group, side, space_count)
    parts = sum_over(near, "space") + [crossing]

    seen = jnp.broadcast_to(step_mask.astype(F32)[:, None], (steps, modes))
    q, r = process_var[None, :], obs_var[None, :]
    flat = (chunks, modes)
    deep = (CHUNK, chunks, modes)
    strips = area((modes // LANES, steps, LANES), F32)
    chunk_totals, block_totals = call(
        totals_kernel, (me, decay, seen, q, r), [shape((3,) + flat), shape((3, modes))], [strips] * 2, 40 * steps * modes
    )
    blocks = gather_rows(block_totals, "tm")
    *maps, whole, carry, edge, log_variance = call(
        functools.partial(gains_kernel, tm_count),
        (me, decay, seen, q, r, prior_var[None, :], chunk_totals, blocks),
        [shape(deep)] * 6 + [shape((3,) + deep), shape((2,) + flat), shape((2, tm_count, modes)), shape((steps, modes))],
        [area((2,) + flat, F32), area(deep, F32), area(deep, F32), strips, strips],
        80 * steps * modes,
    )

    coefficients, mean, smooth, ends = call(
        functools.partial(means_kernel, len(parts)),
        (*parts, *maps, carry),
        [shape((steps, modes)), shape(deep), shape(deep), shape((2, modes))],
        [area((2,) + flat, F32), strips],
        12 * steps * modes,
    )
    ends = gather_rows(ends, "tm")
    filtered, smoothed = call(
        functools.partial(finish_kernel, tm_count),
        (me, prior_mean[None, :], whole, edge, ends, mean, smooth),
        [shape((steps, modes))] * 2,
        [strips, strips],
        8 * steps * modes,
    )
    return coefficients, filtered, smoothed, log_variance


def solution(mesh):
    return jax.shard_map(
        body,
        mesh=mesh,
        in_specs=(
            P(None, "tm", "space", None),
            P(None, "space", None, None),
            P("tm", "space"),
            P("tm"),
            P("space"),
            P("space"),
            P("space"),
            P("space"),
        ),
        out_specs=(P("tm", "space"), P("tm", "space"), P("tm", "space"), P("tm", "space")),
        check_vma=False,
    )
```

```python
import functools

import jax
import jax.numpy as jnp
from jax import lax
from jax.experimental import pallas as pl
from jax.experimental.pallas import tpu as pltpu
from jax.sharding import PartitionSpec as P

CHUNK = 16
LANES = 128
F32 = jnp.float32
LIMIT = 48 * 1024 * 1024


def rotate(block, axis, turn, count, group, outer):
    route = []
    for i in range(count):
        low, high = i % group, i // group
        if outer:
            target = ((high + turn) % (count // group)) * group + low
        else:
            target = high * group + (low + turn) % group
        route.append((i, target))
    return lax.ppermute(block, axis, route)


def inner_size(count):
    group = 1
    while group * group < count:
        group *= 2
    return group if count % group == 0 else count


def gather_rows(rows, axis):
    count = lax.axis_size(axis)
    group = inner_size(count)
    near = jnp.stack([rows] + [rotate(rows, axis, s, count, group, False) for s in range(1, group)])
    far = [near] + [rotate(near, axis, s, count, group, True) for s in range(1, count // group)]
    return jnp.concatenate(far, 0)


def place(me, j, count):
    group = inner_size(count)
    rounds = count // group
    high = lax.rem(me // group - j // group + rounds, rounds)
    low = lax.rem(lax.rem(me, group) - j % group + group, group)
    return high * group + low


def lanes(ref, strip_ref):
    for m in range(strip_ref.shape[0]):
        strip_ref[m] = ref[:, m * LANES : (m + 1) * LANES]


def unlanes(strip_ref, ref):
    for m in range(strip_ref.shape[0]):
        ref[:, m * LANES : (m + 1) * LANES] = strip_ref[m]


def chunk_rows(strip_ref, i, chunks):
    rows = pl.ds(i, chunks, stride=CHUNK)
    return jnp.concatenate([strip_ref[m, rows, :] for m in range(strip_ref.shape[0])], 1)


def put_rows(strip_ref, i, chunks, value):
    rows = pl.ds(i, chunks, stride=CHUNK)
    for m in range(strip_ref.shape[0]):
        strip_ref[m, rows, :] = value[:, m * LANES : (m + 1) * LANES]


def opened(me_ref, shape):
    rows = lax.broadcasted_iota(jnp.int32, shape, 0)
    return jnp.logical_and(rows == 0, me_ref[0] == 0)


def step_terms(i, chunks, first, q, r, decay_ref, seen_ref):
    d = chunk_rows(decay_ref, i, chunks)
    seen = chunk_rows(seen_ref, i, chunks) > 0.5
    base = q
    if i == 0:
        d = jnp.where(first, 1.0, d)
        base = jnp.where(first, 0.0, q)
    return d, seen, base


def element(d, seen, base, r):
    inverse = 1.0 / (base + r)
    retain = jnp.where(seen, r * inverse, 1.0)
    return retain * d, retain * base, jnp.where(seen, d * d * inverse, 0.0), inverse


def join(early, late):
    lead, spread, weight = early
    lead_late, spread_late, weight_late = late
    factor = 1.0 / (1.0 + spread * weight_late)
    return (
        lead_late * factor * lead,
        lead_late * lead_late * factor * spread + spread_late,
        lead * lead * factor * weight_late + weight,
    )


def totals_kernel(me_ref, decay_in, seen_in, q_ref, r_ref, chunk_ref, block_ref, decay_ref, seen_ref):
    steps, modes = decay_in.shape
    lanes(decay_in, decay_ref)
    lanes(seen_in, seen_ref)
    chunks = steps // CHUNK
    shape = (chunks, modes)
    q = jnp.broadcast_to(q_ref[...], shape)
    r = jnp.broadcast_to(r_ref[...], shape)
    first = opened(me_ref, shape)
    total = None
    for i in range(CHUNK):
        step = element(*step_terms(i, chunks, first, q, r, decay_ref, seen_ref), r)[:3]
        total = step if i == 0 else join(total, step)
    for k in range(3):
        chunk_ref[k] = total[k]
    total = tuple(chunk_ref[k, 0:1, :] for k in range(3))
    for c in range(1, chunks):
        total = join(total, tuple(chunk_ref[k, c : c + 1, :] for k in range(3)))
    for k in range(3):
        block_ref[k : k + 1, :] = total[k]


def gains_kernel(
    count, me_ref, decay_in, seen_in, q_ref, r_ref, prior_ref, chunk_ref, blocks_ref,
    a_ref, b_ref, alpha_ref, beta_ref, keep_ref, lift_ref, whole_ref, carry_ref, edge_ref, log_ref,
    enter_ref, var_ref, info_ref, decay_ref, seen_ref,
):
    steps, modes = decay_in.shape
    lanes(decay_in, decay_ref)
    lanes(seen_in, seen_ref)
    chunks = steps // CHUNK
    shape = (chunks, modes)
    me = me_ref[0]
    q = jnp.broadcast_to(q_ref[...], shape)
    r = jnp.broadcast_to(r_ref[...], shape)
    first = opened(me_ref, shape)

    v = prior_ref[...]
    mine = v
    for j in range(count):
        mine = jnp.where(j == me, v, mine)
        at = place(me, j, count)
        lead, spread, weight = (blocks_ref[at, k : k + 1, :] for k in range(3))
        along = lead / (1.0 + weight * v)
        edge_ref[0, j : j + 1, :] = along
        v = spread + lead * along * v
    v = mine
    for c in range(chunks):
        enter_ref[0, c : c + 1, :] = v
        lead, spread, weight = (chunk_ref[k, c : c + 1, :] for k in range(3))
        v = spread + lead * lead * v / (1.0 + weight * v)

    info = jnp.zeros((1, modes), F32)
    mine = info
    for j in reversed(range(count)):
        mine = jnp.where(j == me, info, mine)
        at = place(me, j, count)
        lead, spread, weight = (blocks_ref[at, k : k + 1, :] for k in range(3))
        along = lead / (1.0 + spread * info)
        edge_ref[1, j : j + 1, :] = along
        info = weight + lead * along * info
    info = mine
    for c in reversed(range(chunks)):
        enter_ref[1, c : c + 1, :] = info
        lead, spread, weight = (chunk_ref[k, c : c + 1, :] for k in range(3))
        info = weight + lead * lead * info / (1.0 + spread * info)

    v = enter_ref[0]
    run = None
    for i in range(CHUNK):
        d, seen, base = step_terms(i, chunks, first, q, r, decay_ref, seen_ref)
        ahead = d * d * v + base
        inverse = 1.0 / (ahead + r)
        retain = jnp.where(seen, r * inverse, 1.0)
        v = retain * ahead
        a = retain * d
        run = a if i == 0 else a * run
        a_ref[i] = a
        b_ref[i] = jnp.where(seen, ahead * inverse, 0.0)
        var_ref[i] = v
        whole_ref[0, i] = run
    carry_ref[0] = run

    info = enter_ref[1]
    run = jnp.ones(shape, F32)
    for i in reversed(range(CHUNK)):
        lead, spread, weight, inverse = element(*step_terms(i, chunks, first, q, r, decay_ref, seen_ref), r)
        d, seen, _ = step_terms(i, chunks, first, q, r, decay_ref, seen_ref)
        factor = 1.0 / (1.0 + spread * info)
        alpha = lead * factor
        info_ref[i] = info
        whole_ref[2, i] = run
        alpha_ref[i] = alpha
        beta_ref[i] = jnp.where(seen, d * inverse * factor, 0.0)
        info = weight + lead * alpha * info
        run = alpha * run
    carry_ref[1] = run

    along = jnp.ones((1, modes), F32)
    for c in range(chunks):
        enter_ref[0, c : c + 1, :] = along
        along = along * carry_ref[0, c : c + 1, :]
    along = jnp.ones((1, modes), F32)
    for c in reversed(range(chunks)):
        enter_ref[1, c : c + 1, :] = along
        along = along * carry_ref[1, c : c + 1, :]
    onward = enter_ref[0]
    back = enter_ref[1]
    for i in range(CHUNK):
        v = var_ref[i]
        keep = 1.0 / (1.0 + v * info_ref[i])
        lift = v * keep
        weight = whole_ref[0, i] * onward
        keep_ref[i] = keep
        lift_ref[i] = lift
        whole_ref[0, i] = weight
        whole_ref[1, i] = keep * weight
        whole_ref[2, i] = lift * (whole_ref[2, i] * back)
        put_rows(decay_ref, i, chunks, jnp.log(lift))
    unlanes(decay_ref, log_ref)


def means_kernel(parts, *refs):
    part_refs = refs[:parts]
    a_ref, b_ref, alpha_ref, beta_ref, keep_ref, lift_ref, carry_ref = refs[parts : parts + 7]
    coef_ref, mean_ref, smooth_ref, block_ref, enter_ref, strip_ref = refs[parts + 7 :]
    steps, modes = coef_ref.shape
    chunks = steps // CHUNK
    c = part_refs[0][...]
    for ref in part_refs[1:]:
        c = c + ref[...]
    coef_ref[...] = c
    lanes(coef_ref, strip_ref)
    f = e = jnp.zeros((chunks, modes), F32)
    for i in range(CHUNK):
        f = a_ref[i] * f + b_ref[i] * chunk_rows(strip_ref, i, chunks)
        k = CHUNK - 1 - i
        e = alpha_ref[k] * e + beta_ref[k] * chunk_rows(strip_ref, k, chunks)
    mean_ref[0] = f
    mean_ref[1] = e
    f = e = jnp.zeros((1, modes), F32)
    for c in range(chunks):
        k = chunks - 1 - c
        enter_ref[0, c : c + 1, :] = f
        enter_ref[1, k : k + 1, :] = e
        f = mean_ref[0, c : c + 1, :] + carry_ref[0, c : c + 1, :] * f
        e = mean_ref[1, k : k + 1, :] + carry_ref[1, k : k + 1, :] * e
    block_ref[0:1, :] = f
    block_ref[1:2, :] = e
    f = enter_ref[0]
    e = enter_ref[1]
    for i in range(CHUNK):
        f = a_ref[i] * f + b_ref[i] * chunk_rows(strip_ref, i, chunks)
        mean_ref[i] = f
    for i in reversed(range(CHUNK)):
        smooth_ref[i] = keep_ref[i] * mean_ref[i] + lift_ref[i] * e
        e = alpha_ref[i] * e + beta_ref[i] * chunk_rows(strip_ref, i, chunks)


def finish_kernel(count, me_ref, prior_ref, whole_ref, edge_ref, blocks_ref, mean_ref, smooth_ref, out_mean_ref, out_smooth_ref, mean_strip_ref, smooth_strip_ref):
    steps, modes = out_mean_ref.shape
    chunks = steps // CHUNK
    me = me_ref[0]
    f = prior_ref[...]
    e = jnp.zeros((1, modes), F32)
    for j in range(count - 1):
        f = jnp.where(j < me, blocks_ref[j, 0:1, :] + edge_ref[0, j : j + 1, :] * f, f)
        k = count - 1 - j
        e = jnp.where(k > me, blocks_ref[k, 1:2, :] + edge_ref[1, k : k + 1, :] * e, e)
    f = jnp.broadcast_to(f, (chunks, modes))
    e = jnp.broadcast_to(e, (chunks, modes))
    for i in range(CHUNK):
        put_rows(mean_strip_ref, i, chunks, mean_ref[i] + whole_ref[0, i] * f)
        put_rows(smooth_strip_ref, i, chunks, smooth_ref[i] + whole_ref[1, i] * f + whole_ref[2, i] * e)
    unlanes(mean_strip_ref, out_mean_ref)
    unlanes(smooth_strip_ref, out_smooth_ref)


def project_kernel(at_ref, slab_ref, basis_ref, out_ref, slab_area, basis_area, slab_sems, basis_sems):
    count = slab_ref.shape[0]
    modes = out_ref.shape[1]
    columns = pl.ds(pl.multiple_of(at_ref[1] * modes, LANES), modes)
    copies = []
    for g in range(count):
        copies.append((
            pltpu.make_async_copy(slab_ref.at[g], slab_area.at[g], slab_sems.at[g]),
            pltpu.make_async_copy(basis_ref.at[at_ref[0] + g, :, columns], basis_area.at[g], basis_sems.at[g]),
        ))
    for pair in copies:
        for copy in pair:
            copy.start()
    for g in range(count):
        for copy in copies[g]:
            copy.wait()
        term = jnp.dot(slab_area[g], basis_area[g], preferred_element_type=F32)
        out_ref[...] = term if g == 0 else out_ref[...] + term


def project(slabs, basis, first, owner, modes):
    count, steps, cells = slabs.shape
    return pl.pallas_call(
        project_kernel,
        in_specs=[
            pl.BlockSpec(memory_space=pltpu.SMEM),
            pl.BlockSpec(memory_space=pl.ANY),
            pl.BlockSpec(memory_space=pl.ANY),
        ],
        out_specs=pl.BlockSpec(memory_space=pltpu.VMEM),
        out_shape=jax.ShapeDtypeStruct((steps, modes), F32),
        scratch_shapes=[
            pltpu.VMEM(slabs.shape, slabs.dtype),
            pltpu.VMEM((count, cells, modes), basis.dtype),
            pltpu.SemaphoreType.DMA((count,)),
            pltpu.SemaphoreType.DMA((count,)),
        ],
        compiler_params=pltpu.CompilerParams(vmem_limit_bytes=LIMIT),
        cost_estimate=pl.CostEstimate(
            flops=2 * count * steps * cells * modes,
            bytes_accessed=2 * count * cells * (steps + modes) + 4 * steps * modes,
            transcendentals=0,
        ),
    )(jnp.stack([first, owner]), slabs, basis)


def call(kernel, inputs, outputs, scratch, flops):
    smem = pl.BlockSpec(memory_space=pltpu.SMEM)
    vmem = pl.BlockSpec(memory_space=pltpu.VMEM)
    moved = sum(4 * x.size for x in inputs) + sum(4 * x.size for x in outputs)
    return pl.pallas_call(
        kernel,
        in_specs=[smem if x.dtype == jnp.int32 else vmem for x in inputs],
        out_specs=[vmem] * len(outputs),
        out_shape=outputs,
        scratch_shapes=scratch,
        compiler_params=pltpu.CompilerParams(vmem_limit_bytes=LIMIT),
        cost_estimate=pl.CostEstimate(flops=flops, bytes_accessed=moved, transcendentals=0),
    )(*inputs)


def swap_halves(block, axis):
    half = lax.axis_size(axis) // 2
    return lax.ppermute(block, axis, [(i, (i + half) % (2 * half)) for i in range(2 * half)])


def project_all(slabs, basis, first, side, count, modes):
    arriving = []
    for turn in range(1, count):
        theirs = project(slabs, basis, first, lax.rem(side + turn, count), modes)
        arriving.append(lax.ppermute(theirs, "space", [(i, (i + turn) % count) for i in range(count)]))
    return [project(slabs, basis, first, side, modes)] + arriving


def body(observations, pod_basis, decay, step_mask, process_var, obs_var, prior_mean, prior_var):
    tm_count = lax.axis_size("tm")
    space_count = lax.axis_size("space")
    steps, modes = decay.shape
    chunks = steps // CHUNK
    rank = lax.axis_index("tm").astype(jnp.int32)
    me = rank.reshape(1)
    side = lax.axis_index("space").astype(jnp.int32)
    shape = functools.partial(jax.ShapeDtypeStruct, dtype=F32)
    area = pltpu.VMEM
    group = tm_count // 2
    groups = [[half * group + i for i in range(group)] for half in range(2)]
    half = rank // group

    seen = jnp.broadcast_to(step_mask.astype(F32)[:, None], (steps, modes))
    q, r = process_var[None, :], obs_var[None, :]
    flat = (chunks, modes)
    deep = (CHUNK, chunks, modes)
    strips = area((modes // LANES, steps, LANES), F32)
    slabs = observations.reshape(2, group, steps, observations.shape[3])
    basis = pod_basis.reshape(tm_count, -1, pod_basis.shape[3])
    far = lax.dynamic_index_in_dim(slabs, 1 - half, 0, keepdims=False)
    far, seen = lax.optimization_barrier((far, seen))
    far = lax.all_to_all(far, "tm", 0, 0, axis_index_groups=groups, tiled=True)
    chunk_totals, block_totals = call(
        totals_kernel, (me, decay, seen, q, r), [shape((3,) + flat), shape((3, modes))], [strips] * 2, 40 * steps * modes
    )
    block_totals, own_half = lax.optimization_barrier((block_totals, half))
    near = lax.dynamic_index_in_dim(slabs, own_half, 0, keepdims=False)
    far, near, chunk_totals = lax.optimization_barrier((far, near, chunk_totals))
    near = lax.all_to_all(near, "tm", 0, 0, axis_index_groups=groups, tiled=True)
    blocks = gather_rows(block_totals, "tm")
    crossing = sum(project_all(far, basis, half * group, side, space_count, modes))
    crossing, blocks = lax.optimization_barrier((crossing, blocks))
    crossing = swap_halves(crossing, "tm")
    *maps, whole, carry, edge, log_variance = call(
        functools.partial(gains_kernel, tm_count),
        (me, decay, seen, q, r, prior_var[None, :], chunk_totals, blocks),
        [shape(deep)] * 6 + [shape((3,) + deep), shape((2,) + flat), shape((2, tm_count, modes)), shape((steps, modes))],
        [area((2,) + flat, F32), area(deep, F32), area(deep, F32), strips, strips],
        80 * steps * modes,
    )
    near, maps = lax.optimization_barrier((near, maps))
    parts = project_all(near, basis, half * group, side, space_count, modes) + [crossing]

    coefficients, mean, smooth, ends = call(
        functools.partial(means_kernel, len(parts)),
        (*parts, *maps, carry),
        [shape((steps, modes)), shape(deep), shape(deep), shape((2, modes))],
        [area((2,) + flat, F32), strips],
        12 * steps * modes,
    )
    ends = jnp.broadcast_to(ends[None], (tm_count,) + ends.shape)
    ends = lax.all_to_all(ends, "tm", 0, 0, tiled=True)
    filtered, smoothed = call(
        functools.partial(finish_kernel, tm_count),
        (me, prior_mean[None, :], whole, edge, ends, mean, smooth),
        [shape((steps, modes))] * 2,
        [strips, strips],
        8 * steps * modes,
    )
    return coefficients, filtered, smoothed, log_variance


def solution(mesh):
    return jax.shard_map(
        body,
        mesh=mesh,
        in_specs=(
            P(None, "tm", "space", None),
            P(None, "space", None, None),
            P("tm", "space"),
            P("tm"),
            P("space"),
            P("space"),
            P("space"),
            P("space"),
        ),
        out_specs=(P("tm", "space"), P("tm", "space"), P("tm", "space"), P("tm", "space")),
        check_vma=False,
    )
```

```python
import functools

import jax
import jax.numpy as jnp
from jax import lax
from jax.experimental import pallas as pl
from jax.experimental.pallas import tpu as pltpu
from jax.sharding import PartitionSpec as P

CHUNK = 16
LANES = 128
F32 = jnp.float32
LIMIT = 16 * 1024 * 1024


def rotate(block, axis, turn, count, group, outer):
    route = []
    for i in range(count):
        low, high = i % group, i // group
        if outer:
            target = ((high + turn) % (count // group)) * group + low
        else:
            target = high * group + (low + turn) % group
        route.append((i, target))
    return lax.ppermute(block, axis, route)


def inner_size(count):
    group = 1
    while group * group < count:
        group *= 2
    return group if count % group == 0 else count


def gather_near(rows, axis):
    count = lax.axis_size(axis)
    group = inner_size(count)
    return jnp.stack([rows] + [rotate(rows, axis, s, count, group, False) for s in range(1, group)])


def gather_far(near, axis):
    count = lax.axis_size(axis)
    group = inner_size(count)
    return [rotate(near, axis, s, count, group, True) for s in range(1, count // group)]


def place(me, j, count):
    group = inner_size(count)
    rounds = count // group
    high = lax.rem(me // group - j // group + rounds, rounds)
    low = lax.rem(lax.rem(me, group) - j % group + group, group)
    return high * group + low


def lanes(ref, strip_ref):
    for m in range(strip_ref.shape[0]):
        strip_ref[m] = ref[:, m * LANES : (m + 1) * LANES]


def unlanes(strip_ref, ref):
    for m in range(strip_ref.shape[0]):
        ref[:, m * LANES : (m + 1) * LANES] = strip_ref[m]


def chunk_rows(strip_ref, i, chunks):
    rows = pl.ds(i, chunks, stride=CHUNK)
    return jnp.concatenate([strip_ref[m, rows, :] for m in range(strip_ref.shape[0])], 1)


def put_rows(strip_ref, i, chunks, value):
    rows = pl.ds(i, chunks, stride=CHUNK)
    for m in range(strip_ref.shape[0]):
        strip_ref[m, rows, :] = value[:, m * LANES : (m + 1) * LANES]


def opened(me_ref, shape):
    rows = lax.broadcasted_iota(jnp.int32, shape, 0)
    return jnp.logical_and(rows == 0, me_ref[0] == 0)


def step_terms(i, chunks, first, q, r, decay_ref, seen_ref):
    d = chunk_rows(decay_ref, i, chunks)
    seen = chunk_rows(seen_ref, i, chunks) > 0.5
    base = q
    if i == 0:
        d = jnp.where(first, 1.0, d)
        base = jnp.where(first, 0.0, q)
    return d, seen, base


def element(d, seen, base, r):
    inverse = 1.0 / (base + r)
    retain = jnp.where(seen, r * inverse, 1.0)
    return retain * d, retain * base, jnp.where(seen, d * d * inverse, 0.0), inverse


def join(early, late):
    lead, spread, weight = early
    lead_late, spread_late, weight_late = late
    factor = 1.0 / (1.0 + spread * weight_late)
    return (
        lead_late * factor * lead,
        lead_late * lead_late * factor * spread + spread_late,
        lead * lead * factor * weight_late + weight,
    )


def totals_kernel(me_ref, decay_in, seen_in, q_ref, r_ref, chunk_ref, block_ref, decay_ref, seen_ref):
    steps, modes = decay_in.shape
    lanes(decay_in, decay_ref)
    lanes(seen_in, seen_ref)
    chunks = steps // CHUNK
    shape = (chunks, modes)
    q = jnp.broadcast_to(q_ref[...], shape)
    r = jnp.broadcast_to(r_ref[...], shape)
    first = opened(me_ref, shape)
    total = None
    for i in range(CHUNK):
        step = element(*step_terms(i, chunks, first, q, r, decay_ref, seen_ref), r)[:3]
        total = step if i == 0 else join(total, step)
    for k in range(3):
        chunk_ref[k] = total[k]
    total = tuple(chunk_ref[k, 0:1, :] for k in range(3))
    for c in range(1, chunks):
        total = join(total, tuple(chunk_ref[k, c : c + 1, :] for k in range(3)))
    for k in range(3):
        block_ref[k : k + 1, :] = total[k]


def gains_kernel(
    count, me_ref, decay_in, seen_in, q_ref, r_ref, prior_ref, chunk_ref, blocks_ref,
    a_ref, b_ref, alpha_ref, beta_ref, keep_ref, lift_ref, whole_ref, carry_ref, edge_ref, log_ref,
    enter_ref, var_ref, info_ref, decay_ref, seen_ref,
):
    steps, modes = decay_in.shape
    lanes(decay_in, decay_ref)
    lanes(seen_in, seen_ref)
    chunks = steps // CHUNK
    shape = (chunks, modes)
    me = me_ref[0]
    q = jnp.broadcast_to(q_ref[...], shape)
    r = jnp.broadcast_to(r_ref[...], shape)
    first = opened(me_ref, shape)

    v = prior_ref[...]
    mine = v
    for j in range(count):
        mine = jnp.where(j == me, v, mine)
        at = place(me, j, count)
        lead, spread, weight = (blocks_ref[at, k : k + 1, :] for k in range(3))
        along = lead / (1.0 + weight * v)
        edge_ref[0, j : j + 1, :] = along
        v = spread + lead * along * v
    v = mine
    for c in range(chunks):
        enter_ref[0, c : c + 1, :] = v
        lead, spread, weight = (chunk_ref[k, c : c + 1, :] for k in range(3))
        v = spread + lead * lead * v / (1.0 + weight * v)

    info = jnp.zeros((1, modes), F32)
    mine = info
    for j in reversed(range(count)):
        mine = jnp.where(j == me, info, mine)
        at = place(me, j, count)
        lead, spread, weight = (blocks_ref[at, k : k + 1, :] for k in range(3))
        along = lead / (1.0 + spread * info)
        edge_ref[1, j : j + 1, :] = along
        info = weight + lead * along * info
    info = mine
    for c in reversed(range(chunks)):
        enter_ref[1, c : c + 1, :] = info
        lead, spread, weight = (chunk_ref[k, c : c + 1, :] for k in range(3))
        info = weight + lead * lead * info / (1.0 + spread * info)

    v = enter_ref[0]
    run = None
    for i in range(CHUNK):
        d, seen, base = step_terms(i, chunks, first, q, r, decay_ref, seen_ref)
        ahead = d * d * v + base
        inverse = 1.0 / (ahead + r)
        retain = jnp.where(seen, r * inverse, 1.0)
        v = retain * ahead
        a = retain * d
        run = a if i == 0 else a * run
        a_ref[i] = a
        b_ref[i] = jnp.where(seen, ahead * inverse, 0.0)
        var_ref[i] = v
        whole_ref[0, i] = run
    carry_ref[0] = run

    info = enter_ref[1]
    run = jnp.ones(shape, F32)
    for i in reversed(range(CHUNK)):
        lead, spread, weight, inverse = element(*step_terms(i, chunks, first, q, r, decay_ref, seen_ref), r)
        d, seen, _ = step_terms(i, chunks, first, q, r, decay_ref, seen_ref)
        factor = 1.0 / (1.0 + spread * info)
        alpha = lead * factor
        info_ref[i] = info
        whole_ref[2, i] = run
        alpha_ref[i] = alpha
        beta_ref[i] = jnp.where(seen, d * inverse * factor, 0.0)
        info = weight + lead * alpha * info
        run = alpha * run
    carry_ref[1] = run

    along = jnp.ones((1, modes), F32)
    for c in range(chunks):
        enter_ref[0, c : c + 1, :] = along
        along = along * carry_ref[0, c : c + 1, :]
    along = jnp.ones((1, modes), F32)
    for c in reversed(range(chunks)):
        enter_ref[1, c : c + 1, :] = along
        along = along * carry_ref[1, c : c + 1, :]
    onward = enter_ref[0]
    back = enter_ref[1]
    for i in range(CHUNK):
        v = var_ref[i]
        keep = 1.0 / (1.0 + v * info_ref[i])
        lift = v * keep
        weight = whole_ref[0, i] * onward
        keep_ref[i] = keep
        lift_ref[i] = lift
        whole_ref[0, i] = weight
        whole_ref[1, i] = keep * weight
        whole_ref[2, i] = lift * (whole_ref[2, i] * back)
        put_rows(decay_ref, i, chunks, jnp.log(lift))
    unlanes(decay_ref, log_ref)


def means_kernel(parts, *refs):
    part_refs = refs[:parts]
    a_ref, b_ref, alpha_ref, beta_ref, keep_ref, lift_ref, carry_ref = refs[parts : parts + 7]
    coef_ref, mean_ref, smooth_ref, block_ref, enter_ref, strip_ref = refs[parts + 7 :]
    steps, modes = coef_ref.shape
    chunks = steps // CHUNK
    c = part_refs[0][...]
    for ref in part_refs[1:]:
        c = c + ref[...]
    coef_ref[...] = c
    lanes(coef_ref, strip_ref)
    f = e = jnp.zeros((chunks, modes), F32)
    for i in range(CHUNK):
        f = a_ref[i] * f + b_ref[i] * chunk_rows(strip_ref, i, chunks)
        k = CHUNK - 1 - i
        e = alpha_ref[k] * e + beta_ref[k] * chunk_rows(strip_ref, k, chunks)
    mean_ref[0] = f
    mean_ref[1] = e
    f = e = jnp.zeros((1, modes), F32)
    for c in range(chunks):
        k = chunks - 1 - c
        enter_ref[0, c : c + 1, :] = f
        enter_ref[1, k : k + 1, :] = e
        f = mean_ref[0, c : c + 1, :] + carry_ref[0, c : c + 1, :] * f
        e = mean_ref[1, k : k + 1, :] + carry_ref[1, k : k + 1, :] * e
    block_ref[0:1, :] = f
    block_ref[1:2, :] = e
    f = enter_ref[0]
    e = enter_ref[1]
    for i in range(CHUNK):
        f = a_ref[i] * f + b_ref[i] * chunk_rows(strip_ref, i, chunks)
        mean_ref[i] = f
    for i in reversed(range(CHUNK)):
        smooth_ref[i] = keep_ref[i] * mean_ref[i] + lift_ref[i] * e
        e = alpha_ref[i] * e + beta_ref[i] * chunk_rows(strip_ref, i, chunks)


def finish_kernel(count, me_ref, prior_ref, whole_ref, edge_ref, blocks_ref, mean_ref, smooth_ref, out_mean_ref, out_smooth_ref, mean_strip_ref, smooth_strip_ref):
    steps, modes = out_mean_ref.shape
    chunks = steps // CHUNK
    me = me_ref[0]
    f = prior_ref[...]
    e = jnp.zeros((1, modes), F32)
    for j in range(count - 1):
        f = jnp.where(j < me, blocks_ref[j, 0:1, :] + edge_ref[0, j : j + 1, :] * f, f)
        k = count - 1 - j
        e = jnp.where(k > me, blocks_ref[k, 1:2, :] + edge_ref[1, k : k + 1, :] * e, e)
    f = jnp.broadcast_to(f, (chunks, modes))
    e = jnp.broadcast_to(e, (chunks, modes))
    for i in range(CHUNK):
        put_rows(mean_strip_ref, i, chunks, mean_ref[i] + whole_ref[0, i] * f)
        put_rows(smooth_strip_ref, i, chunks, smooth_ref[i] + whole_ref[1, i] * f + whole_ref[2, i] * e)
    unlanes(mean_strip_ref, out_mean_ref)
    unlanes(smooth_strip_ref, out_smooth_ref)


def take_kernel(at_ref, slabs_ref, out_ref, sems):
    copies = [
        pltpu.make_async_copy(slabs_ref.at[at_ref[0], g], out_ref.at[g], sems.at[g]) for g in range(out_ref.shape[0])
    ]
    for copy in copies:
        copy.start()
    for copy in copies:
        copy.wait()


def take(slabs, half, limit):
    shape = slabs.shape[1:]
    return pl.pallas_call(
        take_kernel,
        in_specs=[pl.BlockSpec(memory_space=pltpu.SMEM), pl.BlockSpec(memory_space=pl.ANY)],
        out_specs=pl.BlockSpec(memory_space=pl.ANY),
        out_shape=jax.ShapeDtypeStruct(shape, slabs.dtype),
        scratch_shapes=[pltpu.SemaphoreType.DMA((shape[0],))],
        compiler_params=pltpu.CompilerParams(vmem_limit_bytes=limit * LIMIT // 16),
        cost_estimate=pl.CostEstimate(flops=0, bytes_accessed=2 * slabs.size, transcendentals=0),
    )(half.reshape(1), slabs)


def project_kernel(at_ref, slab_ref, basis_ref, out_ref):
    modes = out_ref.shape[1]
    columns = pl.ds(pl.multiple_of(at_ref[0] * modes, LANES), modes)
    for g in range(slab_ref.shape[0]):
        term = jnp.dot(slab_ref[g], basis_ref[g, :, columns], preferred_element_type=F32)
        out_ref[...] = term if g == 0 else out_ref[...] + term


def project(slabs, basis, owner, modes):
    count, steps, cells = slabs.shape
    return pl.pallas_call(
        project_kernel,
        in_specs=[
            pl.BlockSpec(memory_space=pltpu.SMEM),
            pl.BlockSpec(memory_space=pltpu.VMEM),
            pl.BlockSpec(memory_space=pltpu.VMEM),
        ],
        out_specs=pl.BlockSpec(memory_space=pltpu.VMEM),
        out_shape=jax.ShapeDtypeStruct((steps, modes), F32),
        compiler_params=pltpu.CompilerParams(vmem_limit_bytes=2 * LIMIT),
        cost_estimate=pl.CostEstimate(
            flops=2 * count * steps * cells * modes,
            bytes_accessed=2 * count * cells * (steps + modes) + 4 * steps * modes,
            transcendentals=0,
        ),
    )(owner.reshape(1), slabs, basis)


def call(kernel, inputs, outputs, scratch, flops):
    smem = pl.BlockSpec(memory_space=pltpu.SMEM)
    vmem = pl.BlockSpec(memory_space=pltpu.VMEM)
    moved = sum(4 * x.size for x in inputs) + sum(4 * x.size for x in outputs)
    return pl.pallas_call(
        kernel,
        in_specs=[smem if x.dtype == jnp.int32 else vmem for x in inputs],
        out_specs=[vmem] * len(outputs),
        out_shape=outputs,
        scratch_shapes=scratch,
        compiler_params=pltpu.CompilerParams(vmem_limit_bytes=LIMIT),
        cost_estimate=pl.CostEstimate(flops=flops, bytes_accessed=moved, transcendentals=0),
    )(*inputs)


def swap_halves(block, axis):
    half = lax.axis_size(axis) // 2
    return lax.ppermute(block, axis, [(i, (i + half) % (2 * half)) for i in range(2 * half)])


def project_all(slabs, basis, side, count, modes):
    arriving = []
    for turn in range(1, count):
        theirs = project(slabs, basis, lax.rem(side + turn, count), modes)
        arriving.append(lax.ppermute(theirs, "space", [(i, (i + turn) % count) for i in range(count)]))
    return [project(slabs, basis, side, modes)] + arriving


def body(observations, pod_basis, decay, step_mask, process_var, obs_var, prior_mean, prior_var):
    tm_count = lax.axis_size("tm")
    space_count = lax.axis_size("space")
    steps, modes = decay.shape
    chunks = steps // CHUNK
    rank = lax.axis_index("tm").astype(jnp.int32)
    me = rank.reshape(1)
    side = lax.axis_index("space").astype(jnp.int32)
    shape = functools.partial(jax.ShapeDtypeStruct, dtype=F32)
    area = pltpu.VMEM
    group = tm_count // 2
    groups = [[half * group + i for i in range(group)] for half in range(2)]
    half = rank // group

    seen = jnp.broadcast_to(step_mask.astype(F32)[:, None], (steps, modes))
    q, r = process_var[None, :], obs_var[None, :]
    flat = (chunks, modes)
    deep = (CHUNK, chunks, modes)
    strips = area((modes // LANES, steps, LANES), F32)
    slabs = observations.reshape(2, group, steps, observations.shape[3])
    far = take(slabs, 1 - half, 60)
    far, q = lax.optimization_barrier((far, q))
    far = lax.all_to_all(far, "tm", 0, 0, axis_index_groups=groups, tiled=True)
    chunk_totals, block_totals = call(
        totals_kernel, (me, decay, seen, q, r), [shape((3,) + flat), shape((3, modes))], [strips] * 2, 40 * steps * modes
    )
    block_totals, own_half = lax.optimization_barrier((block_totals, half))
    near = take(slabs, own_half, 60)
    basis = take(pod_basis.reshape(2, group, -1, pod_basis.shape[3]), own_half, 44)
    blocks = gather_near(block_totals, "tm")
    far, near, blocks = lax.optimization_barrier((far, near, blocks))
    near = lax.all_to_all(near, "tm", 0, 0, axis_index_groups=groups, tiled=True)
    terms = project_all(far, basis, side, space_count, modes)
    terms[0], blocks = lax.optimization_barrier((terms[0], blocks))
    rest = gather_far(blocks, "tm")
    crossing = sum(terms)
    rest, chunk_totals, _ = lax.optimization_barrier((rest, chunk_totals, crossing))
    crossing = swap_halves(crossing, "tm")
    blocks = jnp.concatenate([blocks] + rest, 0)
    *maps, whole, carry, edge, log_variance = call(
        functools.partial(gains_kernel, tm_count),
        (me, decay, seen, q, r, prior_var[None, :], chunk_totals, blocks),
        [shape(deep)] * 6 + [shape((3,) + deep), shape((2,) + flat), shape((2, tm_count, modes)), shape((steps, modes))],
        [area((2,) + flat, F32), area(deep, F32), area(deep, F32), strips, strips],
        80 * steps * modes,
    )
    near, carry = lax.optimization_barrier((near, carry))
    parts = project_all(near, basis, side, space_count, modes) + [crossing]

    coefficients, mean, smooth, ends = call(
        functools.partial(means_kernel, len(parts)),
        (*parts, *maps, carry),
        [shape((steps, modes)), shape(deep), shape(deep), shape((2, modes))],
        [area((2,) + flat, F32), strips],
        12 * steps * modes,
    )
    ends = jnp.broadcast_to(ends[None], (tm_count,) + ends.shape)
    ends = lax.all_to_all(ends, "tm", 0, 0, tiled=True)
    filtered, smoothed = call(
        functools.partial(finish_kernel, tm_count),
        (me, prior_mean[None, :], whole, edge, ends, mean, smooth),
        [shape((steps, modes))] * 2,
        [strips, strips],
        8 * steps * modes,
    )
    return coefficients, filtered, smoothed, log_variance


def solution(mesh):
    return jax.shard_map(
        body,
        mesh=mesh,
        in_specs=(
            P(None, "tm", "space", None),
            P(None, "space", None, None),
            P("tm", "space"),
            P("tm"),
            P("space"),
            P("space"),
            P("space"),
            P("space"),
        ),
        out_specs=(P("tm", "space"), P("tm", "space"), P("tm", "space"), P("tm", "space")),
        check_vma=False,
    )
```

```python
import functools

import jax
import jax.numpy as jnp
from jax import lax
from jax.experimental import pallas as pl
from jax.experimental.pallas import tpu as pltpu
from jax.sharding import PartitionSpec as P

CHUNK = 16
LANES = 128
F32 = jnp.float32
LIMIT = 16 * 1024 * 1024


def rotate(block, axis, turn, count, group, outer):
    route = []
    for i in range(count):
        low, high = i % group, i // group
        if outer:
            target = ((high + turn) % (count // group)) * group + low
        else:
            target = high * group + (low + turn) % group
        route.append((i, target))
    return lax.ppermute(block, axis, route)


def inner_size(count):
    group = 1
    while group * group < count:
        group *= 2
    return group if count % group == 0 else count


def gather_near(rows, axis):
    count = lax.axis_size(axis)
    group = inner_size(count)
    return jnp.stack([rows] + [rotate(rows, axis, s, count, group, False) for s in range(1, group)])


def gather_far(near, axis):
    count = lax.axis_size(axis)
    group = inner_size(count)
    return [rotate(near, axis, s, count, group, True) for s in range(1, count // group)]


def place(me, j, count):
    group = inner_size(count)
    rounds = count // group
    high = lax.rem(me // group - j // group + rounds, rounds)
    low = lax.rem(lax.rem(me, group) - j % group + group, group)
    return high * group + low


def lanes(ref, strip_ref):
    for m in range(strip_ref.shape[0]):
        strip_ref[m] = ref[:, m * LANES : (m + 1) * LANES]


def unlanes(strip_ref, ref):
    for m in range(strip_ref.shape[0]):
        ref[:, m * LANES : (m + 1) * LANES] = strip_ref[m]


def chunk_rows(strip_ref, i, chunks):
    rows = pl.ds(i, chunks, stride=CHUNK)
    return jnp.concatenate([strip_ref[m, rows, :] for m in range(strip_ref.shape[0])], 1)


def put_rows(strip_ref, i, chunks, value):
    rows = pl.ds(i, chunks, stride=CHUNK)
    for m in range(strip_ref.shape[0]):
        strip_ref[m, rows, :] = value[:, m * LANES : (m + 1) * LANES]


def opened(me_ref, shape):
    rows = lax.broadcasted_iota(jnp.int32, shape, 0)
    return jnp.logical_and(rows == 0, me_ref[0] == 0)


def step_terms(i, chunks, first, q, r, decay_ref, seen_ref):
    d = chunk_rows(decay_ref, i, chunks)
    seen = chunk_rows(seen_ref, i, chunks) > 0.5
    base = q
    if i == 0:
        d = jnp.where(first, 1.0, d)
        base = jnp.where(first, 0.0, q)
    return d, seen, base


def element(d, seen, base, r):
    inverse = 1.0 / (base + r)
    retain = jnp.where(seen, r * inverse, 1.0)
    return retain * d, retain * base, jnp.where(seen, d * d * inverse, 0.0), inverse


def join(early, late):
    lead, spread, weight = early
    lead_late, spread_late, weight_late = late
    factor = 1.0 / (1.0 + spread * weight_late)
    return (
        lead_late * factor * lead,
        lead_late * lead_late * factor * spread + spread_late,
        lead * lead * factor * weight_late + weight,
    )


def totals_kernel(me_ref, decay_in, seen_in, q_ref, r_ref, chunk_ref, block_ref, decay_ref, seen_ref):
    steps, modes = decay_in.shape
    lanes(decay_in, decay_ref)
    lanes(seen_in, seen_ref)
    chunks = steps // CHUNK
    shape = (chunks, modes)
    q = jnp.broadcast_to(q_ref[...], shape)
    r = jnp.broadcast_to(r_ref[...], shape)
    first = opened(me_ref, shape)
    total = None
    for i in range(CHUNK):
        step = element(*step_terms(i, chunks, first, q, r, decay_ref, seen_ref), r)[:3]
        total = step if i == 0 else join(total, step)
    for k in range(3):
        chunk_ref[k] = total[k]
    total = tuple(chunk_ref[k, 0:1, :] for k in range(3))
    for c in range(1, chunks):
        total = join(total, tuple(chunk_ref[k, c : c + 1, :] for k in range(3)))
    for k in range(3):
        block_ref[k : k + 1, :] = total[k]


def gains_kernel(
    count, me_ref, decay_in, seen_in, q_ref, r_ref, prior_ref, chunk_ref, blocks_ref,
    a_ref, b_ref, alpha_ref, beta_ref, keep_ref, lift_ref, whole_ref, carry_ref, edge_ref, log_ref,
    enter_ref, var_ref, info_ref, decay_ref, seen_ref,
):
    steps, modes = decay_in.shape
    lanes(decay_in, decay_ref)
    lanes(seen_in, seen_ref)
    chunks = steps // CHUNK
    shape = (chunks, modes)
    me = me_ref[0]
    q = jnp.broadcast_to(q_ref[...], shape)
    r = jnp.broadcast_to(r_ref[...], shape)
    first = opened(me_ref, shape)

    v = prior_ref[...]
    mine = v
    for j in range(count):
        mine = jnp.where(j == me, v, mine)
        at = place(me, j, count)
        lead, spread, weight = (blocks_ref[at, k : k + 1, :] for k in range(3))
        along = lead / (1.0 + weight * v)
        edge_ref[0, j : j + 1, :] = along
        v = spread + lead * along * v
    v = mine
    for c in range(chunks):
        enter_ref[0, c : c + 1, :] = v
        lead, spread, weight = (chunk_ref[k, c : c + 1, :] for k in range(3))
        v = spread + lead * lead * v / (1.0 + weight * v)

    info = jnp.zeros((1, modes), F32)
    mine = info
    for j in reversed(range(count)):
        mine = jnp.where(j == me, info, mine)
        at = place(me, j, count)
        lead, spread, weight = (blocks_ref[at, k : k + 1, :] for k in range(3))
        along = lead / (1.0 + spread * info)
        edge_ref[1, j : j + 1, :] = along
        info = weight + lead * along * info
    info = mine
    for c in reversed(range(chunks)):
        enter_ref[1, c : c + 1, :] = info
        lead, spread, weight = (chunk_ref[k, c : c + 1, :] for k in range(3))
        info = weight + lead * lead * info / (1.0 + spread * info)

    v = enter_ref[0]
    run = None
    for i in range(CHUNK):
        d, seen, base = step_terms(i, chunks, first, q, r, decay_ref, seen_ref)
        ahead = d * d * v + base
        inverse = 1.0 / (ahead + r)
        retain = jnp.where(seen, r * inverse, 1.0)
        v = retain * ahead
        a = retain * d
        run = a if i == 0 else a * run
        a_ref[i] = a
        b_ref[i] = jnp.where(seen, ahead * inverse, 0.0)
        var_ref[i] = v
        whole_ref[0, i] = run
    carry_ref[0] = run

    info = enter_ref[1]
    run = jnp.ones(shape, F32)
    for i in reversed(range(CHUNK)):
        lead, spread, weight, inverse = element(*step_terms(i, chunks, first, q, r, decay_ref, seen_ref), r)
        d, seen, _ = step_terms(i, chunks, first, q, r, decay_ref, seen_ref)
        factor = 1.0 / (1.0 + spread * info)
        alpha = lead * factor
        info_ref[i] = info
        whole_ref[2, i] = run
        alpha_ref[i] = alpha
        beta_ref[i] = jnp.where(seen, d * inverse * factor, 0.0)
        info = weight + lead * alpha * info
        run = alpha * run
    carry_ref[1] = run

    along = jnp.ones((1, modes), F32)
    for c in range(chunks):
        enter_ref[0, c : c + 1, :] = along
        along = along * carry_ref[0, c : c + 1, :]
    along = jnp.ones((1, modes), F32)
    for c in reversed(range(chunks)):
        enter_ref[1, c : c + 1, :] = along
        along = along * carry_ref[1, c : c + 1, :]
    onward = enter_ref[0]
    back = enter_ref[1]
    for i in range(CHUNK):
        v = var_ref[i]
        keep = 1.0 / (1.0 + v * info_ref[i])
        lift = v * keep
        weight = whole_ref[0, i] * onward
        keep_ref[i] = keep
        lift_ref[i] = lift
        whole_ref[0, i] = weight
        whole_ref[1, i] = keep * weight
        whole_ref[2, i] = lift * (whole_ref[2, i] * back)
        put_rows(decay_ref, i, chunks, jnp.log(lift))
    unlanes(decay_ref, log_ref)


def means_kernel(parts, *refs):
    part_refs = refs[:parts]
    a_ref, b_ref, alpha_ref, beta_ref, keep_ref, lift_ref, carry_ref = refs[parts : parts + 7]
    coef_ref, mean_ref, smooth_ref, block_ref, enter_ref, strip_ref = refs[parts + 7 :]
    steps, modes = coef_ref.shape
    chunks = steps // CHUNK
    c = part_refs[0][...]
    for ref in part_refs[1:]:
        c = c + ref[...]
    coef_ref[...] = c
    lanes(coef_ref, strip_ref)
    f = e = jnp.zeros((chunks, modes), F32)
    for i in range(CHUNK):
        f = a_ref[i] * f + b_ref[i] * chunk_rows(strip_ref, i, chunks)
        k = CHUNK - 1 - i
        e = alpha_ref[k] * e + beta_ref[k] * chunk_rows(strip_ref, k, chunks)
    mean_ref[0] = f
    mean_ref[1] = e
    f = e = jnp.zeros((1, modes), F32)
    for c in range(chunks):
        k = chunks - 1 - c
        enter_ref[0, c : c + 1, :] = f
        enter_ref[1, k : k + 1, :] = e
        f = mean_ref[0, c : c + 1, :] + carry_ref[0, c : c + 1, :] * f
        e = mean_ref[1, k : k + 1, :] + carry_ref[1, k : k + 1, :] * e
    block_ref[0:1, :] = f
    block_ref[1:2, :] = e
    f = enter_ref[0]
    e = enter_ref[1]
    for i in range(CHUNK):
        f = a_ref[i] * f + b_ref[i] * chunk_rows(strip_ref, i, chunks)
        mean_ref[i] = f
    for i in reversed(range(CHUNK)):
        smooth_ref[i] = keep_ref[i] * mean_ref[i] + lift_ref[i] * e
        e = alpha_ref[i] * e + beta_ref[i] * chunk_rows(strip_ref, i, chunks)


def finish_kernel(count, me_ref, prior_ref, whole_ref, edge_ref, blocks_ref, mean_ref, smooth_ref, out_mean_ref, out_smooth_ref, mean_strip_ref, smooth_strip_ref):
    steps, modes = out_mean_ref.shape
    chunks = steps // CHUNK
    me = me_ref[0]
    f = prior_ref[...]
    e = jnp.zeros((1, modes), F32)
    for j in range(count - 1):
        f = jnp.where(j < me, blocks_ref[j, 0:1, :] + edge_ref[0, j : j + 1, :] * f, f)
        k = count - 1 - j
        e = jnp.where(k > me, blocks_ref[k, 1:2, :] + edge_ref[1, k : k + 1, :] * e, e)
    f = jnp.broadcast_to(f, (chunks, modes))
    e = jnp.broadcast_to(e, (chunks, modes))
    for i in range(CHUNK):
        put_rows(mean_strip_ref, i, chunks, mean_ref[i] + whole_ref[0, i] * f)
        put_rows(smooth_strip_ref, i, chunks, smooth_ref[i] + whole_ref[1, i] * f + whole_ref[2, i] * e)
    unlanes(mean_strip_ref, out_mean_ref)
    unlanes(smooth_strip_ref, out_smooth_ref)


def cut_kernel(at_ref, slabs_ref, *refs):
    out_refs, sems = refs[:-1], refs[-1]
    copies = []
    for turn, ref in enumerate(out_refs):
        block = lax.bitwise_xor(at_ref[1], turn)
        copies.append(pltpu.make_async_copy(slabs_ref.at[at_ref[0], block], ref, sems.at[turn]))
    for copy in copies:
        copy.start()
    for copy in copies:
        copy.wait()


def cut(slabs, half, place, limit):
    count = slabs.shape[1]
    shape = slabs.shape[2:]
    return pl.pallas_call(
        cut_kernel,
        in_specs=[pl.BlockSpec(memory_space=pltpu.SMEM), pl.BlockSpec(memory_space=pl.ANY)],
        out_specs=[pl.BlockSpec(memory_space=pltpu.VMEM)] * count,
        out_shape=[jax.ShapeDtypeStruct(shape, slabs.dtype)] * count,
        scratch_shapes=[pltpu.SemaphoreType.DMA((count,))],
        compiler_params=pltpu.CompilerParams(vmem_limit_bytes=limit * LIMIT // 16),
        cost_estimate=pl.CostEstimate(flops=0, bytes_accessed=2 * slabs.size, transcendentals=0),
    )(jnp.stack([half, place]), slabs)


def stage_kernel(at_ref, basis_ref, out_ref, sems):
    copies = [
        pltpu.make_async_copy(basis_ref.at[at_ref[0], g], out_ref.at[g], sems.at[g]) for g in range(out_ref.shape[0])
    ]
    for copy in copies:
        copy.start()
    for copy in copies:
        copy.wait()


def stage(basis, half):
    shape = basis.shape[1:]
    return pl.pallas_call(
        stage_kernel,
        in_specs=[pl.BlockSpec(memory_space=pltpu.SMEM), pl.BlockSpec(memory_space=pl.ANY)],
        out_specs=pl.BlockSpec(memory_space=pltpu.VMEM),
        out_shape=jax.ShapeDtypeStruct(shape, basis.dtype),
        scratch_shapes=[pltpu.SemaphoreType.DMA((shape[0],))],
        compiler_params=pltpu.CompilerParams(vmem_limit_bytes=44 * LIMIT // 16),
        cost_estimate=pl.CostEstimate(flops=0, bytes_accessed=2 * basis.size, transcendentals=0),
    )(half.reshape(1), basis)


def project_kernel(at_ref, basis_ref, *refs):
    slab_refs, out_ref = refs[:-1], refs[-1]
    modes = out_ref.shape[1]
    columns = pl.ds(pl.multiple_of(at_ref[0] * modes, LANES), modes)
    for turn, slab_ref in enumerate(slab_refs):
        g = lax.bitwise_xor(at_ref[1], turn)
        term = jnp.dot(slab_ref[...], basis_ref[g, :, columns], preferred_element_type=F32)
        out_ref[...] = term if turn == 0 else out_ref[...] + term


def project(slabs, basis, owner, place, modes):
    count = len(slabs)
    steps, cells = slabs[0].shape
    return pl.pallas_call(
        project_kernel,
        in_specs=[pl.BlockSpec(memory_space=pltpu.SMEM)] + [pl.BlockSpec(memory_space=pltpu.VMEM)] * (count + 1),
        out_specs=pl.BlockSpec(memory_space=pltpu.VMEM),
        out_shape=jax.ShapeDtypeStruct((steps, modes), F32),
        compiler_params=pltpu.CompilerParams(vmem_limit_bytes=2 * LIMIT),
        cost_estimate=pl.CostEstimate(
            flops=2 * count * steps * cells * modes,
            bytes_accessed=2 * count * cells * (steps + modes) + 4 * steps * modes,
            transcendentals=0,
        ),
    )(jnp.stack([owner, place]), basis, *slabs)


def call(kernel, inputs, outputs, scratch, flops):
    smem = pl.BlockSpec(memory_space=pltpu.SMEM)
    vmem = pl.BlockSpec(memory_space=pltpu.VMEM)
    moved = sum(4 * x.size for x in inputs) + sum(4 * x.size for x in outputs)
    return pl.pallas_call(
        kernel,
        in_specs=[smem if x.dtype == jnp.int32 else vmem for x in inputs],
        out_specs=[vmem] * len(outputs),
        out_shape=outputs,
        scratch_shapes=scratch,
        compiler_params=pltpu.CompilerParams(vmem_limit_bytes=LIMIT),
        cost_estimate=pl.CostEstimate(flops=flops, bytes_accessed=moved, transcendentals=0),
    )(*inputs)


def swap_halves(block, axis):
    half = lax.axis_size(axis) // 2
    return lax.ppermute(block, axis, [(i, (i + half) % (2 * half)) for i in range(2 * half)])


def project_all(slabs, basis, side, place, count, modes):
    arriving = []
    for turn in range(1, count):
        theirs = project(slabs, basis, lax.rem(side + turn, count), place, modes)
        arriving.append(lax.ppermute(theirs, "space", [(i, (i + turn) % count) for i in range(count)]))
    return [project(slabs, basis, side, place, modes)] + arriving


def swap(block, axis, turn):
    return lax.ppermute(block, axis, [(i, i ^ turn) for i in range(lax.axis_size(axis))])


def body(observations, pod_basis, decay, step_mask, process_var, obs_var, prior_mean, prior_var):
    tm_count = lax.axis_size("tm")
    space_count = lax.axis_size("space")
    steps, modes = decay.shape
    chunks = steps // CHUNK
    rank = lax.axis_index("tm").astype(jnp.int32)
    me = rank.reshape(1)
    side = lax.axis_index("space").astype(jnp.int32)
    shape = functools.partial(jax.ShapeDtypeStruct, dtype=F32)
    area = pltpu.VMEM
    group = tm_count // 2
    half = rank // group

    seen = jnp.broadcast_to(step_mask.astype(F32)[:, None], (steps, modes))
    q, r = process_var[None, :], obs_var[None, :]
    flat = (chunks, modes)
    deep = (CHUNK, chunks, modes)
    strips = area((modes // LANES, steps, LANES), F32)
    slabs = observations.reshape(2, group, steps, observations.shape[3])
    inside = lax.rem(rank, group)
    far = cut(slabs, 1 - half, inside, 58)
    far, q = lax.optimization_barrier((far, q))
    turns = list(reversed(range(1, group)))
    far = [far[0]] + [swap(far[turn], "tm", turn) for turn in range(1, group)]
    chunk_totals, block_totals = call(
        totals_kernel, (me, decay, seen, q, r), [shape((3,) + flat), shape((3, modes))], [strips] * 2, 40 * steps * modes
    )
    block_totals, own_half = lax.optimization_barrier((block_totals, half))
    near = cut(slabs, own_half, inside, 52)
    basis = stage(pod_basis.reshape(2, group, -1, pod_basis.shape[3]), own_half)
    blocks = gather_near(block_totals, "tm")
    near, basis = lax.optimization_barrier((list(near), basis))
    for turn in turns:
        far[turn], near[turn], far[0] = lax.optimization_barrier((far[turn], near[turn], far[0]))
        near[turn] = swap(near[turn], "tm", turn)
    far[0], blocks = lax.optimization_barrier((far[0], blocks))
    terms = project_all(far, basis, side, inside, space_count, modes)
    terms[0], blocks = lax.optimization_barrier((terms[0], blocks))
    rest = gather_far(blocks, "tm")
    crossing = sum(terms)
    rest, chunk_totals, _ = lax.optimization_barrier((rest, chunk_totals, crossing))
    crossing = swap_halves(crossing, "tm")
    blocks = jnp.concatenate([blocks] + rest, 0)
    *maps, whole, carry, edge, log_variance = call(
        functools.partial(gains_kernel, tm_count),
        (me, decay, seen, q, r, prior_var[None, :], chunk_totals, blocks),
        [shape(deep)] * 6 + [shape((3,) + deep), shape((2,) + flat), shape((2, tm_count, modes)), shape((steps, modes))],
        [area((2,) + flat, F32), area(deep, F32), area(deep, F32), strips, strips],
        80 * steps * modes,
    )
    near[0], carry = lax.optimization_barrier((near[0], carry))
    parts = project_all(near, basis, side, inside, space_count, modes) + [crossing]

    coefficients, mean, smooth, ends = call(
        functools.partial(means_kernel, len(parts)),
        (*parts, *maps, carry),
        [shape((steps, modes)), shape(deep), shape(deep), shape((2, modes))],
        [area((2,) + flat, F32), strips],
        12 * steps * modes,
    )
    ends = jnp.broadcast_to(ends[None], (tm_count,) + ends.shape)
    ends = lax.all_to_all(ends, "tm", 0, 0, tiled=True)
    filtered, smoothed = call(
        functools.partial(finish_kernel, tm_count),
        (me, prior_mean[None, :], whole, edge, ends, mean, smooth),
        [shape((steps, modes))] * 2,
        [strips, strips],
        8 * steps * modes,
    )
    return coefficients, filtered, smoothed, log_variance


def solution(mesh):
    return jax.shard_map(
        body,
        mesh=mesh,
        in_specs=(
            P(None, "tm", "space", None),
            P(None, "space", None, None),
            P("tm", "space"),
            P("tm"),
            P("space"),
            P("space"),
            P("space"),
            P("space"),
        ),
        out_specs=(P("tm", "space"), P("tm", "space"), P("tm", "space"), P("tm", "space")),
        check_vma=False,
    )
```

```python
import functools

import jax
import jax.numpy as jnp
from jax import lax
from jax.experimental import pallas as pl
from jax.experimental.pallas import tpu as pltpu
from jax.sharding import PartitionSpec as P

CHUNK = 16
LANES = 128
F32 = jnp.float32
LIMIT = 16 * 1024 * 1024


def rotate(block, axis, turn, count, group, outer):
    route = []
    for i in range(count):
        low, high = i % group, i // group
        if outer:
            target = ((high + turn) % (count // group)) * group + low
        else:
            target = high * group + (low + turn) % group
        route.append((i, target))
    return lax.ppermute(block, axis, route)


def inner_size(count):
    group = 1
    while group * group < count:
        group *= 2
    return group if count % group == 0 else count


def gather_near(rows, axis):
    count = lax.axis_size(axis)
    group = inner_size(count)
    return jnp.stack([rows] + [rotate(rows, axis, s, count, group, False) for s in range(1, group)])


def gather_far(near, axis):
    count = lax.axis_size(axis)
    group = inner_size(count)
    return [rotate(near, axis, s, count, group, True) for s in range(1, count // group)]


def place(me, j, count):
    group = inner_size(count)
    rounds = count // group
    high = lax.rem(me // group - j // group + rounds, rounds)
    low = lax.rem(lax.rem(me, group) - j % group + group, group)
    return high * group + low


def lanes(ref, strip_ref):
    for m in range(strip_ref.shape[0]):
        strip_ref[m] = ref[:, m * LANES : (m + 1) * LANES]


def unlanes(strip_ref, ref):
    for m in range(strip_ref.shape[0]):
        ref[:, m * LANES : (m + 1) * LANES] = strip_ref[m]


def chunk_rows(strip_ref, i, chunks):
    rows = pl.ds(i, chunks, stride=CHUNK)
    return jnp.concatenate([strip_ref[m, rows, :] for m in range(strip_ref.shape[0])], 1)


def put_rows(strip_ref, i, chunks, value):
    rows = pl.ds(i, chunks, stride=CHUNK)
    for m in range(strip_ref.shape[0]):
        strip_ref[m, rows, :] = value[:, m * LANES : (m + 1) * LANES]


def opened(me_ref, shape):
    rows = lax.broadcasted_iota(jnp.int32, shape, 0)
    return jnp.logical_and(rows == 0, me_ref[0] == 0)


def step_terms(i, chunks, first, q, r, decay_ref, seen_ref):
    d = chunk_rows(decay_ref, i, chunks)
    seen = chunk_rows(seen_ref, i, chunks) > 0.5
    base = q
    if i == 0:
        d = jnp.where(first, 1.0, d)
        base = jnp.where(first, 0.0, q)
    return d, seen, base


def element(d, seen, base, r):
    inverse = 1.0 / (base + r)
    retain = jnp.where(seen, r * inverse, 1.0)
    return retain * d, retain * base, jnp.where(seen, d * d * inverse, 0.0), inverse


def join(early, late):
    lead, spread, weight = early
    lead_late, spread_late, weight_late = late
    factor = 1.0 / (1.0 + spread * weight_late)
    return (
        lead_late * factor * lead,
        lead_late * lead_late * factor * spread + spread_late,
        lead * lead * factor * weight_late + weight,
    )


def totals_kernel(me_ref, decay_in, seen_in, q_ref, r_ref, chunk_ref, block_ref, decay_ref, seen_ref):
    steps, modes = decay_in.shape
    lanes(decay_in, decay_ref)
    lanes(seen_in, seen_ref)
    chunks = steps // CHUNK
    shape = (chunks, modes)
    q = jnp.broadcast_to(q_ref[...], shape)
    r = jnp.broadcast_to(r_ref[...], shape)
    first = opened(me_ref, shape)
    total = None
    for i in range(CHUNK):
        step = element(*step_terms(i, chunks, first, q, r, decay_ref, seen_ref), r)[:3]
        total = step if i == 0 else join(total, step)
    for k in range(3):
        chunk_ref[k] = total[k]
    total = tuple(chunk_ref[k, 0:1, :] for k in range(3))
    for c in range(1, chunks):
        total = join(total, tuple(chunk_ref[k, c : c + 1, :] for k in range(3)))
    for k in range(3):
        block_ref[k : k + 1, :] = total[k]


def gains_kernel(
    count, me_ref, decay_in, seen_in, q_ref, r_ref, prior_ref, chunk_ref, blocks_ref,
    a_ref, b_ref, alpha_ref, beta_ref, keep_ref, lift_ref, whole_ref, carry_ref, edge_ref, log_ref,
    enter_ref, var_ref, info_ref, decay_ref, seen_ref,
):
    steps, modes = decay_in.shape
    lanes(decay_in, decay_ref)
    lanes(seen_in, seen_ref)
    chunks = steps // CHUNK
    shape = (chunks, modes)
    me = me_ref[0]
    q = jnp.broadcast_to(q_ref[...], shape)
    r = jnp.broadcast_to(r_ref[...], shape)
    first = opened(me_ref, shape)

    v = prior_ref[...]
    mine = v
    for j in range(count):
        mine = jnp.where(j == me, v, mine)
        at = place(me, j, count)
        lead, spread, weight = (blocks_ref[at, k : k + 1, :] for k in range(3))
        along = lead / (1.0 + weight * v)
        edge_ref[0, j : j + 1, :] = along
        v = spread + lead * along * v
    v = mine
    for c in range(chunks):
        enter_ref[0, c : c + 1, :] = v
        lead, spread, weight = (chunk_ref[k, c : c + 1, :] for k in range(3))
        v = spread + lead * lead * v / (1.0 + weight * v)

    info = jnp.zeros((1, modes), F32)
    mine = info
    for j in reversed(range(count)):
        mine = jnp.where(j == me, info, mine)
        at = place(me, j, count)
        lead, spread, weight = (blocks_ref[at, k : k + 1, :] for k in range(3))
        along = lead / (1.0 + spread * info)
        edge_ref[1, j : j + 1, :] = along
        info = weight + lead * along * info
    info = mine
    for c in reversed(range(chunks)):
        enter_ref[1, c : c + 1, :] = info
        lead, spread, weight = (chunk_ref[k, c : c + 1, :] for k in range(3))
        info = weight + lead * lead * info / (1.0 + spread * info)

    v = enter_ref[0]
    run = None
    for i in range(CHUNK):
        d, seen, base = step_terms(i, chunks, first, q, r, decay_ref, seen_ref)
        ahead = d * d * v + base
        inverse = 1.0 / (ahead + r)
        retain = jnp.where(seen, r * inverse, 1.0)
        v = retain * ahead
        a = retain * d
        run = a if i == 0 else a * run
        a_ref[i] = a
        b_ref[i] = jnp.where(seen, ahead * inverse, 0.0)
        var_ref[i] = v
        whole_ref[0, i] = run
    carry_ref[0] = run

    info = enter_ref[1]
    run = jnp.ones(shape, F32)
    for i in reversed(range(CHUNK)):
        lead, spread, weight, inverse = element(*step_terms(i, chunks, first, q, r, decay_ref, seen_ref), r)
        d, seen, _ = step_terms(i, chunks, first, q, r, decay_ref, seen_ref)
        factor = 1.0 / (1.0 + spread * info)
        alpha = lead * factor
        info_ref[i] = info
        whole_ref[2, i] = run
        alpha_ref[i] = alpha
        beta_ref[i] = jnp.where(seen, d * inverse * factor, 0.0)
        info = weight + lead * alpha * info
        run = alpha * run
    carry_ref[1] = run

    along = jnp.ones((1, modes), F32)
    for c in range(chunks):
        enter_ref[0, c : c + 1, :] = along
        along = along * carry_ref[0, c : c + 1, :]
    along = jnp.ones((1, modes), F32)
    for c in reversed(range(chunks)):
        enter_ref[1, c : c + 1, :] = along
        along = along * carry_ref[1, c : c + 1, :]
    onward = enter_ref[0]
    back = enter_ref[1]
    for i in range(CHUNK):
        v = var_ref[i]
        keep = 1.0 / (1.0 + v * info_ref[i])
        lift = v * keep
        weight = whole_ref[0, i] * onward
        keep_ref[i] = keep
        lift_ref[i] = lift
        whole_ref[0, i] = weight
        whole_ref[1, i] = keep * weight
        whole_ref[2, i] = lift * (whole_ref[2, i] * back)
        put_rows(decay_ref, i, chunks, jnp.log(lift))
    unlanes(decay_ref, log_ref)


def means_kernel(parts, *refs):
    part_refs = refs[:parts]
    a_ref, b_ref, alpha_ref, beta_ref, keep_ref, lift_ref, carry_ref = refs[parts : parts + 7]
    coef_ref, mean_ref, smooth_ref, block_ref, enter_ref, strip_ref = refs[parts + 7 :]
    steps, modes = coef_ref.shape
    chunks = steps // CHUNK
    c = part_refs[0][...]
    for ref in part_refs[1:]:
        c = c + ref[...]
    coef_ref[...] = c
    lanes(coef_ref, strip_ref)
    f = e = jnp.zeros((chunks, modes), F32)
    for i in range(CHUNK):
        f = a_ref[i] * f + b_ref[i] * chunk_rows(strip_ref, i, chunks)
        k = CHUNK - 1 - i
        e = alpha_ref[k] * e + beta_ref[k] * chunk_rows(strip_ref, k, chunks)
    mean_ref[0] = f
    mean_ref[1] = e
    f = e = jnp.zeros((1, modes), F32)
    for c in range(chunks):
        k = chunks - 1 - c
        enter_ref[0, c : c + 1, :] = f
        enter_ref[1, k : k + 1, :] = e
        f = mean_ref[0, c : c + 1, :] + carry_ref[0, c : c + 1, :] * f
        e = mean_ref[1, k : k + 1, :] + carry_ref[1, k : k + 1, :] * e
    block_ref[0:1, :] = f
    block_ref[1:2, :] = e
    f = enter_ref[0]
    e = enter_ref[1]
    for i in range(CHUNK):
        f = a_ref[i] * f + b_ref[i] * chunk_rows(strip_ref, i, chunks)
        mean_ref[i] = f
    for i in reversed(range(CHUNK)):
        smooth_ref[i] = keep_ref[i] * mean_ref[i] + lift_ref[i] * e
        e = alpha_ref[i] * e + beta_ref[i] * chunk_rows(strip_ref, i, chunks)


def finish_kernel(count, me_ref, prior_ref, whole_ref, edge_ref, blocks_ref, mean_ref, smooth_ref, out_mean_ref, out_smooth_ref, mean_strip_ref, smooth_strip_ref):
    steps, modes = out_mean_ref.shape
    chunks = steps // CHUNK
    me = me_ref[0]
    f = prior_ref[...]
    e = jnp.zeros((1, modes), F32)
    for j in range(count - 1):
        f = jnp.where(j < me, blocks_ref[j, 0:1, :] + edge_ref[0, j : j + 1, :] * f, f)
        k = count - 1 - j
        e = jnp.where(k > me, blocks_ref[k, 1:2, :] + edge_ref[1, k : k + 1, :] * e, e)
    f = jnp.broadcast_to(f, (chunks, modes))
    e = jnp.broadcast_to(e, (chunks, modes))
    for i in range(CHUNK):
        put_rows(mean_strip_ref, i, chunks, mean_ref[i] + whole_ref[0, i] * f)
        put_rows(smooth_strip_ref, i, chunks, smooth_ref[i] + whole_ref[1, i] * f + whole_ref[2, i] * e)
    unlanes(mean_strip_ref, out_mean_ref)
    unlanes(smooth_strip_ref, out_smooth_ref)


def project_kernel(at_ref, slab_ref, basis_ref, out_ref, slab_area, basis_area, slab_sems, basis_sems):
    count = slab_ref.shape[0]
    modes = out_ref.shape[1]
    columns = pl.ds(pl.multiple_of(at_ref[1] * modes, LANES), modes)
    copies = []
    for g in range(count):
        copies.append((
            pltpu.make_async_copy(slab_ref.at[g], slab_area.at[g], slab_sems.at[g]),
            pltpu.make_async_copy(basis_ref.at[at_ref[0] + g, :, columns], basis_area.at[g], basis_sems.at[g]),
        ))
    for pair in copies:
        for copy in pair:
            copy.start()
    for g in range(count):
        for copy in copies[g]:
            copy.wait()
        term = jnp.dot(slab_area[g], basis_area[g], preferred_element_type=F32)
        out_ref[...] = term if g == 0 else out_ref[...] + term


def project(slabs, basis, first, owner, modes):
    count, steps, cells = slabs.shape
    return pl.pallas_call(
        project_kernel,
        in_specs=[
            pl.BlockSpec(memory_space=pltpu.SMEM),
            pl.BlockSpec(memory_space=pl.ANY),
            pl.BlockSpec(memory_space=pl.ANY),
        ],
        out_specs=pl.BlockSpec(memory_space=pltpu.VMEM),
        out_shape=jax.ShapeDtypeStruct((steps, modes), F32),
        scratch_shapes=[
            pltpu.VMEM(slabs.shape, slabs.dtype),
            pltpu.VMEM((count, cells, modes), basis.dtype),
            pltpu.SemaphoreType.DMA((count,)),
            pltpu.SemaphoreType.DMA((count,)),
        ],
        compiler_params=pltpu.CompilerParams(vmem_limit_bytes=60 * LIMIT // 16),
        cost_estimate=pl.CostEstimate(
            flops=2 * count * steps * cells * modes,
            bytes_accessed=2 * count * cells * (steps + modes) + 4 * steps * modes,
            transcendentals=0,
        ),
    )(jnp.stack([first, owner]), slabs, basis)


def call(kernel, inputs, outputs, scratch, flops):
    smem = pl.BlockSpec(memory_space=pltpu.SMEM)
    vmem = pl.BlockSpec(memory_space=pltpu.VMEM)
    moved = sum(4 * x.size for x in inputs) + sum(4 * x.size for x in outputs)
    return pl.pallas_call(
        kernel,
        in_specs=[smem if x.dtype == jnp.int32 else vmem for x in inputs],
        out_specs=[vmem] * len(outputs),
        out_shape=outputs,
        scratch_shapes=scratch,
        compiler_params=pltpu.CompilerParams(vmem_limit_bytes=LIMIT),
        cost_estimate=pl.CostEstimate(flops=flops, bytes_accessed=moved, transcendentals=0),
    )(*inputs)


def swap_halves(block, axis):
    half = lax.axis_size(axis) // 2
    return lax.ppermute(block, axis, [(i, (i + half) % (2 * half)) for i in range(2 * half)])


def send_along(term, axis, turn):
    count = lax.axis_size(axis)
    return lax.ppermute(term, axis, [(i, (i + turn) % count) for i in range(count)])


def body(observations, pod_basis, decay, step_mask, process_var, obs_var, prior_mean, prior_var):
    tm_count = lax.axis_size("tm")
    space_count = lax.axis_size("space")
    steps, modes = decay.shape
    chunks = steps // CHUNK
    rank = lax.axis_index("tm").astype(jnp.int32)
    me = rank.reshape(1)
    side = lax.axis_index("space").astype(jnp.int32)
    shape = functools.partial(jax.ShapeDtypeStruct, dtype=F32)
    area = pltpu.VMEM
    group = tm_count // 2
    groups = [[half * group + i for i in range(group)] for half in range(2)]
    half = rank // group

    seen = jnp.broadcast_to(step_mask.astype(F32)[:, None], (steps, modes))
    q, r = process_var[None, :], obs_var[None, :]
    flat = (chunks, modes)
    deep = (CHUNK, chunks, modes)
    strips = area((modes // LANES, steps, LANES), F32)
    slabs = observations.reshape(2, group, steps, observations.shape[3])
    basis = pod_basis.reshape(tm_count, -1, pod_basis.shape[3])
    first = half * group
    others = [lax.rem(side + turn, space_count) for turn in range(1, space_count)]
    far = lax.dynamic_index_in_dim(slabs, 1 - half, 0, keepdims=False)
    far, q = lax.optimization_barrier((far, q))
    far = lax.all_to_all(far, "tm", 0, 0, axis_index_groups=groups, tiled=True)
    chunk_totals, block_totals = call(
        totals_kernel, (me, decay, seen, q, r), [shape((3,) + flat), shape((3, modes))], [strips] * 2, 40 * steps * modes
    )
    block_totals, own_half = lax.optimization_barrier((block_totals, half))
    near = lax.dynamic_index_in_dim(slabs, own_half, 0, keepdims=False)
    blocks = gather_near(block_totals, "tm")
    far, near, blocks = lax.optimization_barrier((far, near, blocks))
    near = lax.all_to_all(near, "tm", 0, 0, axis_index_groups=groups, tiled=True)

    theirs = [project(far, basis, first, owner, modes) for owner in others]
    arriving = [send_along(term, "space", turn + 1) for turn, term in enumerate(theirs)]
    crossing = sum(arriving, project(far, basis, first, side, modes))
    _, blocks = lax.optimization_barrier((theirs, blocks))
    rest = gather_far(blocks, "tm")
    rest, near, _ = lax.optimization_barrier((rest, near, crossing))
    crossing = swap_halves(crossing, "tm")
    blocks = jnp.concatenate([blocks] + rest, 0)

    theirs = [project(near, basis, first, owner, modes) for owner in others]
    parts = [send_along(term, "space", turn + 1) for turn, term in enumerate(theirs)] + [crossing]
    chunk_totals, own_near, _ = lax.optimization_barrier((chunk_totals, near, theirs))
    parts.append(project(own_near, basis, first, side, modes))
    *maps, whole, carry, edge, log_variance = call(
        functools.partial(gains_kernel, tm_count),
        (me, decay, seen, q, r, prior_var[None, :], chunk_totals, blocks),
        [shape(deep)] * 6 + [shape((3,) + deep), shape((2,) + flat), shape((2, tm_count, modes)), shape((steps, modes))],
        [area((2,) + flat, F32), area(deep, F32), area(deep, F32), strips, strips],
        80 * steps * modes,
    )

    coefficients, mean, smooth, ends = call(
        functools.partial(means_kernel, len(parts)),
        (*parts, *maps, carry),
        [shape((steps, modes)), shape(deep), shape(deep), shape((2, modes))],
        [area((2,) + flat, F32), strips],
        12 * steps * modes,
    )
    ends = jnp.broadcast_to(ends[None], (tm_count,) + ends.shape)
    ends = lax.all_to_all(ends, "tm", 0, 0, tiled=True)
    filtered, smoothed = call(
        functools.partial(finish_kernel, tm_count),
        (me, prior_mean[None, :], whole, edge, ends, mean, smooth),
        [shape((steps, modes))] * 2,
        [strips, strips],
        8 * steps * modes,
    )
    return coefficients, filtered, smoothed, log_variance


def solution(mesh):
    return jax.shard_map(
        body,
        mesh=mesh,
        in_specs=(
            P(None, "tm", "space", None),
            P(None, "space", None, None),
            P("tm", "space"),
            P("tm"),
            P("space"),
            P("space"),
            P("space"),
            P("space"),
        ),
        out_specs=(P("tm", "space"), P("tm", "space"), P("tm", "space"), P("tm", "space")),
        check_vma=False,
    )
```

```python
import functools

import jax
import jax.numpy as jnp
from jax import lax
from jax.experimental import pallas as pl
from jax.experimental.pallas import tpu as pltpu
from jax.sharding import PartitionSpec as P

CHUNK = 16
LANES = 128
PAD = 16
STEPS16 = 32767.0
TINY = 1e-30
F32 = jnp.float32
LIMIT = 16 * 1024 * 1024


def rotate(block, axis, turn, count, group, outer):
    route = []
    for i in range(count):
        low, high = i % group, i // group
        if outer:
            target = ((high + turn) % (count // group)) * group + low
        else:
            target = high * group + (low + turn) % group
        route.append((i, target))
    return lax.ppermute(block, axis, route)


def inner_size(count):
    group = 1
    while group * group < count:
        group *= 2
    return group if count % group == 0 else count


def gather_near(rows, axis):
    count = lax.axis_size(axis)
    group = inner_size(count)
    return jnp.stack([rows] + [rotate(rows, axis, s, count, group, False) for s in range(1, group)])


def gather_far(near, axis):
    count = lax.axis_size(axis)
    group = inner_size(count)
    return [rotate(near, axis, s, count, group, True) for s in range(1, count // group)]


def place(me, j, count):
    group = inner_size(count)
    rounds = count // group
    high = lax.rem(me // group - j // group + rounds, rounds)
    low = lax.rem(lax.rem(me, group) - j % group + group, group)
    return high * group + low


def lanes(ref, strip_ref):
    for m in range(strip_ref.shape[0]):
        strip_ref[m] = ref[:, m * LANES : (m + 1) * LANES]


def unlanes(strip_ref, ref):
    for m in range(strip_ref.shape[0]):
        ref[:, m * LANES : (m + 1) * LANES] = strip_ref[m]


def chunk_rows(strip_ref, i, chunks):
    rows = pl.ds(i, chunks, stride=CHUNK)
    return jnp.concatenate([strip_ref[m, rows, :] for m in range(strip_ref.shape[0])], 1)


def put_rows(strip_ref, i, chunks, value):
    rows = pl.ds(i, chunks, stride=CHUNK)
    for m in range(strip_ref.shape[0]):
        strip_ref[m, rows, :] = value[:, m * LANES : (m + 1) * LANES]


def opened(me_ref, shape):
    rows = lax.broadcasted_iota(jnp.int32, shape, 0)
    return jnp.logical_and(rows == 0, me_ref[0] == 0)


def step_terms(i, chunks, first, q, r, decay_ref, seen_ref):
    d = chunk_rows(decay_ref, i, chunks)
    seen = chunk_rows(seen_ref, i, chunks) > 0.5
    base = q
    if i == 0:
        d = jnp.where(first, 1.0, d)
        base = jnp.where(first, 0.0, q)
    return d, seen, base


def element(d, seen, base, r):
    inverse = 1.0 / (base + r)
    retain = jnp.where(seen, r * inverse, 1.0)
    return retain * d, retain * base, jnp.where(seen, d * d * inverse, 0.0), inverse


def join(early, late):
    lead, spread, weight = early
    lead_late, spread_late, weight_late = late
    factor = 1.0 / (1.0 + spread * weight_late)
    return (
        lead_late * factor * lead,
        lead_late * lead_late * factor * spread + spread_late,
        lead * lead * factor * weight_late + weight,
    )


def totals_kernel(me_ref, decay_in, seen_in, q_ref, r_ref, chunk_ref, block_ref, decay_ref, seen_ref):
    steps, modes = decay_in.shape
    lanes(decay_in, decay_ref)
    lanes(seen_in, seen_ref)
    chunks = steps // CHUNK
    shape = (chunks, modes)
    q = jnp.broadcast_to(q_ref[...], shape)
    r = jnp.broadcast_to(r_ref[...], shape)
    first = opened(me_ref, shape)
    total = None
    for i in range(CHUNK):
        step = element(*step_terms(i, chunks, first, q, r, decay_ref, seen_ref), r)[:3]
        total = step if i == 0 else join(total, step)
    for k in range(3):
        chunk_ref[k] = total[k]
    total = tuple(chunk_ref[k, 0:1, :] for k in range(3))
    for c in range(1, chunks):
        total = join(total, tuple(chunk_ref[k, c : c + 1, :] for k in range(3)))
    for k in range(3):
        block_ref[k : k + 1, :] = total[k]


def gains_kernel(
    count, me_ref, decay_in, seen_in, q_ref, r_ref, prior_ref, chunk_ref, blocks_ref,
    a_ref, b_ref, alpha_ref, beta_ref, keep_ref, lift_ref, whole_ref, carry_ref, edge_ref, log_ref,
    enter_ref, var_ref, info_ref, decay_ref, seen_ref,
):
    steps, modes = decay_in.shape
    lanes(decay_in, decay_ref)
    lanes(seen_in, seen_ref)
    chunks = steps // CHUNK
    shape = (chunks, modes)
    me = me_ref[0]
    q = jnp.broadcast_to(q_ref[...], shape)
    r = jnp.broadcast_to(r_ref[...], shape)
    first = opened(me_ref, shape)

    v = prior_ref[...]
    mine = v
    for j in range(count):
        mine = jnp.where(j == me, v, mine)
        at = place(me, j, count)
        lead, spread, weight = (blocks_ref[at, k : k + 1, :] for k in range(3))
        along = lead / (1.0 + weight * v)
        edge_ref[0, j : j + 1, :] = along
        v = spread + lead * along * v
    v = mine
    for c in range(chunks):
        enter_ref[0, c : c + 1, :] = v
        lead, spread, weight = (chunk_ref[k, c : c + 1, :] for k in range(3))
        v = spread + lead * lead * v / (1.0 + weight * v)

    info = jnp.zeros((1, modes), F32)
    mine = info
    for j in reversed(range(count)):
        mine = jnp.where(j == me, info, mine)
        at = place(me, j, count)
        lead, spread, weight = (blocks_ref[at, k : k + 1, :] for k in range(3))
        along = lead / (1.0 + spread * info)
        edge_ref[1, j : j + 1, :] = along
        info = weight + lead * along * info
    info = mine
    for c in reversed(range(chunks)):
        enter_ref[1, c : c + 1, :] = info
        lead, spread, weight = (chunk_ref[k, c : c + 1, :] for k in range(3))
        info = weight + lead * lead * info / (1.0 + spread * info)

    v = enter_ref[0]
    run = None
    for i in range(CHUNK):
        d, seen, base = step_terms(i, chunks, first, q, r, decay_ref, seen_ref)
        ahead = d * d * v + base
        inverse = 1.0 / (ahead + r)
        retain = jnp.where(seen, r * inverse, 1.0)
        v = retain * ahead
        a = retain * d
        run = a if i == 0 else a * run
        a_ref[i] = a
        b_ref[i] = jnp.where(seen, ahead * inverse, 0.0)
        var_ref[i] = v
        whole_ref[0, i] = run
    carry_ref[0] = run

    info = enter_ref[1]
    run = jnp.ones(shape, F32)
    for i in reversed(range(CHUNK)):
        lead, spread, weight, inverse = element(*step_terms(i, chunks, first, q, r, decay_ref, seen_ref), r)
        d, seen, _ = step_terms(i, chunks, first, q, r, decay_ref, seen_ref)
        factor = 1.0 / (1.0 + spread * info)
        alpha = lead * factor
        info_ref[i] = info
        whole_ref[2, i] = run
        alpha_ref[i] = alpha
        beta_ref[i] = jnp.where(seen, d * inverse * factor, 0.0)
        info = weight + lead * alpha * info
        run = alpha * run
    carry_ref[1] = run

    along = jnp.ones((1, modes), F32)
    for c in range(chunks):
        enter_ref[0, c : c + 1, :] = along
        along = along * carry_ref[0, c : c + 1, :]
    along = jnp.ones((1, modes), F32)
    for c in reversed(range(chunks)):
        enter_ref[1, c : c + 1, :] = along
        along = along * carry_ref[1, c : c + 1, :]
    onward = enter_ref[0]
    back = enter_ref[1]
    for i in range(CHUNK):
        v = var_ref[i]
        keep = 1.0 / (1.0 + v * info_ref[i])
        lift = v * keep
        weight = whole_ref[0, i] * onward
        keep_ref[i] = keep
        lift_ref[i] = lift
        whole_ref[0, i] = weight
        whole_ref[1, i] = keep * weight
        whole_ref[2, i] = lift * (whole_ref[2, i] * back)
        put_rows(decay_ref, i, chunks, jnp.log(lift))
    unlanes(decay_ref, log_ref)


def means_kernel(parts, *refs):
    part_refs = refs[:parts]
    a_ref, b_ref, alpha_ref, beta_ref, keep_ref, lift_ref, carry_ref = refs[parts : parts + 7]
    coef_ref, mean_ref, smooth_ref, block_ref, enter_ref, strip_ref = refs[parts + 7 :]
    steps, modes = coef_ref.shape
    chunks = steps // CHUNK
    c = part_refs[0][...]
    for ref in part_refs[1:]:
        c = c + decode(ref)
    coef_ref[...] = c
    lanes(coef_ref, strip_ref)
    f = e = jnp.zeros((chunks, modes), F32)
    for i in range(CHUNK):
        f = a_ref[i] * f + b_ref[i] * chunk_rows(strip_ref, i, chunks)
        k = CHUNK - 1 - i
        e = alpha_ref[k] * e + beta_ref[k] * chunk_rows(strip_ref, k, chunks)
    mean_ref[0] = f
    mean_ref[1] = e
    f = e = jnp.zeros((1, modes), F32)
    for c in range(chunks):
        k = chunks - 1 - c
        enter_ref[0, c : c + 1, :] = f
        enter_ref[1, k : k + 1, :] = e
        f = mean_ref[0, c : c + 1, :] + carry_ref[0, c : c + 1, :] * f
        e = mean_ref[1, k : k + 1, :] + carry_ref[1, k : k + 1, :] * e
    block_ref[0:1, :] = f
    block_ref[1:2, :] = e
    f = enter_ref[0]
    e = enter_ref[1]
    for i in range(CHUNK):
        f = a_ref[i] * f + b_ref[i] * chunk_rows(strip_ref, i, chunks)
        mean_ref[i] = f
    for i in reversed(range(CHUNK)):
        smooth_ref[i] = keep_ref[i] * mean_ref[i] + lift_ref[i] * e
        e = alpha_ref[i] * e + beta_ref[i] * chunk_rows(strip_ref, i, chunks)


def finish_kernel(count, me_ref, prior_ref, whole_ref, edge_ref, blocks_ref, mean_ref, smooth_ref, out_mean_ref, out_smooth_ref, mean_strip_ref, smooth_strip_ref):
    steps, modes = out_mean_ref.shape
    chunks = steps // CHUNK
    me = me_ref[0]
    f = prior_ref[...]
    e = jnp.zeros((1, modes), F32)
    for j in range(count - 1):
        f = jnp.where(j < me, blocks_ref[j, 0:1, :] + edge_ref[0, j : j + 1, :] * f, f)
        k = count - 1 - j
        e = jnp.where(k > me, blocks_ref[k, 1:2, :] + edge_ref[1, k : k + 1, :] * e, e)
    f = jnp.broadcast_to(f, (chunks, modes))
    e = jnp.broadcast_to(e, (chunks, modes))
    for i in range(CHUNK):
        put_rows(mean_strip_ref, i, chunks, mean_ref[i] + whole_ref[0, i] * f)
        put_rows(smooth_strip_ref, i, chunks, smooth_ref[i] + whole_ref[1, i] * f + whole_ref[2, i] * e)
    unlanes(mean_strip_ref, out_mean_ref)
    unlanes(smooth_strip_ref, out_smooth_ref)


def encode(values, ref):
    steps = values.shape[0]
    top = jnp.max(jnp.abs(values), axis=0, keepdims=True)
    power = jnp.floor(jnp.log2(jnp.maximum(top, TINY))) + 1.0
    coded = jnp.floor(values * (jnp.exp2(-power) * STEPS16) + 0.5)
    ref[0:steps, :] = jnp.clip(coded, -STEPS16, STEPS16).astype(jnp.int32).astype(jnp.int16)
    power = jnp.broadcast_to(power, (PAD, power.shape[1]))
    ref[steps : steps + PAD, :] = power.astype(jnp.int32).astype(jnp.int16)


def decode(ref):
    steps = ref.shape[0] - PAD
    power = ref[steps : steps + PAD, :].astype(jnp.int32).astype(F32)[0:1, :]
    return ref[0:steps, :].astype(jnp.int32).astype(F32) * (jnp.exp2(power) * (1.0 / STEPS16))


def project_kernel(at_ref, slab_ref, basis_ref, own_ref, *refs):
    owners = at_ref.shape[0] - 1
    coded_refs = refs[: owners - 1]
    slab_area, basis_area, sum_area, slab_sems, basis_sems = refs[owners - 1 :]
    count = slab_ref.shape[0]
    modes = own_ref.shape[1]
    copies = []
    for g in range(count):
        copies.append((
            pltpu.make_async_copy(slab_ref.at[g], slab_area.at[g], slab_sems.at[g]),
            pltpu.make_async_copy(basis_ref.at[at_ref[0] + g], basis_area.at[g], basis_sems.at[g]),
        ))
    for pair in copies:
        for copy in pair:
            copy.start()
    for g in range(count):
        for copy in copies[g]:
            copy.wait()
        for turn in range(owners):
            columns = pl.ds(pl.multiple_of(at_ref[1 + turn] * modes, LANES), modes)
            term = jnp.dot(slab_area[g], basis_area[g, :, columns], preferred_element_type=F32)
            sum_area[turn] = term if g == 0 else sum_area[turn] + term
    own_ref[...] = sum_area[0]
    for turn in range(1, owners):
        encode(sum_area[turn], coded_refs[turn - 1])


def project(slabs, basis, first, owners, modes):
    count, steps, cells = slabs.shape
    others = len(owners) - 1
    own, *coded = pl.pallas_call(
        project_kernel,
        in_specs=[
            pl.BlockSpec(memory_space=pltpu.SMEM),
            pl.BlockSpec(memory_space=pl.ANY),
            pl.BlockSpec(memory_space=pl.ANY),
        ],
        out_specs=[pl.BlockSpec(memory_space=pltpu.VMEM)] * (1 + others),
        out_shape=[jax.ShapeDtypeStruct((steps, modes), F32)]
        + [jax.ShapeDtypeStruct((steps + PAD, modes), jnp.int16)] * others,
        scratch_shapes=[
            pltpu.VMEM(slabs.shape, slabs.dtype),
            pltpu.VMEM((count,) + basis.shape[1:], basis.dtype),
            pltpu.VMEM((1 + others, steps, modes), F32),
            pltpu.SemaphoreType.DMA((count,)),
            pltpu.SemaphoreType.DMA((count,)),
        ],
        compiler_params=pltpu.CompilerParams(vmem_limit_bytes=60 * LIMIT // 16),
        cost_estimate=pl.CostEstimate(
            flops=2 * count * steps * cells * modes * (1 + others),
            bytes_accessed=2 * count * cells * (steps + modes * (1 + others)) + 4 * steps * modes,
            transcendentals=0,
        ),
    )(jnp.stack([first] + owners), slabs, basis)
    return own, coded


def fold_kernel(own_ref, *refs):
    total = own_ref[...]
    for ref in refs[:-1]:
        total = total + decode(ref)
    encode(total, refs[-1])


def call(kernel, inputs, outputs, scratch, flops):
    smem = pl.BlockSpec(memory_space=pltpu.SMEM)
    vmem = pl.BlockSpec(memory_space=pltpu.VMEM)
    moved = sum(4 * x.size for x in inputs) + sum(4 * x.size for x in outputs)
    return pl.pallas_call(
        kernel,
        in_specs=[smem if x.dtype == jnp.int32 else vmem for x in inputs],
        out_specs=[vmem] * len(outputs),
        out_shape=outputs,
        scratch_shapes=scratch,
        compiler_params=pltpu.CompilerParams(vmem_limit_bytes=LIMIT),
        cost_estimate=pl.CostEstimate(flops=flops, bytes_accessed=moved, transcendentals=0),
    )(*inputs)


def swap_halves(block, axis):
    half = lax.axis_size(axis) // 2
    return lax.ppermute(block, axis, [(i, (i + half) % (2 * half)) for i in range(2 * half)])


def send_along(term, axis, turn):
    count = lax.axis_size(axis)
    return lax.ppermute(term, axis, [(i, (i + turn) % count) for i in range(count)])


def body(observations, pod_basis, decay, step_mask, process_var, obs_var, prior_mean, prior_var):
    tm_count = lax.axis_size("tm")
    space_count = lax.axis_size("space")
    steps, modes = decay.shape
    chunks = steps // CHUNK
    rank = lax.axis_index("tm").astype(jnp.int32)
    me = rank.reshape(1)
    side = lax.axis_index("space").astype(jnp.int32)
    shape = functools.partial(jax.ShapeDtypeStruct, dtype=F32)
    area = pltpu.VMEM
    group = tm_count // 2
    groups = [[half * group + i for i in range(group)] for half in range(2)]
    half = rank // group

    seen = jnp.broadcast_to(step_mask.astype(F32)[:, None], (steps, modes))
    q, r = process_var[None, :], obs_var[None, :]
    flat = (chunks, modes)
    deep = (CHUNK, chunks, modes)
    strips = area((modes // LANES, steps, LANES), F32)
    slabs = observations.reshape(2, group, steps, observations.shape[3])
    basis = pod_basis.reshape(tm_count, -1, pod_basis.shape[3])
    first = half * group
    owners = [lax.rem(side + turn, space_count) for turn in range(space_count)]
    far = lax.dynamic_index_in_dim(slabs, 1 - half, 0, keepdims=False)
    far, q = lax.optimization_barrier((far, q))
    far = lax.all_to_all(far, "tm", 0, 0, axis_index_groups=groups, tiled=True)
    chunk_totals, block_totals = call(
        totals_kernel, (me, decay, seen, q, r), [shape((3,) + flat), shape((3, modes))], [strips] * 2, 40 * steps * modes
    )
    block_totals, own_half = lax.optimization_barrier((block_totals, half))
    near = lax.dynamic_index_in_dim(slabs, own_half, 0, keepdims=False)
    blocks = gather_near(block_totals, "tm")
    far, near, blocks = lax.optimization_barrier((far, near, blocks))
    near = lax.all_to_all(near, "tm", 0, 0, axis_index_groups=groups, tiled=True)

    own, theirs = project(far, basis, first, owners, modes)
    arriving = [send_along(term, "space", turn + 1) for turn, term in enumerate(theirs)]
    own, blocks = lax.optimization_barrier((own, blocks))
    rest = gather_far(blocks, "tm")
    coded = jax.ShapeDtypeStruct((steps + PAD, modes), jnp.int16)
    (crossing,) = call(fold_kernel, (own, *arriving), [coded], [], 8 * steps * modes)
    rest, near, _ = lax.optimization_barrier((rest, near, crossing))
    crossing = swap_halves(crossing, "tm")
    blocks = jnp.concatenate([blocks] + rest, 0)

    own, theirs = project(near, basis, first, owners, modes)
    parts = [send_along(term, "space", turn + 1) for turn, term in enumerate(theirs)] + [crossing]
    own, chunk_totals = lax.optimization_barrier((own, chunk_totals))
    parts.insert(0, own)
    *maps, whole, carry, edge, log_variance = call(
        functools.partial(gains_kernel, tm_count),
        (me, decay, seen, q, r, prior_var[None, :], chunk_totals, blocks),
        [shape(deep)] * 6 + [shape((3,) + deep), shape((2,) + flat), shape((2, tm_count, modes)), shape((steps, modes))],
        [area((2,) + flat, F32), area(deep, F32), area(deep, F32), strips, strips],
        80 * steps * modes,
    )

    coefficients, mean, smooth, ends = call(
        functools.partial(means_kernel, len(parts)),
        (*parts, *maps, carry),
        [shape((steps, modes)), shape(deep), shape(deep), shape((2, modes))],
        [area((2,) + flat, F32), strips],
        12 * steps * modes,
    )
    ends = jnp.broadcast_to(ends[None], (tm_count,) + ends.shape)
    ends = lax.all_to_all(ends, "tm", 0, 0, tiled=True)
    filtered, smoothed = call(
        functools.partial(finish_kernel, tm_count),
        (me, prior_mean[None, :], whole, edge, ends, mean, smooth),
        [shape((steps, modes))] * 2,
        [strips, strips],
        8 * steps * modes,
    )
    return coefficients, filtered, smoothed, log_variance


def solution(mesh):
    return jax.shard_map(
        body,
        mesh=mesh,
        in_specs=(
            P(None, "tm", "space", None),
            P(None, "space", None, None),
            P("tm", "space"),
            P("tm"),
            P("space"),
            P("space"),
            P("space"),
            P("space"),
        ),
        out_specs=(P("tm", "space"), P("tm", "space"), P("tm", "space"), P("tm", "space")),
        check_vma=False,
    )
```

```python
import functools

import jax
import jax.numpy as jnp
from jax import lax
from jax.experimental import pallas as pl
from jax.experimental.pallas import tpu as pltpu
from jax.sharding import PartitionSpec as P

CHUNK = 16
LANES = 128
PAD = 16
STEPS16 = 32512.0
TINY = 1e-30
F32 = jnp.float32
LIMIT = 16 * 1024 * 1024


def rotate(block, axis, turn, count, group, outer):
    route = []
    for i in range(count):
        low, high = i % group, i // group
        if outer:
            target = ((high + turn) % (count // group)) * group + low
        else:
            target = high * group + (low + turn) % group
        route.append((i, target))
    return lax.ppermute(block, axis, route)


def inner_size(count):
    group = 1
    while group * group < count:
        group *= 2
    return group if count % group == 0 else count


def gather_near(rows, axis):
    count = lax.axis_size(axis)
    group = inner_size(count)
    return jnp.stack([rows] + [rotate(rows, axis, s, count, group, False) for s in range(1, group)])


def gather_far(near, axis):
    count = lax.axis_size(axis)
    group = inner_size(count)
    return [rotate(near, axis, s, count, group, True) for s in range(1, count // group)]


def place(me, j, count):
    group = inner_size(count)
    rounds = count // group
    high = lax.rem(me // group - j // group + rounds, rounds)
    low = lax.rem(lax.rem(me, group) - j % group + group, group)
    return high * group + low


def lanes(ref, strip_ref):
    for m in range(strip_ref.shape[0]):
        strip_ref[m] = ref[:, m * LANES : (m + 1) * LANES]


def unlanes(strip_ref, ref):
    for m in range(strip_ref.shape[0]):
        ref[:, m * LANES : (m + 1) * LANES] = strip_ref[m]


def chunk_rows(strip_ref, i, chunks):
    rows = pl.ds(i, chunks, stride=CHUNK)
    return jnp.concatenate([strip_ref[m, rows, :] for m in range(strip_ref.shape[0])], 1)


def put_rows(strip_ref, i, chunks, value):
    rows = pl.ds(i, chunks, stride=CHUNK)
    for m in range(strip_ref.shape[0]):
        strip_ref[m, rows, :] = value[:, m * LANES : (m + 1) * LANES]


def opened(me_ref, shape):
    rows = lax.broadcasted_iota(jnp.int32, shape, 0)
    return jnp.logical_and(rows == 0, me_ref[0] == 0)


def step_terms(i, chunks, first, q, r, decay_ref, seen_ref):
    d = chunk_rows(decay_ref, i, chunks)
    seen = chunk_rows(seen_ref, i, chunks) > 0.5
    base = q
    if i == 0:
        d = jnp.where(first, 1.0, d)
        base = jnp.where(first, 0.0, q)
    return d, seen, base


def element(d, seen, base, r):
    inverse = 1.0 / (base + r)
    retain = jnp.where(seen, r * inverse, 1.0)
    return retain * d, retain * base, jnp.where(seen, d * d * inverse, 0.0), inverse


def join(early, late):
    lead, spread, weight = early
    lead_late, spread_late, weight_late = late
    factor = 1.0 / (1.0 + spread * weight_late)
    return (
        lead_late * factor * lead,
        lead_late * lead_late * factor * spread + spread_late,
        lead * lead * factor * weight_late + weight,
    )


def totals_kernel(me_ref, decay_in, seen_in, q_ref, r_ref, chunk_ref, block_ref, decay_ref, seen_ref):
    steps, modes = decay_in.shape
    lanes(decay_in, decay_ref)
    lanes(seen_in, seen_ref)
    chunks = steps // CHUNK
    shape = (chunks, modes)
    q = jnp.broadcast_to(q_ref[...], shape)
    r = jnp.broadcast_to(r_ref[...], shape)
    first = opened(me_ref, shape)
    total = None
    for i in range(CHUNK):
        step = element(*step_terms(i, chunks, first, q, r, decay_ref, seen_ref), r)[:3]
        total = step if i == 0 else join(total, step)
    for k in range(3):
        chunk_ref[k] = total[k]
    total = tuple(chunk_ref[k, 0:1, :] for k in range(3))
    for c in range(1, chunks):
        total = join(total, tuple(chunk_ref[k, c : c + 1, :] for k in range(3)))
    for k in range(3):
        block_ref[k : k + 1, :] = total[k]


def gains_kernel(
    count, me_ref, decay_in, seen_in, q_ref, r_ref, prior_ref, chunk_ref, blocks_ref,
    a_ref, b_ref, alpha_ref, beta_ref, keep_ref, lift_ref, whole_ref, carry_ref, edge_ref, log_ref,
    enter_ref, var_ref, info_ref, decay_ref, seen_ref,
):
    steps, modes = decay_in.shape
    lanes(decay_in, decay_ref)
    lanes(seen_in, seen_ref)
    chunks = steps // CHUNK
    shape = (chunks, modes)
    me = me_ref[0]
    q = jnp.broadcast_to(q_ref[...], shape)
    r = jnp.broadcast_to(r_ref[...], shape)
    first = opened(me_ref, shape)

    v = prior_ref[...]
    mine = v
    for j in range(count):
        mine = jnp.where(j == me, v, mine)
        at = place(me, j, count)
        lead, spread, weight = (blocks_ref[at, k : k + 1, :] for k in range(3))
        along = lead / (1.0 + weight * v)
        edge_ref[0, j : j + 1, :] = along
        v = spread + lead * along * v
    v = mine
    for c in range(chunks):
        enter_ref[0, c : c + 1, :] = v
        lead, spread, weight = (chunk_ref[k, c : c + 1, :] for k in range(3))
        v = spread + lead * lead * v / (1.0 + weight * v)

    info = jnp.zeros((1, modes), F32)
    mine = info
    for j in reversed(range(count)):
        mine = jnp.where(j == me, info, mine)
        at = place(me, j, count)
        lead, spread, weight = (blocks_ref[at, k : k + 1, :] for k in range(3))
        along = lead / (1.0 + spread * info)
        edge_ref[1, j : j + 1, :] = along
        info = weight + lead * along * info
    info = mine
    for c in reversed(range(chunks)):
        enter_ref[1, c : c + 1, :] = info
        lead, spread, weight = (chunk_ref[k, c : c + 1, :] for k in range(3))
        info = weight + lead * lead * info / (1.0 + spread * info)

    v = enter_ref[0]
    run = None
    for i in range(CHUNK):
        d, seen, base = step_terms(i, chunks, first, q, r, decay_ref, seen_ref)
        ahead = d * d * v + base
        inverse = 1.0 / (ahead + r)
        retain = jnp.where(seen, r * inverse, 1.0)
        v = retain * ahead
        a = retain * d
        run = a if i == 0 else a * run
        a_ref[i] = a
        b_ref[i] = jnp.where(seen, ahead * inverse, 0.0)
        var_ref[i] = v
        whole_ref[0, i] = run
    carry_ref[0] = run

    info = enter_ref[1]
    run = jnp.ones(shape, F32)
    for i in reversed(range(CHUNK)):
        lead, spread, weight, inverse = element(*step_terms(i, chunks, first, q, r, decay_ref, seen_ref), r)
        d, seen, _ = step_terms(i, chunks, first, q, r, decay_ref, seen_ref)
        factor = 1.0 / (1.0 + spread * info)
        alpha = lead * factor
        info_ref[i] = info
        whole_ref[2, i] = run
        alpha_ref[i] = alpha
        beta_ref[i] = jnp.where(seen, d * inverse * factor, 0.0)
        info = weight + lead * alpha * info
        run = alpha * run
    carry_ref[1] = run

    along = jnp.ones((1, modes), F32)
    for c in range(chunks):
        enter_ref[0, c : c + 1, :] = along
        along = along * carry_ref[0, c : c + 1, :]
    along = jnp.ones((1, modes), F32)
    for c in reversed(range(chunks)):
        enter_ref[1, c : c + 1, :] = along
        along = along * carry_ref[1, c : c + 1, :]
    onward = enter_ref[0]
    back = enter_ref[1]
    for i in range(CHUNK):
        v = var_ref[i]
        keep = 1.0 / (1.0 + v * info_ref[i])
        lift = v * keep
        weight = whole_ref[0, i] * onward
        keep_ref[i] = keep
        lift_ref[i] = lift
        whole_ref[0, i] = weight
        whole_ref[1, i] = keep * weight
        whole_ref[2, i] = lift * (whole_ref[2, i] * back)
        put_rows(decay_ref, i, chunks, jnp.log(lift))
    unlanes(decay_ref, log_ref)


def means_kernel(parts, *refs):
    part_refs = refs[:parts]
    a_ref, b_ref, alpha_ref, beta_ref, keep_ref, lift_ref, carry_ref = refs[parts : parts + 7]
    coef_ref, mean_ref, smooth_ref, block_ref, enter_ref, strip_ref = refs[parts + 7 :]
    steps, modes = coef_ref.shape
    chunks = steps // CHUNK
    c = part_refs[0][...]
    for ref in part_refs[1:]:
        c = c + decode(ref)
    coef_ref[...] = c
    lanes(coef_ref, strip_ref)
    f = e = jnp.zeros((chunks, modes), F32)
    for i in range(CHUNK):
        f = a_ref[i] * f + b_ref[i] * chunk_rows(strip_ref, i, chunks)
        k = CHUNK - 1 - i
        e = alpha_ref[k] * e + beta_ref[k] * chunk_rows(strip_ref, k, chunks)
    mean_ref[0] = f
    mean_ref[1] = e
    f = e = jnp.zeros((1, modes), F32)
    for c in range(chunks):
        k = chunks - 1 - c
        enter_ref[0, c : c + 1, :] = f
        enter_ref[1, k : k + 1, :] = e
        f = mean_ref[0, c : c + 1, :] + carry_ref[0, c : c + 1, :] * f
        e = mean_ref[1, k : k + 1, :] + carry_ref[1, k : k + 1, :] * e
    block_ref[0:1, :] = f
    block_ref[1:2, :] = e
    f = enter_ref[0]
    e = enter_ref[1]
    for i in range(CHUNK):
        f = a_ref[i] * f + b_ref[i] * chunk_rows(strip_ref, i, chunks)
        mean_ref[i] = f
    for i in reversed(range(CHUNK)):
        smooth_ref[i] = keep_ref[i] * mean_ref[i] + lift_ref[i] * e
        e = alpha_ref[i] * e + beta_ref[i] * chunk_rows(strip_ref, i, chunks)


def finish_kernel(count, me_ref, prior_ref, whole_ref, edge_ref, blocks_ref, mean_ref, smooth_ref, out_mean_ref, out_smooth_ref, mean_strip_ref, smooth_strip_ref):
    steps, modes = out_mean_ref.shape
    chunks = steps // CHUNK
    me = me_ref[0]
    f = prior_ref[...]
    e = jnp.zeros((1, modes), F32)
    for j in range(count - 1):
        f = jnp.where(j < me, blocks_ref[j, 0:1, :] + edge_ref[0, j : j + 1, :] * f, f)
        k = count - 1 - j
        e = jnp.where(k > me, blocks_ref[k, 1:2, :] + edge_ref[1, k : k + 1, :] * e, e)
    f = jnp.broadcast_to(f, (chunks, modes))
    e = jnp.broadcast_to(e, (chunks, modes))
    for i in range(CHUNK):
        put_rows(mean_strip_ref, i, chunks, mean_ref[i] + whole_ref[0, i] * f)
        put_rows(smooth_strip_ref, i, chunks, smooth_ref[i] + whole_ref[1, i] * f + whole_ref[2, i] * e)
    unlanes(mean_strip_ref, out_mean_ref)
    unlanes(smooth_strip_ref, out_smooth_ref)


def encode(values, ref):
    steps = values.shape[0]
    top = jnp.max(jnp.abs(values), axis=0, keepdims=True)
    power = jnp.floor(jnp.log2(jnp.maximum(top, TINY))) + 1.0
    coded = jnp.floor(values * (jnp.exp2(-power) * STEPS16) + 0.5)
    ref[0:steps, :] = coded.astype(jnp.int32).astype(jnp.int16)
    power = jnp.broadcast_to(power, (PAD, power.shape[1]))
    ref[steps : steps + PAD, :] = power.astype(jnp.int32).astype(jnp.int16)


def decode(ref):
    steps = ref.shape[0] - PAD
    power = ref[steps : steps + PAD, :].astype(jnp.int32).astype(F32)[0:1, :]
    return ref[0:steps, :].astype(jnp.int32).astype(F32) * (jnp.exp2(power) * (1.0 / STEPS16))


def project_kernel(held, at_ref, slab_ref, basis_ref, own_ref, *refs):
    owners = at_ref.shape[0] - 1
    coded_refs = refs[: owners - 1]
    basis_area, sum_area, basis_sems, *refs = refs[owners - 1 :]
    slab_area = slab_ref if held else refs[0]
    count = slab_ref.shape[0]
    modes = own_ref.shape[1]
    copies = []
    for g in range(count):
        pair = [pltpu.make_async_copy(basis_ref.at[at_ref[0] + g], basis_area.at[g], basis_sems.at[g])]
        if not held:
            pair.append(pltpu.make_async_copy(slab_ref.at[g], slab_area.at[g], refs[1].at[g]))
        copies.append(pair)
    for pair in copies:
        for copy in pair:
            copy.start()
    for g in range(count):
        for copy in copies[g]:
            copy.wait()
        for turn in range(owners):
            columns = pl.ds(pl.multiple_of(at_ref[1 + turn] * modes, LANES), modes)
            term = jnp.dot(slab_area[g], basis_area[g, :, columns], preferred_element_type=F32)
            sum_area[turn] = term if g == 0 else sum_area[turn] + term
    own_ref[...] = sum_area[0]
    for turn in range(1, owners):
        encode(sum_area[turn], coded_refs[turn - 1])


def project(slabs, basis, first, owners, modes, held=False):
    count, steps, cells = slabs.shape
    others = len(owners) - 1
    own, *coded = pl.pallas_call(
        functools.partial(project_kernel, held),
        in_specs=[
            pl.BlockSpec(memory_space=pltpu.SMEM),
            pl.BlockSpec(memory_space=pltpu.VMEM if held else pl.ANY),
            pl.BlockSpec(memory_space=pl.ANY),
        ],
        out_specs=[pl.BlockSpec(memory_space=pltpu.VMEM)] * (1 + others),
        out_shape=[jax.ShapeDtypeStruct((steps, modes), F32)]
        + [jax.ShapeDtypeStruct((steps + PAD, modes), jnp.int16)] * others,
        scratch_shapes=[
            pltpu.VMEM((count,) + basis.shape[1:], basis.dtype),
            pltpu.VMEM((1 + others, steps, modes), F32),
            pltpu.SemaphoreType.DMA((count,)),
        ]
        + ([] if held else [pltpu.VMEM(slabs.shape, slabs.dtype), pltpu.SemaphoreType.DMA((count,))]),
        compiler_params=pltpu.CompilerParams(vmem_limit_bytes=(36 if held else 60) * LIMIT // 16),
        cost_estimate=pl.CostEstimate(
            flops=2 * count * steps * cells * modes * (1 + others),
            bytes_accessed=2 * count * cells * (steps + modes * (1 + others)) + 4 * steps * modes,
            transcendentals=0,
        ),
    )(jnp.stack([first] + owners), slabs, basis)
    return own, coded


def fold_kernel(own_ref, *refs):
    total = own_ref[...]
    for ref in refs[:-1]:
        total = total + decode(ref)
    encode(total, refs[-1])


def call(kernel, inputs, outputs, scratch, flops):
    smem = pl.BlockSpec(memory_space=pltpu.SMEM)
    vmem = pl.BlockSpec(memory_space=pltpu.VMEM)
    moved = sum(4 * x.size for x in inputs) + sum(4 * x.size for x in outputs)
    return pl.pallas_call(
        kernel,
        in_specs=[smem if x.dtype == jnp.int32 else vmem for x in inputs],
        out_specs=[vmem] * len(outputs),
        out_shape=outputs,
        scratch_shapes=scratch,
        compiler_params=pltpu.CompilerParams(vmem_limit_bytes=LIMIT),
        cost_estimate=pl.CostEstimate(flops=flops, bytes_accessed=moved, transcendentals=0),
    )(*inputs)


def swap_halves(block, axis):
    half = lax.axis_size(axis) // 2
    return lax.ppermute(block, axis, [(i, (i + half) % (2 * half)) for i in range(2 * half)])


def send_along(term, axis, turn):
    count = lax.axis_size(axis)
    return lax.ppermute(term, axis, [(i, (i + turn) % count) for i in range(count)])


def body(observations, pod_basis, decay, step_mask, process_var, obs_var, prior_mean, prior_var):
    tm_count = lax.axis_size("tm")
    space_count = lax.axis_size("space")
    steps, modes = decay.shape
    chunks = steps // CHUNK
    rank = lax.axis_index("tm").astype(jnp.int32)
    me = rank.reshape(1)
    side = lax.axis_index("space").astype(jnp.int32)
    shape = functools.partial(jax.ShapeDtypeStruct, dtype=F32)
    area = pltpu.VMEM
    group = tm_count // 2
    groups = [[half * group + i for i in range(group)] for half in range(2)]
    half = rank // group

    seen = jnp.broadcast_to(step_mask.astype(F32)[:, None], (steps, modes))
    q, r = process_var[None, :], obs_var[None, :]
    flat = (chunks, modes)
    deep = (CHUNK, chunks, modes)
    strips = area((modes // LANES, steps, LANES), F32)
    slabs = observations.reshape(2, group, steps, observations.shape[3])
    basis = pod_basis.reshape(tm_count, -1, pod_basis.shape[3])
    first = half * group
    owners = [lax.rem(side + turn, space_count) for turn in range(space_count)]
    far = lax.dynamic_index_in_dim(slabs, 1 - half, 0, keepdims=False)
    far, q = lax.optimization_barrier((far, q))
    far = lax.all_to_all(far, "tm", 0, 0, axis_index_groups=groups, tiled=True)
    chunk_totals, block_totals = call(
        totals_kernel, (me, decay, seen, q, r), [shape((3,) + flat), shape((3, modes))], [strips] * 2, 40 * steps * modes
    )
    block_totals, own_half = lax.optimization_barrier((block_totals, half))
    near = lax.dynamic_index_in_dim(slabs, own_half, 0, keepdims=False)
    blocks = gather_near(block_totals, "tm")
    far, blocks = lax.optimization_barrier((far, blocks))
    near = lax.all_to_all(near, "tm", 0, 0, axis_index_groups=groups, tiled=True)

    own, theirs = project(far, basis, first, owners, modes)
    arriving = [send_along(term, "space", turn + 1) for turn, term in enumerate(theirs)]
    own, blocks = lax.optimization_barrier((own, blocks))
    rest = gather_far(blocks, "tm")
    coded = jax.ShapeDtypeStruct((steps + PAD, modes), jnp.int16)
    (crossing,) = call(fold_kernel, (own, *arriving), [coded], [], 8 * steps * modes)
    rest, near, _ = lax.optimization_barrier((rest, near, crossing))
    crossing = swap_halves(crossing, "tm")

    own, theirs = project(near, basis, first, owners, modes, True)
    parts = [send_along(term, "space", turn + 1) for turn, term in enumerate(theirs)] + [crossing]
    own, chunk_totals, rest = lax.optimization_barrier((own, chunk_totals, rest))
    blocks = jnp.concatenate([blocks] + rest, 0)
    parts.insert(0, own)
    *maps, whole, carry, edge, log_variance = call(
        functools.partial(gains_kernel, tm_count),
        (me, decay, seen, q, r, prior_var[None, :], chunk_totals, blocks),
        [shape(deep)] * 6 + [shape((3,) + deep), shape((2,) + flat), shape((2, tm_count, modes)), shape((steps, modes))],
        [area((2,) + flat, F32), area(deep, F32), area(deep, F32), strips, strips],
        80 * steps * modes,
    )

    coefficients, mean, smooth, ends = call(
        functools.partial(means_kernel, len(parts)),
        (*parts, *maps, carry),
        [shape((steps, modes)), shape(deep), shape(deep), shape((2, modes))],
        [area((2,) + flat, F32), strips],
        12 * steps * modes,
    )
    ends = jnp.broadcast_to(ends[None], (tm_count,) + ends.shape)
    ends = lax.all_to_all(ends, "tm", 0, 0, tiled=True)
    filtered, smoothed = call(
        functools.partial(finish_kernel, tm_count),
        (me, prior_mean[None, :], whole, edge, ends, mean, smooth),
        [shape((steps, modes))] * 2,
        [strips, strips],
        8 * steps * modes,
    )
    return coefficients, filtered, smoothed, log_variance


def solution(mesh):
    return jax.shard_map(
        body,
        mesh=mesh,
        in_specs=(
            P(None, "tm", "space", None),
            P(None, "space", None, None),
            P("tm", "space"),
            P("tm"),
            P("space"),
            P("space"),
            P("space"),
            P("space"),
        ),
        out_specs=(P("tm", "space"), P("tm", "space"), P("tm", "space"), P("tm", "space")),
        check_vma=False,
    )
```

```python
import functools

import jax
import jax.numpy as jnp
from jax import lax
from jax.experimental import pallas as pl
from jax.experimental.pallas import tpu as pltpu
from jax.sharding import PartitionSpec as P

CHUNK = 16
LANES = 128
PAD = 16
STEPS16 = 32512.0
TINY = 1e-30
F32 = jnp.float32
LIMIT = 16 * 1024 * 1024


def rotate(block, axis, turn, group):
    route = [(i, i // group * group + (i + turn) % group) for i in range(lax.axis_size(axis))]
    return lax.ppermute(block, axis, route)


def inner_size(count):
    group = 1
    while group * group < count:
        group *= 2
    return group if count % group == 0 else count


def gather_near(rows, axis):
    count = lax.axis_size(axis)
    group = inner_size(count)
    return jnp.stack([rows] + [rotate(rows, axis, s, group) for s in range(1, group)])


def gather_across(blocks, axis):
    away = blocks.shape[0]
    return jnp.concatenate(
        [blocks, lax.ppermute(blocks, axis, [(i, i ^ away) for i in range(lax.axis_size(axis))])], 0
    )


def place(me, j, count):
    group = inner_size(count)
    high = lax.bitwise_xor(me // group, j // group)
    low = lax.rem(lax.rem(me, group) - j % group + group, group)
    return high * group + low


def lanes(ref, strip_ref):
    for m in range(strip_ref.shape[0]):
        strip_ref[m] = ref[:, m * LANES : (m + 1) * LANES]


def unlanes(strip_ref, ref):
    for m in range(strip_ref.shape[0]):
        ref[:, m * LANES : (m + 1) * LANES] = strip_ref[m]


def chunk_rows(strip_ref, i, chunks):
    rows = pl.ds(i, chunks, stride=CHUNK)
    return jnp.concatenate([strip_ref[m, rows, :] for m in range(strip_ref.shape[0])], 1)


def put_rows(strip_ref, i, chunks, value):
    rows = pl.ds(i, chunks, stride=CHUNK)
    for m in range(strip_ref.shape[0]):
        strip_ref[m, rows, :] = value[:, m * LANES : (m + 1) * LANES]


def opened(me_ref, shape):
    rows = lax.broadcasted_iota(jnp.int32, shape, 0)
    return jnp.logical_and(rows == 0, me_ref[0] == 0)


def step_terms(i, chunks, first, q, r, decay_ref, seen_ref):
    d = chunk_rows(decay_ref, i, chunks)
    seen = chunk_rows(seen_ref, i, chunks) > 0.5
    base = q
    if i == 0:
        d = jnp.where(first, 1.0, d)
        base = jnp.where(first, 0.0, q)
    return d, seen, base


def element(d, seen, base, r):
    inverse = 1.0 / (base + r)
    retain = jnp.where(seen, r * inverse, 1.0)
    return retain * d, retain * base, jnp.where(seen, d * d * inverse, 0.0), inverse


def join(early, late):
    lead, spread, weight = early
    lead_late, spread_late, weight_late = late
    factor = 1.0 / (1.0 + spread * weight_late)
    return (
        lead_late * factor * lead,
        lead_late * lead_late * factor * spread + spread_late,
        lead * lead * factor * weight_late + weight,
    )


def totals_kernel(me_ref, decay_in, seen_in, q_ref, r_ref, chunk_ref, block_ref, decay_ref, seen_ref):
    steps, modes = decay_in.shape
    lanes(decay_in, decay_ref)
    lanes(seen_in, seen_ref)
    chunks = steps // CHUNK
    shape = (chunks, modes)
    q = jnp.broadcast_to(q_ref[...], shape)
    r = jnp.broadcast_to(r_ref[...], shape)
    first = opened(me_ref, shape)
    total = None
    for i in range(CHUNK):
        step = element(*step_terms(i, chunks, first, q, r, decay_ref, seen_ref), r)[:3]
        total = step if i == 0 else join(total, step)
    for k in range(3):
        chunk_ref[k] = total[k]
    total = tuple(chunk_ref[k, 0:1, :] for k in range(3))
    for c in range(1, chunks):
        total = join(total, tuple(chunk_ref[k, c : c + 1, :] for k in range(3)))
    for k in range(3):
        block_ref[k : k + 1, :] = total[k]


def gains_kernel(
    count, me_ref, decay_in, seen_in, q_ref, r_ref, prior_ref, chunk_ref, blocks_ref,
    a_ref, b_ref, alpha_ref, beta_ref, keep_ref, lift_ref, whole_ref, carry_ref, edge_ref, log_ref,
    enter_ref, var_ref, info_ref, decay_ref, seen_ref,
):
    steps, modes = decay_in.shape
    lanes(decay_in, decay_ref)
    lanes(seen_in, seen_ref)
    chunks = steps // CHUNK
    shape = (chunks, modes)
    me = me_ref[0]
    q = jnp.broadcast_to(q_ref[...], shape)
    r = jnp.broadcast_to(r_ref[...], shape)
    first = opened(me_ref, shape)

    v = prior_ref[...]
    mine = v
    for j in range(count):
        mine = jnp.where(j == me, v, mine)
        at = place(me, j, count)
        lead, spread, weight = (blocks_ref[at, k : k + 1, :] for k in range(3))
        along = lead / (1.0 + weight * v)
        edge_ref[0, j : j + 1, :] = along
        v = spread + lead * along * v
    v = mine
    for c in range(chunks):
        enter_ref[0, c : c + 1, :] = v
        lead, spread, weight = (chunk_ref[k, c : c + 1, :] for k in range(3))
        v = spread + lead * lead * v / (1.0 + weight * v)

    info = jnp.zeros((1, modes), F32)
    mine = info
    for j in reversed(range(count)):
        mine = jnp.where(j == me, info, mine)
        at = place(me, j, count)
        lead, spread, weight = (blocks_ref[at, k : k + 1, :] for k in range(3))
        along = lead / (1.0 + spread * info)
        edge_ref[1, j : j + 1, :] = along
        info = weight + lead * along * info
    info = mine
    for c in reversed(range(chunks)):
        enter_ref[1, c : c + 1, :] = info
        lead, spread, weight = (chunk_ref[k, c : c + 1, :] for k in range(3))
        info = weight + lead * lead * info / (1.0 + spread * info)

    v = enter_ref[0]
    run = None
    for i in range(CHUNK):
        d, seen, base = step_terms(i, chunks, first, q, r, decay_ref, seen_ref)
        ahead = d * d * v + base
        inverse = 1.0 / (ahead + r)
        retain = jnp.where(seen, r * inverse, 1.0)
        v = retain * ahead
        a = retain * d
        run = a if i == 0 else a * run
        a_ref[i] = a
        b_ref[i] = jnp.where(seen, ahead * inverse, 0.0)
        var_ref[i] = v
        whole_ref[0, i] = run
    carry_ref[0] = run

    info = enter_ref[1]
    run = jnp.ones(shape, F32)
    for i in reversed(range(CHUNK)):
        lead, spread, weight, inverse = element(*step_terms(i, chunks, first, q, r, decay_ref, seen_ref), r)
        d, seen, _ = step_terms(i, chunks, first, q, r, decay_ref, seen_ref)
        factor = 1.0 / (1.0 + spread * info)
        alpha = lead * factor
        info_ref[i] = info
        whole_ref[2, i] = run
        alpha_ref[i] = alpha
        beta_ref[i] = jnp.where(seen, d * inverse * factor, 0.0)
        info = weight + lead * alpha * info
        run = alpha * run
    carry_ref[1] = run

    along = jnp.ones((1, modes), F32)
    for c in range(chunks):
        enter_ref[0, c : c + 1, :] = along
        along = along * carry_ref[0, c : c + 1, :]
    along = jnp.ones((1, modes), F32)
    for c in reversed(range(chunks)):
        enter_ref[1, c : c + 1, :] = along
        along = along * carry_ref[1, c : c + 1, :]
    onward = enter_ref[0]
    back = enter_ref[1]
    for i in range(CHUNK):
        v = var_ref[i]
        keep = 1.0 / (1.0 + v * info_ref[i])
        lift = v * keep
        weight = whole_ref[0, i] * onward
        keep_ref[i] = keep
        lift_ref[i] = lift
        whole_ref[0, i] = weight
        whole_ref[1, i] = keep * weight
        whole_ref[2, i] = lift * (whole_ref[2, i] * back)
        put_rows(decay_ref, i, chunks, jnp.log(lift))
    unlanes(decay_ref, log_ref)


def means_kernel(parts, *refs):
    part_refs = refs[:parts]
    a_ref, b_ref, alpha_ref, beta_ref, keep_ref, lift_ref, carry_ref = refs[parts : parts + 7]
    coef_ref, mean_ref, smooth_ref, block_ref, enter_ref, strip_ref = refs[parts + 7 :]
    steps, modes = coef_ref.shape
    chunks = steps // CHUNK
    c = part_refs[0][...]
    for ref in part_refs[1:]:
        c = c + decode(ref)
    coef_ref[...] = c
    lanes(coef_ref, strip_ref)
    f = e = jnp.zeros((chunks, modes), F32)
    for i in range(CHUNK):
        f = a_ref[i] * f + b_ref[i] * chunk_rows(strip_ref, i, chunks)
        k = CHUNK - 1 - i
        e = alpha_ref[k] * e + beta_ref[k] * chunk_rows(strip_ref, k, chunks)
    mean_ref[0] = f
    mean_ref[1] = e
    f = e = jnp.zeros((1, modes), F32)
    for c in range(chunks):
        k = chunks - 1 - c
        enter_ref[0, c : c + 1, :] = f
        enter_ref[1, k : k + 1, :] = e
        f = mean_ref[0, c : c + 1, :] + carry_ref[0, c : c + 1, :] * f
        e = mean_ref[1, k : k + 1, :] + carry_ref[1, k : k + 1, :] * e
    block_ref[0:1, :] = f
    block_ref[1:2, :] = e
    f = enter_ref[0]
    e = enter_ref[1]
    for i in range(CHUNK):
        f = a_ref[i] * f + b_ref[i] * chunk_rows(strip_ref, i, chunks)
        mean_ref[i] = f
    for i in reversed(range(CHUNK)):
        smooth_ref[i] = keep_ref[i] * mean_ref[i] + lift_ref[i] * e
        e = alpha_ref[i] * e + beta_ref[i] * chunk_rows(strip_ref, i, chunks)


def finish_kernel(count, me_ref, prior_ref, whole_ref, edge_ref, blocks_ref, mean_ref, smooth_ref, out_mean_ref, out_smooth_ref, mean_strip_ref, smooth_strip_ref):
    steps, modes = out_mean_ref.shape
    chunks = steps // CHUNK
    me = me_ref[0]
    f = prior_ref[...]
    e = jnp.zeros((1, modes), F32)
    for j in range(count - 1):
        f = jnp.where(j < me, blocks_ref[j, 0:1, :] + edge_ref[0, j : j + 1, :] * f, f)
        k = count - 1 - j
        e = jnp.where(k > me, blocks_ref[k, 1:2, :] + edge_ref[1, k : k + 1, :] * e, e)
    f = jnp.broadcast_to(f, (chunks, modes))
    e = jnp.broadcast_to(e, (chunks, modes))
    for i in range(CHUNK):
        put_rows(mean_strip_ref, i, chunks, mean_ref[i] + whole_ref[0, i] * f)
        put_rows(smooth_strip_ref, i, chunks, smooth_ref[i] + whole_ref[1, i] * f + whole_ref[2, i] * e)
    unlanes(mean_strip_ref, out_mean_ref)
    unlanes(smooth_strip_ref, out_smooth_ref)


def encode(values, ref):
    steps = values.shape[0]
    top = jnp.max(jnp.abs(values), axis=0, keepdims=True)
    power = jnp.floor(jnp.log2(jnp.maximum(top, TINY))) + 1.0
    coded = jnp.floor(values * (jnp.exp2(-power) * STEPS16) + 0.5)
    ref[0:steps, :] = coded.astype(jnp.int32).astype(jnp.int16)
    power = jnp.broadcast_to(power, (PAD, power.shape[1]))
    ref[steps : steps + PAD, :] = power.astype(jnp.int32).astype(jnp.int16)


def decode(ref):
    steps = ref.shape[0] - PAD
    power = ref[steps : steps + PAD, :].astype(jnp.int32).astype(F32)[0:1, :]
    return ref[0:steps, :].astype(jnp.int32).astype(F32) * (jnp.exp2(power) * (1.0 / STEPS16))


def project_kernel(held, at_ref, slab_ref, basis_ref, own_ref, *refs):
    owners = at_ref.shape[0] - 1
    coded_refs = refs[: owners - 1]
    basis_area, sum_area, basis_sems, *refs = refs[owners - 1 :]
    slab_area = slab_ref if held else refs[0]
    count = slab_ref.shape[0]
    modes = own_ref.shape[1]
    copies = []
    for g in range(count):
        pair = [pltpu.make_async_copy(basis_ref.at[at_ref[0] + g], basis_area.at[g], basis_sems.at[g])]
        if not held:
            pair.append(pltpu.make_async_copy(slab_ref.at[g], slab_area.at[g], refs[1].at[g]))
        copies.append(pair)
    for pair in copies:
        for copy in pair:
            copy.start()
    for g in range(count):
        for copy in copies[g]:
            copy.wait()
        for turn in range(owners):
            columns = pl.ds(pl.multiple_of(at_ref[1 + turn] * modes, LANES), modes)
            term = jnp.dot(slab_area[g], basis_area[g, :, columns], preferred_element_type=F32)
            sum_area[turn] = term if g == 0 else sum_area[turn] + term
    own_ref[...] = sum_area[0]
    for turn in range(1, owners):
        encode(sum_area[turn], coded_refs[turn - 1])


def project(slabs, basis, first, owners, modes, held=False):
    count, steps, cells = slabs.shape
    others = len(owners) - 1
    own, *coded = pl.pallas_call(
        functools.partial(project_kernel, held),
        in_specs=[
            pl.BlockSpec(memory_space=pltpu.SMEM),
            pl.BlockSpec(memory_space=pltpu.VMEM if held else pl.ANY),
            pl.BlockSpec(memory_space=pl.ANY),
        ],
        out_specs=[pl.BlockSpec(memory_space=pltpu.VMEM)] * (1 + others),
        out_shape=[jax.ShapeDtypeStruct((steps, modes), F32)]
        + [jax.ShapeDtypeStruct((steps + PAD, modes), jnp.int16)] * others,
        scratch_shapes=[
            pltpu.VMEM((count,) + basis.shape[1:], basis.dtype),
            pltpu.VMEM((1 + others, steps, modes), F32),
            pltpu.SemaphoreType.DMA((count,)),
        ]
        + ([] if held else [pltpu.VMEM(slabs.shape, slabs.dtype), pltpu.SemaphoreType.DMA((count,))]),
        compiler_params=pltpu.CompilerParams(vmem_limit_bytes=(36 if held else 60) * LIMIT // 16),
        cost_estimate=pl.CostEstimate(
            flops=2 * count * steps * cells * modes * (1 + others),
            bytes_accessed=2 * count * cells * (steps + modes * (1 + others)) + 4 * steps * modes,
            transcendentals=0,
        ),
    )(jnp.stack([first] + owners), slabs, basis)
    return own, coded


def fold_kernel(own_ref, *refs):
    total = own_ref[...]
    for ref in refs[:-1]:
        total = total + decode(ref)
    encode(total, refs[-1])


def call(kernel, inputs, outputs, scratch, flops):
    smem = pl.BlockSpec(memory_space=pltpu.SMEM)
    vmem = pl.BlockSpec(memory_space=pltpu.VMEM)
    moved = sum(4 * x.size for x in inputs) + sum(4 * x.size for x in outputs)
    return pl.pallas_call(
        kernel,
        in_specs=[smem if x.dtype == jnp.int32 else vmem for x in inputs],
        out_specs=[vmem] * len(outputs),
        out_shape=outputs,
        scratch_shapes=scratch,
        compiler_params=pltpu.CompilerParams(vmem_limit_bytes=LIMIT),
        cost_estimate=pl.CostEstimate(flops=flops, bytes_accessed=moved, transcendentals=0),
    )(*inputs)


def swap_halves(block, axis):
    half = lax.axis_size(axis) // 2
    return lax.ppermute(block, axis, [(i, (i + half) % (2 * half)) for i in range(2 * half)])


def send_along(term, axis, turn):
    count = lax.axis_size(axis)
    return lax.ppermute(term, axis, [(i, (i + turn) % count) for i in range(count)])


def body(observations, pod_basis, decay, step_mask, process_var, obs_var, prior_mean, prior_var):
    tm_count = lax.axis_size("tm")
    space_count = lax.axis_size("space")
    steps, modes = decay.shape
    chunks = steps // CHUNK
    rank = lax.axis_index("tm").astype(jnp.int32)
    me = rank.reshape(1)
    side = lax.axis_index("space").astype(jnp.int32)
    shape = functools.partial(jax.ShapeDtypeStruct, dtype=F32)
    area = pltpu.VMEM
    group = tm_count // 2
    groups = [[half * group + i for i in range(group)] for half in range(2)]
    half = rank // group

    seen = jnp.broadcast_to(step_mask.astype(F32)[:, None], (steps, modes))
    q, r = process_var[None, :], obs_var[None, :]
    flat = (chunks, modes)
    deep = (CHUNK, chunks, modes)
    strips = area((modes // LANES, steps, LANES), F32)
    slabs = observations.reshape(2, group, steps, observations.shape[3])
    basis = pod_basis.reshape(tm_count, -1, pod_basis.shape[3])
    first = half * group
    owners = [lax.rem(side + turn, space_count) for turn in range(space_count)]
    far = lax.dynamic_index_in_dim(slabs, 1 - half, 0, keepdims=False)
    far, q = lax.optimization_barrier((far, q))
    far = lax.all_to_all(far, "tm", 0, 0, axis_index_groups=groups, tiled=True)
    chunk_totals, block_totals = call(
        totals_kernel, (me, decay, seen, q, r), [shape((3,) + flat), shape((3, modes))], [strips] * 2, 40 * steps * modes
    )
    block_totals, own_half = lax.optimization_barrier((block_totals, half))
    near = lax.dynamic_index_in_dim(slabs, own_half, 0, keepdims=False)
    blocks = gather_near(block_totals, "tm")
    far, near, blocks = lax.optimization_barrier((far, near, blocks))
    near = lax.all_to_all(near, "tm", 0, 0, axis_index_groups=groups, tiled=True)

    own, theirs = project(far, basis, first, owners, modes)
    arriving = [send_along(term, "space", turn + 1) for turn, term in enumerate(theirs)]
    coded = jax.ShapeDtypeStruct((steps + PAD, modes), jnp.int16)
    (crossing,) = call(fold_kernel, (own, *arriving), [coded], [], 8 * steps * modes)
    blocks, near, _ = lax.optimization_barrier((blocks, near, crossing))
    while blocks.shape[0] * 2 < tm_count:
        blocks = gather_across(blocks, "tm")
    blocks, near = lax.optimization_barrier((blocks, near))
    crossing = swap_halves(crossing, "tm")
    blocks = gather_across(blocks, "tm")

    own, theirs = project(near, basis, first, owners, modes, True)
    parts = [send_along(term, "space", turn + 1) for turn, term in enumerate(theirs)] + [crossing]
    own, chunk_totals = lax.optimization_barrier((own, chunk_totals))
    parts.insert(0, own)
    *maps, whole, carry, edge, log_variance = call(
        functools.partial(gains_kernel, tm_count),
        (me, decay, seen, q, r, prior_var[None, :], chunk_totals, blocks),
        [shape(deep)] * 6 + [shape((3,) + deep), shape((2,) + flat), shape((2, tm_count, modes)), shape((steps, modes))],
        [area((2,) + flat, F32), area(deep, F32), area(deep, F32), strips, strips],
        80 * steps * modes,
    )

    coefficients, mean, smooth, ends = call(
        functools.partial(means_kernel, len(parts)),
        (*parts, *maps, carry),
        [shape((steps, modes)), shape(deep), shape(deep), shape((2, modes))],
        [area((2,) + flat, F32), strips],
        12 * steps * modes,
    )
    ends = jnp.broadcast_to(ends[None], (tm_count,) + ends.shape)
    ends = lax.all_to_all(ends, "tm", 0, 0, tiled=True)
    filtered, smoothed = call(
        functools.partial(finish_kernel, tm_count),
        (me, prior_mean[None, :], whole, edge, ends, mean, smooth),
        [shape((steps, modes))] * 2,
        [strips, strips],
        8 * steps * modes,
    )
    return coefficients, filtered, smoothed, log_variance


def solution(mesh):
    return jax.shard_map(
        body,
        mesh=mesh,
        in_specs=(
            P(None, "tm", "space", None),
            P(None, "space", None, None),
            P("tm", "space"),
            P("tm"),
            P("space"),
            P("space"),
            P("space"),
            P("space"),
        ),
        out_specs=(P("tm", "space"), P("tm", "space"), P("tm", "space"), P("tm", "space")),
        check_vma=False,
    )
```

```python
import functools

import jax
import jax.numpy as jnp
from jax import lax
from jax.experimental import pallas as pl
from jax.experimental.pallas import tpu as pltpu
from jax.sharding import PartitionSpec as P

CHUNK = 16
LANES = 128
PAD = 16
STEPS16 = 32512.0
TINY = 1e-30
F32 = jnp.float32
LIMIT = 16 * 1024 * 1024


def rotate(block, axis, turn, group):
    route = [(i, i // group * group + (i + turn) % group) for i in range(lax.axis_size(axis))]
    return lax.ppermute(block, axis, route)


def inner_size(count):
    group = 1
    while group * group < count:
        group *= 2
    return group if count % group == 0 else count


def gather_near(rows, axis):
    count = lax.axis_size(axis)
    group = inner_size(count)
    return jnp.stack([rows] + [rotate(rows, axis, s, group) for s in range(1, group)])


def gather_far(near, axis):
    count = lax.axis_size(axis)
    group = near.shape[0]
    rest = [
        lax.ppermute(near, axis, [(i, i ^ (turn * group)) for i in range(count)]) for turn in range(1, count // group)
    ]
    return jnp.concatenate([near] + rest, 0)


def place(me, j, count):
    group = inner_size(count)
    high = lax.bitwise_xor(me // group, j // group)
    low = lax.rem(lax.rem(me, group) - j % group + group, group)
    return high * group + low


def lanes(ref, strip_ref):
    for m in range(strip_ref.shape[0]):
        strip_ref[m] = ref[:, m * LANES : (m + 1) * LANES]


def unlanes(strip_ref, ref):
    for m in range(strip_ref.shape[0]):
        ref[:, m * LANES : (m + 1) * LANES] = strip_ref[m]


def chunk_rows(strip_ref, i, chunks):
    rows = pl.ds(i, chunks, stride=CHUNK)
    return jnp.concatenate([strip_ref[m, rows, :] for m in range(strip_ref.shape[0])], 1)


def put_rows(strip_ref, i, chunks, value):
    rows = pl.ds(i, chunks, stride=CHUNK)
    for m in range(strip_ref.shape[0]):
        strip_ref[m, rows, :] = value[:, m * LANES : (m + 1) * LANES]


def opened(me_ref, shape):
    rows = lax.broadcasted_iota(jnp.int32, shape, 0)
    return jnp.logical_and(rows == 0, me_ref[0] == 0)


def step_terms(i, chunks, first, q, r, decay_ref, seen_ref):
    d = chunk_rows(decay_ref, i, chunks)
    seen = chunk_rows(seen_ref, i, chunks) > 0.5
    base = q
    if i == 0:
        d = jnp.where(first, 1.0, d)
        base = jnp.where(first, 0.0, q)
    return d, seen, base


def element(d, seen, base, r):
    inverse = 1.0 / (base + r)
    retain = jnp.where(seen, r * inverse, 1.0)
    return retain * d, retain * base, jnp.where(seen, d * d * inverse, 0.0), inverse


def join(early, late):
    lead, spread, weight = early
    lead_late, spread_late, weight_late = late
    factor = 1.0 / (1.0 + spread * weight_late)
    return (
        lead_late * factor * lead,
        lead_late * lead_late * factor * spread + spread_late,
        lead * lead * factor * weight_late + weight,
    )


def totals_kernel(me_ref, decay_in, seen_in, q_ref, r_ref, chunk_ref, block_ref, decay_ref, seen_ref):
    steps, modes = decay_in.shape
    lanes(decay_in, decay_ref)
    lanes(seen_in, seen_ref)
    chunks = steps // CHUNK
    shape = (chunks, modes)
    q = jnp.broadcast_to(q_ref[...], shape)
    r = jnp.broadcast_to(r_ref[...], shape)
    first = opened(me_ref, shape)
    total = None
    for i in range(CHUNK):
        step = element(*step_terms(i, chunks, first, q, r, decay_ref, seen_ref), r)[:3]
        total = step if i == 0 else join(total, step)
    for k in range(3):
        chunk_ref[k] = total[k]
    total = tuple(chunk_ref[k, 0:1, :] for k in range(3))
    for c in range(1, chunks):
        total = join(total, tuple(chunk_ref[k, c : c + 1, :] for k in range(3)))
    for k in range(3):
        block_ref[k : k + 1, :] = total[k]


def gains_kernel(
    count, me_ref, decay_in, seen_in, q_ref, r_ref, prior_ref, chunk_ref, blocks_ref,
    a_ref, b_ref, alpha_ref, beta_ref, keep_ref, lift_ref, whole_ref, carry_ref, edge_ref, log_ref,
    enter_ref, var_ref, info_ref, decay_ref, seen_ref,
):
    steps, modes = decay_in.shape
    lanes(decay_in, decay_ref)
    lanes(seen_in, seen_ref)
    chunks = steps // CHUNK
    shape = (chunks, modes)
    me = me_ref[0]
    q = jnp.broadcast_to(q_ref[...], shape)
    r = jnp.broadcast_to(r_ref[...], shape)
    first = opened(me_ref, shape)

    v = prior_ref[...]
    mine = v
    for j in range(count):
        mine = jnp.where(j == me, v, mine)
        at = place(me, j, count)
        lead, spread, weight = (blocks_ref[at, k : k + 1, :] for k in range(3))
        along = lead / (1.0 + weight * v)
        edge_ref[0, j : j + 1, :] = along
        v = spread + lead * along * v
    v = mine
    for c in range(chunks):
        enter_ref[0, c : c + 1, :] = v
        lead, spread, weight = (chunk_ref[k, c : c + 1, :] for k in range(3))
        v = spread + lead * lead * v / (1.0 + weight * v)

    info = jnp.zeros((1, modes), F32)
    mine = info
    for j in reversed(range(count)):
        mine = jnp.where(j == me, info, mine)
        at = place(me, j, count)
        lead, spread, weight = (blocks_ref[at, k : k + 1, :] for k in range(3))
        along = lead / (1.0 + spread * info)
        edge_ref[1, j : j + 1, :] = along
        info = weight + lead * along * info
    info = mine
    for c in reversed(range(chunks)):
        enter_ref[1, c : c + 1, :] = info
        lead, spread, weight = (chunk_ref[k, c : c + 1, :] for k in range(3))
        info = weight + lead * lead * info / (1.0 + spread * info)

    v = enter_ref[0]
    run = None
    for i in range(CHUNK):
        d, seen, base = step_terms(i, chunks, first, q, r, decay_ref, seen_ref)
        ahead = d * d * v + base
        inverse = 1.0 / (ahead + r)
        retain = jnp.where(seen, r * inverse, 1.0)
        v = retain * ahead
        a = retain * d
        run = a if i == 0 else a * run
        a_ref[i] = a
        b_ref[i] = jnp.where(seen, ahead * inverse, 0.0)
        var_ref[i] = v
        whole_ref[0, i] = run
    carry_ref[0] = run

    info = enter_ref[1]
    run = jnp.ones(shape, F32)
    for i in reversed(range(CHUNK)):
        lead, spread, weight, inverse = element(*step_terms(i, chunks, first, q, r, decay_ref, seen_ref), r)
        d, seen, _ = step_terms(i, chunks, first, q, r, decay_ref, seen_ref)
        factor = 1.0 / (1.0 + spread * info)
        alpha = lead * factor
        info_ref[i] = info
        whole_ref[2, i] = run
        alpha_ref[i] = alpha
        beta_ref[i] = jnp.where(seen, d * inverse * factor, 0.0)
        info = weight + lead * alpha * info
        run = alpha * run
    carry_ref[1] = run

    along = jnp.ones((1, modes), F32)
    for c in range(chunks):
        enter_ref[0, c : c + 1, :] = along
        along = along * carry_ref[0, c : c + 1, :]
    along = jnp.ones((1, modes), F32)
    for c in reversed(range(chunks)):
        enter_ref[1, c : c + 1, :] = along
        along = along * carry_ref[1, c : c + 1, :]
    onward = enter_ref[0]
    back = enter_ref[1]
    for i in range(CHUNK):
        v = var_ref[i]
        keep = 1.0 / (1.0 + v * info_ref[i])
        lift = v * keep
        weight = whole_ref[0, i] * onward
        keep_ref[i] = keep
        lift_ref[i] = lift
        whole_ref[0, i] = weight
        whole_ref[1, i] = keep * weight
        whole_ref[2, i] = lift * (whole_ref[2, i] * back)
        put_rows(decay_ref, i, chunks, jnp.log(lift))
    unlanes(decay_ref, log_ref)


def means_kernel(parts, *refs):
    part_refs = refs[:parts]
    a_ref, b_ref, alpha_ref, beta_ref, keep_ref, lift_ref, carry_ref = refs[parts : parts + 7]
    coef_ref, mean_ref, smooth_ref, block_ref, enter_ref, strip_ref = refs[parts + 7 :]
    steps, modes = coef_ref.shape
    chunks = steps // CHUNK
    c = part_refs[0][...]
    for ref in part_refs[1:]:
        c = c + decode(ref)
    coef_ref[...] = c
    lanes(coef_ref, strip_ref)
    f = e = jnp.zeros((chunks, modes), F32)
    for i in range(CHUNK):
        f = a_ref[i] * f + b_ref[i] * chunk_rows(strip_ref, i, chunks)
        k = CHUNK - 1 - i
        e = alpha_ref[k] * e + beta_ref[k] * chunk_rows(strip_ref, k, chunks)
    mean_ref[0] = f
    mean_ref[1] = e
    f = e = jnp.zeros((1, modes), F32)
    for c in range(chunks):
        k = chunks - 1 - c
        enter_ref[0, c : c + 1, :] = f
        enter_ref[1, k : k + 1, :] = e
        f = mean_ref[0, c : c + 1, :] + carry_ref[0, c : c + 1, :] * f
        e = mean_ref[1, k : k + 1, :] + carry_ref[1, k : k + 1, :] * e
    block_ref[0:1, :] = f
    block_ref[1:2, :] = e
    f = enter_ref[0]
    e = enter_ref[1]
    for i in range(CHUNK):
        f = a_ref[i] * f + b_ref[i] * chunk_rows(strip_ref, i, chunks)
        mean_ref[i] = f
    for i in reversed(range(CHUNK)):
        smooth_ref[i] = keep_ref[i] * mean_ref[i] + lift_ref[i] * e
        e = alpha_ref[i] * e + beta_ref[i] * chunk_rows(strip_ref, i, chunks)


def finish_kernel(count, me_ref, prior_ref, whole_ref, edge_ref, blocks_ref, mean_ref, smooth_ref, out_mean_ref, out_smooth_ref, mean_strip_ref, smooth_strip_ref):
    steps, modes = out_mean_ref.shape
    chunks = steps // CHUNK
    me = me_ref[0]
    f = prior_ref[...]
    e = jnp.zeros((1, modes), F32)
    for j in range(count - 1):
        f = jnp.where(j < me, blocks_ref[j, 0:1, :] + edge_ref[0, j : j + 1, :] * f, f)
        k = count - 1 - j
        e = jnp.where(k > me, blocks_ref[k, 1:2, :] + edge_ref[1, k : k + 1, :] * e, e)
    f = jnp.broadcast_to(f, (chunks, modes))
    e = jnp.broadcast_to(e, (chunks, modes))
    for i in range(CHUNK):
        put_rows(mean_strip_ref, i, chunks, mean_ref[i] + whole_ref[0, i] * f)
        put_rows(smooth_strip_ref, i, chunks, smooth_ref[i] + whole_ref[1, i] * f + whole_ref[2, i] * e)
    unlanes(mean_strip_ref, out_mean_ref)
    unlanes(smooth_strip_ref, out_smooth_ref)


def encode(values, ref):
    steps = values.shape[0]
    top = jnp.max(jnp.abs(values), axis=0, keepdims=True)
    power = jnp.floor(jnp.log2(jnp.maximum(top, TINY))) + 1.0
    coded = jnp.floor(values * (jnp.exp2(-power) * STEPS16) + 0.5)
    ref[0:steps, :] = coded.astype(jnp.int32).astype(jnp.int16)
    power = jnp.broadcast_to(power, (PAD, power.shape[1]))
    ref[steps : steps + PAD, :] = power.astype(jnp.int32).astype(jnp.int16)


def decode(ref):
    steps = ref.shape[0] - PAD
    power = ref[steps : steps + PAD, :].astype(jnp.int32).astype(F32)[0:1, :]
    return ref[0:steps, :].astype(jnp.int32).astype(F32) * (jnp.exp2(power) * (1.0 / STEPS16))


def project_kernel(held, at_ref, slab_ref, basis_ref, own_ref, *refs):
    owners = at_ref.shape[0] - 1
    coded_refs = refs[: owners - 1]
    basis_area, sum_area, basis_sems, *refs = refs[owners - 1 :]
    slab_area = slab_ref if held else refs[0]
    count = slab_ref.shape[0]
    modes = own_ref.shape[1]
    copies = []
    for g in range(count):
        pair = [pltpu.make_async_copy(basis_ref.at[at_ref[0] + g], basis_area.at[g], basis_sems.at[g])]
        if not held:
            pair.append(pltpu.make_async_copy(slab_ref.at[g], slab_area.at[g], refs[1].at[g]))
        copies.append(pair)
    for pair in copies:
        for copy in pair:
            copy.start()
    for g in range(count):
        for copy in copies[g]:
            copy.wait()
        for turn in range(owners):
            columns = pl.ds(pl.multiple_of(at_ref[1 + turn] * modes, LANES), modes)
            term = jnp.dot(slab_area[g], basis_area[g, :, columns], preferred_element_type=F32)
            sum_area[turn] = term if g == 0 else sum_area[turn] + term
    own_ref[...] = sum_area[0]
    for turn in range(1, owners):
        encode(sum_area[turn], coded_refs[turn - 1])


def project(slabs, basis, first, owners, modes, held=False):
    count, steps, cells = slabs.shape
    others = len(owners) - 1
    own, *coded = pl.pallas_call(
        functools.partial(project_kernel, held),
        in_specs=[
            pl.BlockSpec(memory_space=pltpu.SMEM),
            pl.BlockSpec(memory_space=pltpu.VMEM if held else pl.ANY),
            pl.BlockSpec(memory_space=pl.ANY),
        ],
        out_specs=[pl.BlockSpec(memory_space=pltpu.VMEM)] * (1 + others),
        out_shape=[jax.ShapeDtypeStruct((steps, modes), F32)]
        + [jax.ShapeDtypeStruct((steps + PAD, modes), jnp.int16)] * others,
        scratch_shapes=[
            pltpu.VMEM((count,) + basis.shape[1:], basis.dtype),
            pltpu.VMEM((1 + others, steps, modes), F32),
            pltpu.SemaphoreType.DMA((count,)),
        ]
        + ([] if held else [pltpu.VMEM(slabs.shape, slabs.dtype), pltpu.SemaphoreType.DMA((count,))]),
        compiler_params=pltpu.CompilerParams(vmem_limit_bytes=(36 if held else 60) * LIMIT // 16),
        cost_estimate=pl.CostEstimate(
            flops=2 * count * steps * cells * modes * (1 + others),
            bytes_accessed=2 * count * cells * (steps + modes * (1 + others)) + 4 * steps * modes,
            transcendentals=0,
        ),
    )(jnp.stack([first] + owners), slabs, basis)
    return own, coded


def fold_kernel(own_ref, *refs):
    total = own_ref[...]
    for ref in refs[:-1]:
        total = total + decode(ref)
    encode(total, refs[-1])


def call(kernel, inputs, outputs, scratch, flops):
    smem = pl.BlockSpec(memory_space=pltpu.SMEM)
    vmem = pl.BlockSpec(memory_space=pltpu.VMEM)
    moved = sum(4 * x.size for x in inputs) + sum(4 * x.size for x in outputs)
    return pl.pallas_call(
        kernel,
        in_specs=[smem if x.dtype == jnp.int32 else vmem for x in inputs],
        out_specs=[vmem] * len(outputs),
        out_shape=outputs,
        scratch_shapes=scratch,
        compiler_params=pltpu.CompilerParams(vmem_limit_bytes=LIMIT),
        cost_estimate=pl.CostEstimate(flops=flops, bytes_accessed=moved, transcendentals=0),
    )(*inputs)


def swap_halves(block, axis):
    half = lax.axis_size(axis) // 2
    return lax.ppermute(block, axis, [(i, (i + half) % (2 * half)) for i in range(2 * half)])


def send_along(term, axis, turn):
    count = lax.axis_size(axis)
    return lax.ppermute(term, axis, [(i, (i + turn) % count) for i in range(count)])


def body(observations, pod_basis, decay, step_mask, process_var, obs_var, prior_mean, prior_var):
    tm_count = lax.axis_size("tm")
    space_count = lax.axis_size("space")
    steps, modes = decay.shape
    chunks = steps // CHUNK
    rank = lax.axis_index("tm").astype(jnp.int32)
    me = rank.reshape(1)
    side = lax.axis_index("space").astype(jnp.int32)
    shape = functools.partial(jax.ShapeDtypeStruct, dtype=F32)
    area = pltpu.VMEM
    group = tm_count // 2
    groups = [[half * group + i for i in range(group)] for half in range(2)]
    half = rank // group

    seen = jnp.broadcast_to(step_mask.astype(F32)[:, None], (steps, modes))
    q, r = process_var[None, :], obs_var[None, :]
    flat = (chunks, modes)
    deep = (CHUNK, chunks, modes)
    strips = area((modes // LANES, steps, LANES), F32)
    slabs = observations.reshape(2, group, steps, observations.shape[3])
    basis = pod_basis.reshape(tm_count, -1, pod_basis.shape[3])
    first = half * group
    owners = [lax.rem(side + turn, space_count) for turn in range(space_count)]
    far = lax.dynamic_index_in_dim(slabs, 1 - half, 0, keepdims=False)
    far, q = lax.optimization_barrier((far, q))
    far = lax.all_to_all(far, "tm", 0, 0, axis_index_groups=groups, tiled=True)
    chunk_totals, block_totals = call(
        totals_kernel, (me, decay, seen, q, r), [shape((3,) + flat), shape((3, modes))], [strips] * 2, 40 * steps * modes
    )
    block_totals, own_half = lax.optimization_barrier((block_totals, half))
    near = lax.dynamic_index_in_dim(slabs, own_half, 0, keepdims=False)
    blocks = gather_near(block_totals, "tm")
    far, near, blocks = lax.optimization_barrier((far, near, blocks))
    near = lax.all_to_all(near, "tm", 0, 0, axis_index_groups=groups, tiled=True)

    own, theirs = project(far, basis, first, owners, modes)
    arriving = [send_along(term, "space", turn + 1) for turn, term in enumerate(theirs)]
    coded = jax.ShapeDtypeStruct((steps + PAD, modes), jnp.int16)
    (crossing,) = call(fold_kernel, (own, *arriving), [coded], [], 8 * steps * modes)
    near, _ = lax.optimization_barrier((near, crossing))
    crossing = swap_halves(crossing, "tm")
    blocks = gather_far(blocks, "tm")

    own, theirs = project(near, basis, first, owners, modes, True)
    parts = [send_along(term, "space", turn + 1) for turn, term in enumerate(theirs)] + [crossing]
    own, chunk_totals, blocks = lax.optimization_barrier((own, chunk_totals, blocks))
    parts.insert(0, own)
    *maps, whole, carry, edge, log_variance = call(
        functools.partial(gains_kernel, tm_count),
        (me, decay, seen, q, r, prior_var[None, :], chunk_totals, blocks),
        [shape(deep)] * 6 + [shape((3,) + deep), shape((2,) + flat), shape((2, tm_count, modes)), shape((steps, modes))],
        [area((2,) + flat, F32), area(deep, F32), area(deep, F32), strips, strips],
        80 * steps * modes,
    )

    coefficients, mean, smooth, ends = call(
        functools.partial(means_kernel, len(parts)),
        (*parts, *maps, carry),
        [shape((steps, modes)), shape(deep), shape(deep), shape((2, modes))],
        [area((2,) + flat, F32), strips],
        12 * steps * modes,
    )
    ends = jnp.broadcast_to(ends[None], (tm_count,) + ends.shape)
    ends = lax.all_to_all(ends, "tm", 0, 0, tiled=True)
    filtered, smoothed = call(
        functools.partial(finish_kernel, tm_count),
        (me, prior_mean[None, :], whole, edge, ends, mean, smooth),
        [shape((steps, modes))] * 2,
        [strips, strips],
        8 * steps * modes,
    )
    return coefficients, filtered, smoothed, log_variance


def solution(mesh):
    return jax.shard_map(
        body,
        mesh=mesh,
        in_specs=(
            P(None, "tm", "space", None),
            P(None, "space", None, None),
            P("tm", "space"),
            P("tm"),
            P("space"),
            P("space"),
            P("space"),
            P("space"),
        ),
        out_specs=(P("tm", "space"), P("tm", "space"), P("tm", "space"), P("tm", "space")),
        check_vma=False,
    )
```

```python
import functools

import jax
import jax.numpy as jnp
from jax import lax
from jax.experimental import pallas as pl
from jax.experimental.pallas import tpu as pltpu
from jax.sharding import PartitionSpec as P

CHUNK = 16
LANES = 128
PAD = 16
STEPS16 = 32512.0
TINY = 1e-30
F32 = jnp.float32
LIMIT = 16 * 1024 * 1024


def rotate(block, axis, turn, group):
    route = [(i, i // group * group + (i + turn) % group) for i in range(lax.axis_size(axis))]
    return lax.ppermute(block, axis, route)


def inner_size(count):
    group = 1
    while group * group < count:
        group *= 2
    return group if count % group == 0 else count


def gather_near(rows, axis):
    count = lax.axis_size(axis)
    group = inner_size(count)
    return jnp.stack([rows] + [rotate(rows, axis, s, group) for s in range(1, group)])


def gather_far(near, axis):
    count = lax.axis_size(axis)
    group = near.shape[0]
    return [
        lax.ppermute(near, axis, [(i, i ^ (turn * group)) for i in range(count)]) for turn in range(1, count // group)
    ]


def place(me, j, count):
    group = inner_size(count)
    high = lax.bitwise_xor(me // group, j // group)
    low = lax.rem(lax.rem(me, group) - j % group + group, group)
    return high * group + low


def lanes(ref, strip_ref):
    for m in range(strip_ref.shape[0]):
        strip_ref[m] = ref[:, m * LANES : (m + 1) * LANES]


def unlanes(strip_ref, ref):
    for m in range(strip_ref.shape[0]):
        ref[:, m * LANES : (m + 1) * LANES] = strip_ref[m]


def chunk_rows(strip_ref, i, chunks):
    rows = pl.ds(i, chunks, stride=CHUNK)
    return jnp.concatenate([strip_ref[m, rows, :] for m in range(strip_ref.shape[0])], 1)


def put_rows(strip_ref, i, chunks, value):
    rows = pl.ds(i, chunks, stride=CHUNK)
    for m in range(strip_ref.shape[0]):
        strip_ref[m, rows, :] = value[:, m * LANES : (m + 1) * LANES]


def opened(me_ref, shape):
    rows = lax.broadcasted_iota(jnp.int32, shape, 0)
    return jnp.logical_and(rows == 0, me_ref[0] == 0)


def step_terms(i, chunks, first, q, r, decay_ref, seen_ref):
    d = chunk_rows(decay_ref, i, chunks)
    seen = chunk_rows(seen_ref, i, chunks) > 0.5
    base = q
    if i == 0:
        d = jnp.where(first, 1.0, d)
        base = jnp.where(first, 0.0, q)
    return d, seen, base


def element(d, seen, base, r):
    inverse = 1.0 / (base + r)
    retain = jnp.where(seen, r * inverse, 1.0)
    return retain * d, retain * base, jnp.where(seen, d * d * inverse, 0.0), inverse


def join(early, late):
    lead, spread, weight = early
    lead_late, spread_late, weight_late = late
    factor = 1.0 / (1.0 + spread * weight_late)
    return (
        lead_late * factor * lead,
        lead_late * lead_late * factor * spread + spread_late,
        lead * lead * factor * weight_late + weight,
    )


def totals_kernel(me_ref, decay_in, seen_in, q_ref, r_ref, chunk_ref, block_ref, decay_ref, seen_ref):
    steps, modes = decay_in.shape
    lanes(decay_in, decay_ref)
    lanes(seen_in, seen_ref)
    chunks = steps // CHUNK
    shape = (chunks, modes)
    q = jnp.broadcast_to(q_ref[...], shape)
    r = jnp.broadcast_to(r_ref[...], shape)
    first = opened(me_ref, shape)
    total = None
    for i in range(CHUNK):
        step = element(*step_terms(i, chunks, first, q, r, decay_ref, seen_ref), r)[:3]
        total = step if i == 0 else join(total, step)
    for k in range(3):
        chunk_ref[k] = total[k]
    total = tuple(chunk_ref[k, 0:1, :] for k in range(3))
    for c in range(1, chunks):
        total = join(total, tuple(chunk_ref[k, c : c + 1, :] for k in range(3)))
    for k in range(3):
        block_ref[k : k + 1, :] = total[k]


def gains_kernel(
    count, me_ref, decay_in, seen_in, q_ref, r_ref, prior_ref, chunk_ref, blocks_ref,
    a_ref, b_ref, alpha_ref, beta_ref, keep_ref, lift_ref, whole_ref, carry_ref, edge_ref, log_ref,
    enter_ref, var_ref, info_ref, decay_ref, seen_ref,
):
    steps, modes = decay_in.shape
    lanes(decay_in, decay_ref)
    lanes(seen_in, seen_ref)
    chunks = steps // CHUNK
    shape = (chunks, modes)
    me = me_ref[0]
    q = jnp.broadcast_to(q_ref[...], shape)
    r = jnp.broadcast_to(r_ref[...], shape)
    first = opened(me_ref, shape)

    v = prior_ref[...]
    mine = v
    for j in range(count):
        mine = jnp.where(j == me, v, mine)
        at = place(me, j, count)
        lead, spread, weight = (blocks_ref[at, k : k + 1, :] for k in range(3))
        along = lead / (1.0 + weight * v)
        edge_ref[0, j : j + 1, :] = along
        v = spread + lead * along * v
    v = mine
    for c in range(chunks):
        enter_ref[0, c : c + 1, :] = v
        lead, spread, weight = (chunk_ref[k, c : c + 1, :] for k in range(3))
        v = spread + lead * lead * v / (1.0 + weight * v)

    info = jnp.zeros((1, modes), F32)
    mine = info
    for j in reversed(range(count)):
        mine = jnp.where(j == me, info, mine)
        at = place(me, j, count)
        lead, spread, weight = (blocks_ref[at, k : k + 1, :] for k in range(3))
        along = lead / (1.0 + spread * info)
        edge_ref[1, j : j + 1, :] = along
        info = weight + lead * along * info
    info = mine
    for c in reversed(range(chunks)):
        enter_ref[1, c : c + 1, :] = info
        lead, spread, weight = (chunk_ref[k, c : c + 1, :] for k in range(3))
        info = weight + lead * lead * info / (1.0 + spread * info)

    v = enter_ref[0]
    run = None
    for i in range(CHUNK):
        d, seen, base = step_terms(i, chunks, first, q, r, decay_ref, seen_ref)
        ahead = d * d * v + base
        inverse = 1.0 / (ahead + r)
        retain = jnp.where(seen, r * inverse, 1.0)
        v = retain * ahead
        a = retain * d
        run = a if i == 0 else a * run
        a_ref[i] = a
        b_ref[i] = jnp.where(seen, ahead * inverse, 0.0)
        var_ref[i] = v
        whole_ref[0, i] = run
    carry_ref[0] = run

    info = enter_ref[1]
    run = jnp.ones(shape, F32)
    for i in reversed(range(CHUNK)):
        lead, spread, weight, inverse = element(*step_terms(i, chunks, first, q, r, decay_ref, seen_ref), r)
        d, seen, _ = step_terms(i, chunks, first, q, r, decay_ref, seen_ref)
        factor = 1.0 / (1.0 + spread * info)
        alpha = lead * factor
        info_ref[i] = info
        whole_ref[2, i] = run
        alpha_ref[i] = alpha
        beta_ref[i] = jnp.where(seen, d * inverse * factor, 0.0)
        info = weight + lead * alpha * info
        run = alpha * run
    carry_ref[1] = run

    along = jnp.ones((1, modes), F32)
    for c in range(chunks):
        enter_ref[0, c : c + 1, :] = along
        along = along * carry_ref[0, c : c + 1, :]
    along = jnp.ones((1, modes), F32)
    for c in reversed(range(chunks)):
        enter_ref[1, c : c + 1, :] = along
        along = along * carry_ref[1, c : c + 1, :]
    onward = enter_ref[0]
    back = enter_ref[1]
    for i in range(CHUNK):
        v = var_ref[i]
        keep = 1.0 / (1.0 + v * info_ref[i])
        lift = v * keep
        weight = whole_ref[0, i] * onward
        keep_ref[i] = keep
        lift_ref[i] = lift
        whole_ref[0, i] = weight
        whole_ref[1, i] = keep * weight
        whole_ref[2, i] = lift * (whole_ref[2, i] * back)
        put_rows(decay_ref, i, chunks, jnp.log(lift))
    unlanes(decay_ref, log_ref)


def means_kernel(parts, *refs):
    part_refs = refs[:parts]
    a_ref, b_ref, alpha_ref, beta_ref, keep_ref, lift_ref, carry_ref = refs[parts : parts + 7]
    coef_ref, mean_ref, smooth_ref, block_ref, enter_ref, strip_ref = refs[parts + 7 :]
    steps, modes = coef_ref.shape
    chunks = steps // CHUNK
    c = part_refs[0][...]
    for ref in part_refs[1:]:
        c = c + decode(ref)
    coef_ref[...] = c
    lanes(coef_ref, strip_ref)
    f = e = jnp.zeros((chunks, modes), F32)
    for i in range(CHUNK):
        f = a_ref[i] * f + b_ref[i] * chunk_rows(strip_ref, i, chunks)
        k = CHUNK - 1 - i
        e = alpha_ref[k] * e + beta_ref[k] * chunk_rows(strip_ref, k, chunks)
    mean_ref[0] = f
    mean_ref[1] = e
    f = e = jnp.zeros((1, modes), F32)
    for c in range(chunks):
        k = chunks - 1 - c
        enter_ref[0, c : c + 1, :] = f
        enter_ref[1, k : k + 1, :] = e
        f = mean_ref[0, c : c + 1, :] + carry_ref[0, c : c + 1, :] * f
        e = mean_ref[1, k : k + 1, :] + carry_ref[1, k : k + 1, :] * e
    block_ref[0:1, :] = f
    block_ref[1:2, :] = e
    f = enter_ref[0]
    e = enter_ref[1]
    for i in range(CHUNK):
        f = a_ref[i] * f + b_ref[i] * chunk_rows(strip_ref, i, chunks)
        mean_ref[i] = f
    for i in reversed(range(CHUNK)):
        smooth_ref[i] = keep_ref[i] * mean_ref[i] + lift_ref[i] * e
        e = alpha_ref[i] * e + beta_ref[i] * chunk_rows(strip_ref, i, chunks)


def finish_kernel(count, me_ref, prior_ref, whole_ref, edge_ref, blocks_ref, mean_ref, smooth_ref, out_mean_ref, out_smooth_ref, mean_strip_ref, smooth_strip_ref):
    steps, modes = out_mean_ref.shape
    chunks = steps // CHUNK
    me = me_ref[0]
    f = prior_ref[...]
    e = jnp.zeros((1, modes), F32)
    for j in range(count - 1):
        f = jnp.where(j < me, blocks_ref[j, 0:1, :] + edge_ref[0, j : j + 1, :] * f, f)
        k = count - 1 - j
        e = jnp.where(k > me, blocks_ref[k, 1:2, :] + edge_ref[1, k : k + 1, :] * e, e)
    f = jnp.broadcast_to(f, (chunks, modes))
    e = jnp.broadcast_to(e, (chunks, modes))
    for i in range(CHUNK):
        put_rows(mean_strip_ref, i, chunks, mean_ref[i] + whole_ref[0, i] * f)
        put_rows(smooth_strip_ref, i, chunks, smooth_ref[i] + whole_ref[1, i] * f + whole_ref[2, i] * e)
    unlanes(mean_strip_ref, out_mean_ref)
    unlanes(smooth_strip_ref, out_smooth_ref)


def encode(values, ref):
    steps = values.shape[0]
    top = jnp.max(jnp.abs(values), axis=0, keepdims=True)
    power = jnp.floor(jnp.log2(jnp.maximum(top, TINY))) + 1.0
    coded = jnp.floor(values * (jnp.exp2(-power) * STEPS16) + 0.5)
    ref[0:steps, :] = coded.astype(jnp.int32).astype(jnp.int16)
    power = jnp.broadcast_to(power, (PAD, power.shape[1]))
    ref[steps : steps + PAD, :] = power.astype(jnp.int32).astype(jnp.int16)


def decode(ref):
    steps = ref.shape[0] - PAD
    power = ref[steps : steps + PAD, :].astype(jnp.int32).astype(F32)[0:1, :]
    return ref[0:steps, :].astype(jnp.int32).astype(F32) * (jnp.exp2(power) * (1.0 / STEPS16))


def project_kernel(held, at_ref, slab_ref, basis_ref, own_ref, *refs):
    owners = at_ref.shape[0] - 1
    coded_refs = refs[: owners - 1]
    basis_area, sum_area, basis_sems, *refs = refs[owners - 1 :]
    slab_area = slab_ref if held else refs[0]
    count = slab_ref.shape[0]
    modes = own_ref.shape[1]
    copies = []
    for g in range(count):
        pair = [pltpu.make_async_copy(basis_ref.at[at_ref[0] + g], basis_area.at[g], basis_sems.at[g])]
        if not held:
            pair.append(pltpu.make_async_copy(slab_ref.at[g], slab_area.at[g], refs[1].at[g]))
        copies.append(pair)
    for pair in copies:
        for copy in pair:
            copy.start()
    for g in range(count):
        for copy in copies[g]:
            copy.wait()
        for turn in range(owners):
            columns = pl.ds(pl.multiple_of(at_ref[1 + turn] * modes, LANES), modes)
            term = jnp.dot(slab_area[g], basis_area[g, :, columns], preferred_element_type=F32)
            sum_area[turn] = term if g == 0 else sum_area[turn] + term
    own_ref[...] = sum_area[0]
    for turn in range(1, owners):
        encode(sum_area[turn], coded_refs[turn - 1])


def project(slabs, basis, first, owners, modes, held=False):
    count, steps, cells = slabs.shape
    others = len(owners) - 1
    own, *coded = pl.pallas_call(
        functools.partial(project_kernel, held),
        in_specs=[
            pl.BlockSpec(memory_space=pltpu.SMEM),
            pl.BlockSpec(memory_space=pltpu.VMEM if held else pl.ANY),
            pl.BlockSpec(memory_space=pl.ANY),
        ],
        out_specs=[pl.BlockSpec(memory_space=pltpu.VMEM)] * (1 + others),
        out_shape=[jax.ShapeDtypeStruct((steps, modes), F32)]
        + [jax.ShapeDtypeStruct((steps + PAD, modes), jnp.int16)] * others,
        scratch_shapes=[
            pltpu.VMEM((count,) + basis.shape[1:], basis.dtype),
            pltpu.VMEM((1 + others, steps, modes), F32),
            pltpu.SemaphoreType.DMA((count,)),
        ]
        + ([] if held else [pltpu.VMEM(slabs.shape, slabs.dtype), pltpu.SemaphoreType.DMA((count,))]),
        compiler_params=pltpu.CompilerParams(vmem_limit_bytes=(36 if held else 60) * LIMIT // 16),
        cost_estimate=pl.CostEstimate(
            flops=2 * count * steps * cells * modes * (1 + others),
            bytes_accessed=2 * count * cells * (steps + modes * (1 + others)) + 4 * steps * modes,
            transcendentals=0,
        ),
    )(jnp.stack([first] + owners), slabs, basis)
    return own, coded


def fold_kernel(own_ref, *refs):
    total = own_ref[...]
    for ref in refs[:-1]:
        total = total + decode(ref)
    encode(total, refs[-1])


def call(kernel, inputs, outputs, scratch, flops):
    smem = pl.BlockSpec(memory_space=pltpu.SMEM)
    vmem = pl.BlockSpec(memory_space=pltpu.VMEM)
    moved = sum(4 * x.size for x in inputs) + sum(4 * x.size for x in outputs)
    return pl.pallas_call(
        kernel,
        in_specs=[smem if x.dtype == jnp.int32 else vmem for x in inputs],
        out_specs=[vmem] * len(outputs),
        out_shape=outputs,
        scratch_shapes=scratch,
        compiler_params=pltpu.CompilerParams(vmem_limit_bytes=LIMIT),
        cost_estimate=pl.CostEstimate(flops=flops, bytes_accessed=moved, transcendentals=0),
    )(*inputs)


def swap_halves(block, axis):
    half = lax.axis_size(axis) // 2
    return lax.ppermute(block, axis, [(i, (i + half) % (2 * half)) for i in range(2 * half)])


def send_along(term, axis, turn):
    count = lax.axis_size(axis)
    return lax.ppermute(term, axis, [(i, (i + turn) % count) for i in range(count)])


def body(observations, pod_basis, decay, step_mask, process_var, obs_var, prior_mean, prior_var):
    tm_count = lax.axis_size("tm")
    space_count = lax.axis_size("space")
    steps, modes = decay.shape
    chunks = steps // CHUNK
    rank = lax.axis_index("tm").astype(jnp.int32)
    me = rank.reshape(1)
    side = lax.axis_index("space").astype(jnp.int32)
    shape = functools.partial(jax.ShapeDtypeStruct, dtype=F32)
    area = pltpu.VMEM
    group = tm_count // 2
    groups = [[half * group + i for i in range(group)] for half in range(2)]
    half = rank // group

    seen = jnp.broadcast_to(step_mask.astype(F32)[:, None], (steps, modes))
    q, r = process_var[None, :], obs_var[None, :]
    flat = (chunks, modes)
    deep = (CHUNK, chunks, modes)
    strips = area((modes // LANES, steps, LANES), F32)
    slabs = observations.reshape(2, group, steps, observations.shape[3])
    basis = pod_basis.reshape(tm_count, -1, pod_basis.shape[3])
    first = half * group
    owners = [lax.rem(side + turn, space_count) for turn in range(space_count)]
    far = lax.dynamic_index_in_dim(slabs, 1 - half, 0, keepdims=False)
    far, q = lax.optimization_barrier((far, q))
    far = lax.all_to_all(far, "tm", 0, 0, axis_index_groups=groups, tiled=True)
    chunk_totals, block_totals = call(
        totals_kernel, (me, decay, seen, q, r), [shape((3,) + flat), shape((3, modes))], [strips] * 2, 40 * steps * modes
    )
    block_totals, own_half = lax.optimization_barrier((block_totals, half))
    near = lax.dynamic_index_in_dim(slabs, own_half, 0, keepdims=False)
    blocks = gather_near(block_totals, "tm")
    far, near, blocks = lax.optimization_barrier((far, near, blocks))
    near = lax.all_to_all(near, "tm", 0, 0, axis_index_groups=groups, tiled=True)

    own, theirs = project(far, basis, first, owners, modes)
    own, blocks = lax.optimization_barrier((own, blocks))
    rest = gather_far(blocks, "tm")
    arriving = [send_along(term, "space", turn + 1) for turn, term in enumerate(theirs)]
    coded = jax.ShapeDtypeStruct((steps + PAD, modes), jnp.int16)
    (crossing,) = call(fold_kernel, (own, *arriving), [coded], [], 8 * steps * modes)
    rest, near, crossing = lax.optimization_barrier((rest, near, crossing))
    crossing = swap_halves(crossing, "tm")

    own, theirs = project(near, basis, first, owners, modes, True)
    parts = [send_along(term, "space", turn + 1) for turn, term in enumerate(theirs)] + [crossing]
    own, chunk_totals, rest = lax.optimization_barrier((own, chunk_totals, rest))
    blocks = jnp.concatenate([blocks] + rest, 0)
    parts.insert(0, own)
    *maps, whole, carry, edge, log_variance = call(
        functools.partial(gains_kernel, tm_count),
        (me, decay, seen, q, r, prior_var[None, :], chunk_totals, blocks),
        [shape(deep)] * 6 + [shape((3,) + deep), shape((2,) + flat), shape((2, tm_count, modes)), shape((steps, modes))],
        [area((2,) + flat, F32), area(deep, F32), area(deep, F32), strips, strips],
        80 * steps * modes,
    )

    coefficients, mean, smooth, ends = call(
        functools.partial(means_kernel, len(parts)),
        (*parts, *maps, carry),
        [shape((steps, modes)), shape(deep), shape(deep), shape((2, modes))],
        [area((2,) + flat, F32), strips],
        12 * steps * modes,
    )
    ends = jnp.broadcast_to(ends[None], (tm_count,) + ends.shape)
    ends = lax.all_to_all(ends, "tm", 0, 0, tiled=True)
    filtered, smoothed = call(
        functools.partial(finish_kernel, tm_count),
        (me, prior_mean[None, :], whole, edge, ends, mean, smooth),
        [shape((steps, modes))] * 2,
        [strips, strips],
        8 * steps * modes,
    )
    return coefficients, filtered, smoothed, log_variance


def solution(mesh):
    return jax.shard_map(
        body,
        mesh=mesh,
        in_specs=(
            P(None, "tm", "space", None),
            P(None, "space", None, None),
            P("tm", "space"),
            P("tm"),
            P("space"),
            P("space"),
            P("space"),
            P("space"),
        ),
        out_specs=(P("tm", "space"), P("tm", "space"), P("tm", "space"), P("tm", "space")),
        check_vma=False,
    )
```

```python
import functools

import jax
import jax.numpy as jnp
from jax import lax
from jax.experimental import pallas as pl
from jax.experimental.pallas import tpu as pltpu
from jax.sharding import PartitionSpec as P

CHUNK = 16
LANES = 128
PAD = 16
STEPS16 = 32512.0
TINY = 1e-30
EARLY = 1 << 34
F32 = jnp.float32
LIMIT = 16 * 1024 * 1024


def rotate(block, axis, turn, group):
    route = [(i, i // group * group + (i + turn) % group) for i in range(lax.axis_size(axis))]
    return lax.ppermute(block, axis, route)


def inner_size(count):
    group = 1
    while group * group < count:
        group *= 2
    return group if count % group == 0 else count


def gather_near(rows, axis):
    count = lax.axis_size(axis)
    group = inner_size(count)
    return jnp.stack([rows] + [rotate(rows, axis, s, group) for s in range(1, group)])


def gather_far(near, axis):
    count = lax.axis_size(axis)
    group = near.shape[0]
    return [
        lax.ppermute(near, axis, [(i, i ^ (turn * group)) for i in range(count)]) for turn in range(1, count // group)
    ]


def place(me, j, count):
    group = inner_size(count)
    high = lax.bitwise_xor(me // group, j // group)
    low = lax.rem(lax.rem(me, group) - j % group + group, group)
    return high * group + low


def lanes(ref, strip_ref):
    for m in range(strip_ref.shape[0]):
        strip_ref[m] = ref[:, m * LANES : (m + 1) * LANES]


def unlanes(strip_ref, ref):
    for m in range(strip_ref.shape[0]):
        ref[:, m * LANES : (m + 1) * LANES] = strip_ref[m]


def chunk_rows(strip_ref, i, chunks):
    rows = pl.ds(i, chunks, stride=CHUNK)
    return jnp.concatenate([strip_ref[m, rows, :] for m in range(strip_ref.shape[0])], 1)


def put_rows(strip_ref, i, chunks, value):
    rows = pl.ds(i, chunks, stride=CHUNK)
    for m in range(strip_ref.shape[0]):
        strip_ref[m, rows, :] = value[:, m * LANES : (m + 1) * LANES]


def opened(me_ref, shape):
    rows = lax.broadcasted_iota(jnp.int32, shape, 0)
    return jnp.logical_and(rows == 0, me_ref[0] == 0)


def step_terms(i, chunks, first, q, r, decay_ref, seen_ref):
    d = chunk_rows(decay_ref, i, chunks)
    seen = chunk_rows(seen_ref, i, chunks) > 0.5
    base = q
    if i == 0:
        d = jnp.where(first, 1.0, d)
        base = jnp.where(first, 0.0, q)
    return d, seen, base


def element(d, seen, base, r):
    inverse = 1.0 / (base + r)
    retain = jnp.where(seen, r * inverse, 1.0)
    return retain * d, retain * base, jnp.where(seen, d * d * inverse, 0.0), inverse


def join(early, late):
    lead, spread, weight = early
    lead_late, spread_late, weight_late = late
    factor = 1.0 / (1.0 + spread * weight_late)
    return (
        lead_late * factor * lead,
        lead_late * lead_late * factor * spread + spread_late,
        lead * lead * factor * weight_late + weight,
    )


def totals_kernel(me_ref, decay_in, seen_in, q_ref, r_ref, chunk_ref, block_ref, decay_ref, seen_ref):
    steps, modes = decay_in.shape
    lanes(decay_in, decay_ref)
    lanes(seen_in, seen_ref)
    chunks = steps // CHUNK
    shape = (chunks, modes)
    q = jnp.broadcast_to(q_ref[...], shape)
    r = jnp.broadcast_to(r_ref[...], shape)
    first = opened(me_ref, shape)
    total = None
    for i in range(CHUNK):
        step = element(*step_terms(i, chunks, first, q, r, decay_ref, seen_ref), r)[:3]
        total = step if i == 0 else join(total, step)
    for k in range(3):
        chunk_ref[k] = total[k]
    total = tuple(chunk_ref[k, 0:1, :] for k in range(3))
    for c in range(1, chunks):
        total = join(total, tuple(chunk_ref[k, c : c + 1, :] for k in range(3)))
    for k in range(3):
        block_ref[k : k + 1, :] = total[k]


def gains_kernel(
    count, me_ref, decay_in, seen_in, q_ref, r_ref, prior_ref, chunk_ref, blocks_ref,
    a_ref, b_ref, alpha_ref, beta_ref, keep_ref, lift_ref, whole_ref, carry_ref, edge_ref, log_ref,
    enter_ref, var_ref, info_ref, decay_ref, seen_ref,
):
    steps, modes = decay_in.shape
    lanes(decay_in, decay_ref)
    lanes(seen_in, seen_ref)
    chunks = steps // CHUNK
    shape = (chunks, modes)
    me = me_ref[0]
    q = jnp.broadcast_to(q_ref[...], shape)
    r = jnp.broadcast_to(r_ref[...], shape)
    first = opened(me_ref, shape)

    v = prior_ref[...]
    mine = v
    for j in range(count):
        mine = jnp.where(j == me, v, mine)
        at = place(me, j, count)
        lead, spread, weight = (blocks_ref[at, k : k + 1, :] for k in range(3))
        along = lead / (1.0 + weight * v)
        edge_ref[0, j : j + 1, :] = along
        v = spread + lead * along * v
    v = mine
    for c in range(chunks):
        enter_ref[0, c : c + 1, :] = v
        lead, spread, weight = (chunk_ref[k, c : c + 1, :] for k in range(3))
        v = spread + lead * lead * v / (1.0 + weight * v)

    info = jnp.zeros((1, modes), F32)
    mine = info
    for j in reversed(range(count)):
        mine = jnp.where(j == me, info, mine)
        at = place(me, j, count)
        lead, spread, weight = (blocks_ref[at, k : k + 1, :] for k in range(3))
        along = lead / (1.0 + spread * info)
        edge_ref[1, j : j + 1, :] = along
        info = weight + lead * along * info
    info = mine
    for c in reversed(range(chunks)):
        enter_ref[1, c : c + 1, :] = info
        lead, spread, weight = (chunk_ref[k, c : c + 1, :] for k in range(3))
        info = weight + lead * lead * info / (1.0 + spread * info)

    v = enter_ref[0]
    run = None
    for i in range(CHUNK):
        d, seen, base = step_terms(i, chunks, first, q, r, decay_ref, seen_ref)
        ahead = d * d * v + base
        inverse = 1.0 / (ahead + r)
        retain = jnp.where(seen, r * inverse, 1.0)
        v = retain * ahead
        a = retain * d
        run = a if i == 0 else a * run
        a_ref[i] = a
        b_ref[i] = jnp.where(seen, ahead * inverse, 0.0)
        var_ref[i] = v
        whole_ref[0, i] = run
    carry_ref[0] = run

    info = enter_ref[1]
    run = jnp.ones(shape, F32)
    for i in reversed(range(CHUNK)):
        lead, spread, weight, inverse = element(*step_terms(i, chunks, first, q, r, decay_ref, seen_ref), r)
        d, seen, _ = step_terms(i, chunks, first, q, r, decay_ref, seen_ref)
        factor = 1.0 / (1.0 + spread * info)
        alpha = lead * factor
        info_ref[i] = info
        whole_ref[2, i] = run
        alpha_ref[i] = alpha
        beta_ref[i] = jnp.where(seen, d * inverse * factor, 0.0)
        info = weight + lead * alpha * info
        run = alpha * run
    carry_ref[1] = run

    along = jnp.ones((1, modes), F32)
    for c in range(chunks):
        enter_ref[0, c : c + 1, :] = along
        along = along * carry_ref[0, c : c + 1, :]
    along = jnp.ones((1, modes), F32)
    for c in reversed(range(chunks)):
        enter_ref[1, c : c + 1, :] = along
        along = along * carry_ref[1, c : c + 1, :]
    onward = enter_ref[0]
    back = enter_ref[1]
    for i in range(CHUNK):
        v = var_ref[i]
        keep = 1.0 / (1.0 + v * info_ref[i])
        lift = v * keep
        weight = whole_ref[0, i] * onward
        keep_ref[i] = keep
        lift_ref[i] = lift
        whole_ref[0, i] = weight
        whole_ref[1, i] = keep * weight
        whole_ref[2, i] = lift * (whole_ref[2, i] * back)
        put_rows(decay_ref, i, chunks, jnp.log(lift))
    unlanes(decay_ref, log_ref)


def means_kernel(parts, *refs):
    part_refs = refs[:parts]
    a_ref, b_ref, alpha_ref, beta_ref, keep_ref, lift_ref, carry_ref = refs[parts : parts + 7]
    coef_ref, mean_ref, smooth_ref, block_ref, enter_ref, strip_ref = refs[parts + 7 :]
    steps, modes = coef_ref.shape
    chunks = steps // CHUNK
    c = part_refs[0][...]
    for ref in part_refs[1:]:
        c = c + decode(ref)
    coef_ref[...] = c
    lanes(coef_ref, strip_ref)
    f = e = jnp.zeros((chunks, modes), F32)
    for i in range(CHUNK):
        f = a_ref[i] * f + b_ref[i] * chunk_rows(strip_ref, i, chunks)
        k = CHUNK - 1 - i
        e = alpha_ref[k] * e + beta_ref[k] * chunk_rows(strip_ref, k, chunks)
    mean_ref[0] = f
    mean_ref[1] = e
    f = e = jnp.zeros((1, modes), F32)
    for c in range(chunks):
        k = chunks - 1 - c
        enter_ref[0, c : c + 1, :] = f
        enter_ref[1, k : k + 1, :] = e
        f = mean_ref[0, c : c + 1, :] + carry_ref[0, c : c + 1, :] * f
        e = mean_ref[1, k : k + 1, :] + carry_ref[1, k : k + 1, :] * e
    block_ref[0:1, :] = f
    block_ref[1:2, :] = e
    f = enter_ref[0]
    e = enter_ref[1]
    for i in range(CHUNK):
        f = a_ref[i] * f + b_ref[i] * chunk_rows(strip_ref, i, chunks)
        mean_ref[i] = f
    for i in reversed(range(CHUNK)):
        smooth_ref[i] = keep_ref[i] * mean_ref[i] + lift_ref[i] * e
        e = alpha_ref[i] * e + beta_ref[i] * chunk_rows(strip_ref, i, chunks)


def finish_kernel(count, me_ref, prior_ref, whole_ref, edge_ref, blocks_ref, mean_ref, smooth_ref, out_mean_ref, out_smooth_ref, mean_strip_ref, smooth_strip_ref):
    steps, modes = out_mean_ref.shape
    chunks = steps // CHUNK
    me = me_ref[0]
    f = prior_ref[...]
    e = jnp.zeros((1, modes), F32)
    for j in range(count - 1):
        f = jnp.where(j < me, blocks_ref[j, 0:1, :] + edge_ref[0, j : j + 1, :] * f, f)
        k = count - 1 - j
        e = jnp.where(k > me, blocks_ref[k, 1:2, :] + edge_ref[1, k : k + 1, :] * e, e)
    f = jnp.broadcast_to(f, (chunks, modes))
    e = jnp.broadcast_to(e, (chunks, modes))
    for i in range(CHUNK):
        put_rows(mean_strip_ref, i, chunks, mean_ref[i] + whole_ref[0, i] * f)
        put_rows(smooth_strip_ref, i, chunks, smooth_ref[i] + whole_ref[1, i] * f + whole_ref[2, i] * e)
    unlanes(mean_strip_ref, out_mean_ref)
    unlanes(smooth_strip_ref, out_smooth_ref)


def encode(values, ref):
    steps = values.shape[0]
    top = jnp.max(jnp.abs(values), axis=0, keepdims=True)
    power = jnp.floor(jnp.log2(jnp.maximum(top, TINY))) + 1.0
    coded = jnp.floor(values * (jnp.exp2(-power) * STEPS16) + 0.5)
    ref[0:steps, :] = coded.astype(jnp.int32).astype(jnp.int16)
    power = jnp.broadcast_to(power, (PAD, power.shape[1]))
    ref[steps : steps + PAD, :] = power.astype(jnp.int32).astype(jnp.int16)


def decode(ref):
    steps = ref.shape[0] - PAD
    power = ref[steps : steps + PAD, :].astype(jnp.int32).astype(F32)[0:1, :]
    return ref[0:steps, :].astype(jnp.int32).astype(F32) * (jnp.exp2(power) * (1.0 / STEPS16))


def project_kernel(held, at_ref, slab_ref, basis_ref, own_ref, *refs):
    owners = at_ref.shape[0] - 1
    coded_refs = refs[: owners - 1]
    basis_area, sum_area, basis_sems, *refs = refs[owners - 1 :]
    slab_area = slab_ref if held else refs[0]
    count = slab_ref.shape[0]
    modes = own_ref.shape[1]
    copies = []
    for g in range(count):
        pair = [pltpu.make_async_copy(basis_ref.at[at_ref[0] + g], basis_area.at[g], basis_sems.at[g])]
        if not held:
            pair.append(pltpu.make_async_copy(slab_ref.at[g], slab_area.at[g], refs[1].at[g]))
        copies.append(pair)
    for pair in copies:
        for copy in pair:
            copy.start()
    for g in range(count):
        for copy in copies[g]:
            copy.wait()
        for turn in range(owners):
            columns = pl.ds(pl.multiple_of(at_ref[1 + turn] * modes, LANES), modes)
            term = jnp.dot(slab_area[g], basis_area[g, :, columns], preferred_element_type=F32)
            sum_area[turn] = term if g == 0 else sum_area[turn] + term
    own_ref[...] = sum_area[0]
    for turn in range(1, owners):
        encode(sum_area[turn], coded_refs[turn - 1])


def project(slabs, basis, first, owners, modes, held=False):
    count, steps, cells = slabs.shape
    others = len(owners) - 1
    own, *coded = pl.pallas_call(
        functools.partial(project_kernel, held),
        in_specs=[
            pl.BlockSpec(memory_space=pltpu.SMEM),
            pl.BlockSpec(memory_space=pltpu.VMEM if held else pl.ANY),
            pl.BlockSpec(memory_space=pl.ANY),
        ],
        out_specs=[pl.BlockSpec(memory_space=pltpu.VMEM)] * (1 + others),
        out_shape=[jax.ShapeDtypeStruct((steps, modes), F32)]
        + [jax.ShapeDtypeStruct((steps + PAD, modes), jnp.int16)] * others,
        scratch_shapes=[
            pltpu.VMEM((count,) + basis.shape[1:], basis.dtype),
            pltpu.VMEM((1 + others, steps, modes), F32),
            pltpu.SemaphoreType.DMA((count,)),
        ]
        + ([] if held else [pltpu.VMEM(slabs.shape, slabs.dtype), pltpu.SemaphoreType.DMA((count,))]),
        compiler_params=pltpu.CompilerParams(vmem_limit_bytes=(36 if held else 60) * LIMIT // 16),
        cost_estimate=pl.CostEstimate(
            flops=2 * count * steps * cells * modes * (1 + others),
            bytes_accessed=2 * count * cells * (steps + modes * (1 + others)) + 4 * steps * modes,
            transcendentals=0,
        ),
    )(jnp.stack([first] + owners), slabs, basis)
    return own, coded


def add_kernel(own_ref, coded_ref, out_ref):
    out_ref[...] = own_ref[...] + decode(coded_ref)


def fold_kernel(own_ref, *refs):
    total = own_ref[...]
    for ref in refs[:-1]:
        total = total + decode(ref)
    encode(total, refs[-1])


def call(kernel, inputs, outputs, scratch, flops):
    smem = pl.BlockSpec(memory_space=pltpu.SMEM)
    vmem = pl.BlockSpec(memory_space=pltpu.VMEM)
    moved = sum(4 * x.size for x in inputs) + sum(4 * x.size for x in outputs)
    return pl.pallas_call(
        kernel,
        in_specs=[smem if x.dtype == jnp.int32 else vmem for x in inputs],
        out_specs=[vmem] * len(outputs),
        out_shape=outputs,
        scratch_shapes=scratch,
        compiler_params=pltpu.CompilerParams(vmem_limit_bytes=LIMIT),
        cost_estimate=pl.CostEstimate(flops=flops, bytes_accessed=moved, transcendentals=0),
    )(*inputs)


def swap_halves(block, axis):
    half = lax.axis_size(axis) // 2
    return lax.ppermute(block, axis, [(i, (i + half) % (2 * half)) for i in range(2 * half)])


def send_along(term, axis, turn):
    count = lax.axis_size(axis)
    return lax.ppermute(term, axis, [(i, (i + turn) % count) for i in range(count)])


def body(observations, pod_basis, decay, step_mask, process_var, obs_var, prior_mean, prior_var):
    tm_count = lax.axis_size("tm")
    space_count = lax.axis_size("space")
    steps, modes = decay.shape
    chunks = steps // CHUNK
    rank = lax.axis_index("tm").astype(jnp.int32)
    me = rank.reshape(1)
    side = lax.axis_index("space").astype(jnp.int32)
    shape = functools.partial(jax.ShapeDtypeStruct, dtype=F32)
    area = pltpu.VMEM
    group = tm_count // 2
    groups = [[half * group + i for i in range(group)] for half in range(2)]
    half = rank // group

    seen = jnp.broadcast_to(step_mask.astype(F32)[:, None], (steps, modes))
    q, r = process_var[None, :], obs_var[None, :]
    flat = (chunks, modes)
    deep = (CHUNK, chunks, modes)
    strips = area((modes // LANES, steps, LANES), F32)
    slabs = observations.reshape(2, group, steps, observations.shape[3])
    basis = pod_basis.reshape(tm_count, -1, pod_basis.shape[3])
    first = half * group
    owners = [lax.rem(side + turn, space_count) for turn in range(space_count)]
    far = lax.dynamic_index_in_dim(slabs, 1 - half, 0, keepdims=False)
    far, q = lax.optimization_barrier((far, q))
    far = lax.all_to_all(far, "tm", 0, 0, axis_index_groups=groups, tiled=True)
    chunk_totals, block_totals = call(
        totals_kernel, (me, decay, seen, q, r), [shape((3,) + flat), shape((3, modes))], [strips] * 2, 40 * steps * modes
    )
    block_totals, own_half = lax.optimization_barrier((block_totals, half))
    near = lax.dynamic_index_in_dim(slabs, own_half, 0, keepdims=False)
    blocks = gather_near(block_totals, "tm")
    far, near, blocks = lax.optimization_barrier((far, near, blocks))
    near = lax.all_to_all(near, "tm", 0, 0, axis_index_groups=groups, tiled=True)

    own, theirs = project(far, basis, first, owners, modes)
    arriving = [send_along(term, "space", turn + 1) for turn, term in enumerate(theirs)]
    coded = jax.ShapeDtypeStruct((steps + PAD, modes), jnp.int16)
    (crossing,) = call(fold_kernel, (own, *arriving), [coded], [], 8 * steps * modes)
    near, crossing = lax.optimization_barrier((near, crossing))
    crossing = swap_halves(crossing, "tm")
    rest = gather_far(blocks, "tm")

    own, theirs = project(near, basis, first, owners, modes, True)
    parts = [send_along(term, "space", turn + 1) for turn, term in enumerate(theirs)]
    own, chunk_totals, rest = lax.optimization_barrier((own, chunk_totals, rest))
    blocks = jnp.concatenate([blocks] + rest, 0)
    (own,) = call(add_kernel, (own, crossing), [shape((steps, modes))], [], EARLY)
    parts.insert(0, own)
    *maps, whole, carry, edge, log_variance = call(
        functools.partial(gains_kernel, tm_count),
        (me, decay, seen, q, r, prior_var[None, :], chunk_totals, blocks),
        [shape(deep)] * 6 + [shape((3,) + deep), shape((2,) + flat), shape((2, tm_count, modes)), shape((steps, modes))],
        [area((2,) + flat, F32), area(deep, F32), area(deep, F32), strips, strips],
        80 * steps * modes,
    )

    coefficients, mean, smooth, ends = call(
        functools.partial(means_kernel, len(parts)),
        (*parts, *maps, carry),
        [shape((steps, modes)), shape(deep), shape(deep), shape((2, modes))],
        [area((2,) + flat, F32), strips],
        12 * steps * modes,
    )
    ends = jnp.broadcast_to(ends[None], (tm_count,) + ends.shape)
    ends = lax.all_to_all(ends, "tm", 0, 0, tiled=True)
    filtered, smoothed = call(
        functools.partial(finish_kernel, tm_count),
        (me, prior_mean[None, :], whole, edge, ends, mean, smooth),
        [shape((steps, modes))] * 2,
        [strips, strips],
        8 * steps * modes,
    )
    return coefficients, filtered, smoothed, log_variance


def solution(mesh):
    return jax.shard_map(
        body,
        mesh=mesh,
        in_specs=(
            P(None, "tm", "space", None),
            P(None, "space", None, None),
            P("tm", "space"),
            P("tm"),
            P("space"),
            P("space"),
            P("space"),
            P("space"),
        ),
        out_specs=(P("tm", "space"), P("tm", "space"), P("tm", "space"), P("tm", "space")),
        check_vma=False,
    )
```

```python
import functools

import jax
import jax.numpy as jnp
from jax import lax
from jax.experimental import pallas as pl
from jax.experimental.pallas import tpu as pltpu
from jax.sharding import PartitionSpec as P

CHUNK = 16
LANES = 128
PAD = 16
STEPS16 = 32512.0
TINY = 1e-30
EARLY = 1 << 34
F32 = jnp.float32
LIMIT = 16 * 1024 * 1024


def swap(block, axis, turn):
    return lax.ppermute(block, axis, [(i, i ^ turn) for i in range(lax.axis_size(axis))])


def inner_size(count):
    group = 1
    while group * group < count:
        group *= 2
    return group if count % group == 0 else count


def gather_near(rows, axis):
    return [rows] + [swap(rows, axis, turn) for turn in range(1, inner_size(lax.axis_size(axis)))]


def gather_far(near, axis):
    count = lax.axis_size(axis)
    return [swap(near, axis, turn) for turn in range(near.shape[0], count, near.shape[0])]


def lanes(ref, strip_ref):
    for m in range(strip_ref.shape[0]):
        strip_ref[m] = ref[:, m * LANES : (m + 1) * LANES]


def unlanes(strip_ref, ref):
    for m in range(strip_ref.shape[0]):
        ref[:, m * LANES : (m + 1) * LANES] = strip_ref[m]


def chunk_rows(strip_ref, i, chunks):
    rows = pl.ds(i, chunks, stride=CHUNK)
    return jnp.concatenate([strip_ref[m, rows, :] for m in range(strip_ref.shape[0])], 1)


def put_rows(strip_ref, i, chunks, value):
    rows = pl.ds(i, chunks, stride=CHUNK)
    for m in range(strip_ref.shape[0]):
        strip_ref[m, rows, :] = value[:, m * LANES : (m + 1) * LANES]


def opened(me_ref, shape):
    rows = lax.broadcasted_iota(jnp.int32, shape, 0)
    return jnp.logical_and(rows == 0, me_ref[0] == 0)


def step_terms(i, chunks, first, q, r, decay_ref, seen_ref):
    d = chunk_rows(decay_ref, i, chunks)
    seen = chunk_rows(seen_ref, i, chunks) > 0.5
    base = q
    if i == 0:
        d = jnp.where(first, 1.0, d)
        base = jnp.where(first, 0.0, q)
    return d, seen, base


def element(d, seen, base, r):
    inverse = 1.0 / (base + r)
    retain = jnp.where(seen, r * inverse, 1.0)
    return retain * d, retain * base, jnp.where(seen, d * d * inverse, 0.0), inverse


def join(early, late):
    lead, spread, weight = early
    lead_late, spread_late, weight_late = late
    factor = 1.0 / (1.0 + spread * weight_late)
    return (
        lead_late * factor * lead,
        lead_late * lead_late * factor * spread + spread_late,
        lead * lead * factor * weight_late + weight,
    )


def totals_kernel(me_ref, decay_in, seen_in, q_ref, r_ref, chunk_ref, block_ref, decay_ref, seen_ref):
    steps, modes = decay_in.shape
    lanes(decay_in, decay_ref)
    lanes(seen_in, seen_ref)
    chunks = steps // CHUNK
    shape = (chunks, modes)
    q = jnp.broadcast_to(q_ref[...], shape)
    r = jnp.broadcast_to(r_ref[...], shape)
    first = opened(me_ref, shape)
    total = None
    for i in range(CHUNK):
        step = element(*step_terms(i, chunks, first, q, r, decay_ref, seen_ref), r)[:3]
        total = step if i == 0 else join(total, step)
    for k in range(3):
        chunk_ref[k] = total[k]
    total = tuple(chunk_ref[k, 0:1, :] for k in range(3))
    for c in range(1, chunks):
        total = join(total, tuple(chunk_ref[k, c : c + 1, :] for k in range(3)))
    for k in range(3):
        block_ref[k : k + 1, :] = total[k]


def gains_kernel(
    count, me_ref, decay_in, seen_in, q_ref, r_ref, prior_ref, chunk_ref, blocks_ref,
    a_ref, b_ref, alpha_ref, beta_ref, keep_ref, lift_ref, whole_ref, carry_ref, edge_ref, log_ref,
    enter_ref, var_ref, info_ref, decay_ref, seen_ref,
):
    steps, modes = decay_in.shape
    lanes(decay_in, decay_ref)
    lanes(seen_in, seen_ref)
    chunks = steps // CHUNK
    shape = (chunks, modes)
    me = me_ref[0]
    q = jnp.broadcast_to(q_ref[...], shape)
    r = jnp.broadcast_to(r_ref[...], shape)
    first = opened(me_ref, shape)

    v = prior_ref[...]
    mine = v
    for j in range(count):
        mine = jnp.where(j == me, v, mine)
        at = lax.bitwise_xor(me, j)
        lead, spread, weight = (blocks_ref[at, k : k + 1, :] for k in range(3))
        along = lead / (1.0 + weight * v)
        edge_ref[0, j : j + 1, :] = along
        v = spread + lead * along * v
    v = mine
    for c in range(chunks):
        enter_ref[0, c : c + 1, :] = v
        lead, spread, weight = (chunk_ref[k, c : c + 1, :] for k in range(3))
        v = spread + lead * lead * v / (1.0 + weight * v)

    info = jnp.zeros((1, modes), F32)
    mine = info
    for j in reversed(range(count)):
        mine = jnp.where(j == me, info, mine)
        at = lax.bitwise_xor(me, j)
        lead, spread, weight = (blocks_ref[at, k : k + 1, :] for k in range(3))
        along = lead / (1.0 + spread * info)
        edge_ref[1, j : j + 1, :] = along
        info = weight + lead * along * info
    info = mine
    for c in reversed(range(chunks)):
        enter_ref[1, c : c + 1, :] = info
        lead, spread, weight = (chunk_ref[k, c : c + 1, :] for k in range(3))
        info = weight + lead * lead * info / (1.0 + spread * info)

    v = enter_ref[0]
    run = None
    for i in range(CHUNK):
        d, seen, base = step_terms(i, chunks, first, q, r, decay_ref, seen_ref)
        ahead = d * d * v + base
        inverse = 1.0 / (ahead + r)
        retain = jnp.where(seen, r * inverse, 1.0)
        v = retain * ahead
        a = retain * d
        run = a if i == 0 else a * run
        a_ref[i] = a
        b_ref[i] = jnp.where(seen, ahead * inverse, 0.0)
        var_ref[i] = v
        whole_ref[0, i] = run
    carry_ref[0] = run

    info = enter_ref[1]
    run = jnp.ones(shape, F32)
    for i in reversed(range(CHUNK)):
        lead, spread, weight, inverse = element(*step_terms(i, chunks, first, q, r, decay_ref, seen_ref), r)
        d, seen, _ = step_terms(i, chunks, first, q, r, decay_ref, seen_ref)
        factor = 1.0 / (1.0 + spread * info)
        alpha = lead * factor
        info_ref[i] = info
        whole_ref[2, i] = run
        alpha_ref[i] = alpha
        beta_ref[i] = jnp.where(seen, d * inverse * factor, 0.0)
        info = weight + lead * alpha * info
        run = alpha * run
    carry_ref[1] = run

    along = jnp.ones((1, modes), F32)
    for c in range(chunks):
        enter_ref[0, c : c + 1, :] = along
        along = along * carry_ref[0, c : c + 1, :]
    along = jnp.ones((1, modes), F32)
    for c in reversed(range(chunks)):
        enter_ref[1, c : c + 1, :] = along
        along = along * carry_ref[1, c : c + 1, :]
    onward = enter_ref[0]
    back = enter_ref[1]
    for i in range(CHUNK):
        v = var_ref[i]
        keep = 1.0 / (1.0 + v * info_ref[i])
        lift = v * keep
        weight = whole_ref[0, i] * onward
        keep_ref[i] = keep
        lift_ref[i] = lift
        whole_ref[0, i] = weight
        whole_ref[1, i] = keep * weight
        whole_ref[2, i] = lift * (whole_ref[2, i] * back)
        put_rows(decay_ref, i, chunks, jnp.log(lift))
    unlanes(decay_ref, log_ref)


def means_kernel(parts, *refs):
    part_refs = refs[:parts]
    a_ref, b_ref, alpha_ref, beta_ref, keep_ref, lift_ref, carry_ref = refs[parts : parts + 7]
    coef_ref, mean_ref, smooth_ref, block_ref, enter_ref, strip_ref = refs[parts + 7 :]
    steps, modes = coef_ref.shape
    chunks = steps // CHUNK
    c = part_refs[0][...]
    for ref in part_refs[1:]:
        c = c + decode(ref)
    coef_ref[...] = c
    lanes(coef_ref, strip_ref)
    f = e = jnp.zeros((chunks, modes), F32)
    for i in range(CHUNK):
        f = a_ref[i] * f + b_ref[i] * chunk_rows(strip_ref, i, chunks)
        k = CHUNK - 1 - i
        e = alpha_ref[k] * e + beta_ref[k] * chunk_rows(strip_ref, k, chunks)
    mean_ref[0] = f
    mean_ref[1] = e
    f = e = jnp.zeros((1, modes), F32)
    for c in range(chunks):
        k = chunks - 1 - c
        enter_ref[0, c : c + 1, :] = f
        enter_ref[1, k : k + 1, :] = e
        f = mean_ref[0, c : c + 1, :] + carry_ref[0, c : c + 1, :] * f
        e = mean_ref[1, k : k + 1, :] + carry_ref[1, k : k + 1, :] * e
    block_ref[0:1, :] = f
    block_ref[1:2, :] = e
    f = enter_ref[0]
    e = enter_ref[1]
    for i in range(CHUNK):
        f = a_ref[i] * f + b_ref[i] * chunk_rows(strip_ref, i, chunks)
        mean_ref[i] = f
    for i in reversed(range(CHUNK)):
        smooth_ref[i] = keep_ref[i] * mean_ref[i] + lift_ref[i] * e
        e = alpha_ref[i] * e + beta_ref[i] * chunk_rows(strip_ref, i, chunks)


def finish_kernel(count, me_ref, prior_ref, whole_ref, edge_ref, blocks_ref, mean_ref, smooth_ref, out_mean_ref, out_smooth_ref, mean_strip_ref, smooth_strip_ref):
    steps, modes = out_mean_ref.shape
    chunks = steps // CHUNK
    me = me_ref[0]
    f = prior_ref[...]
    e = jnp.zeros((1, modes), F32)
    for j in range(count - 1):
        f = jnp.where(j < me, blocks_ref[j, 0:1, :] + edge_ref[0, j : j + 1, :] * f, f)
        k = count - 1 - j
        e = jnp.where(k > me, blocks_ref[k, 1:2, :] + edge_ref[1, k : k + 1, :] * e, e)
    f = jnp.broadcast_to(f, (chunks, modes))
    e = jnp.broadcast_to(e, (chunks, modes))
    for i in range(CHUNK):
        put_rows(mean_strip_ref, i, chunks, mean_ref[i] + whole_ref[0, i] * f)
        put_rows(smooth_strip_ref, i, chunks, smooth_ref[i] + whole_ref[1, i] * f + whole_ref[2, i] * e)
    unlanes(mean_strip_ref, out_mean_ref)
    unlanes(smooth_strip_ref, out_smooth_ref)


def encode(values, ref):
    steps = values.shape[0]
    top = jnp.max(jnp.abs(values), axis=0, keepdims=True)
    power = jnp.floor(jnp.log2(jnp.maximum(top, TINY))) + 1.0
    coded = jnp.floor(values * (jnp.exp2(-power) * STEPS16) + 0.5)
    ref[0:steps, :] = coded.astype(jnp.int32).astype(jnp.int16)
    power = jnp.broadcast_to(power, (PAD, power.shape[1]))
    ref[steps : steps + PAD, :] = power.astype(jnp.int32).astype(jnp.int16)


def decode(ref):
    steps = ref.shape[0] - PAD
    power = ref[steps : steps + PAD, :].astype(jnp.int32).astype(F32)[0:1, :]
    return ref[0:steps, :].astype(jnp.int32).astype(F32) * (jnp.exp2(power) * (1.0 / STEPS16))


def project_kernel(held, at_ref, slab_ref, basis_ref, own_ref, *refs):
    owners = at_ref.shape[0] - 1
    coded_refs = refs[: owners - 1]
    basis_area, sum_area, basis_sems, *refs = refs[owners - 1 :]
    slab_area = slab_ref if held else refs[0]
    count = slab_ref.shape[0]
    modes = own_ref.shape[1]
    copies = []
    for g in range(count):
        pair = [pltpu.make_async_copy(basis_ref.at[at_ref[0] + g], basis_area.at[g], basis_sems.at[g])]
        if not held:
            pair.append(pltpu.make_async_copy(slab_ref.at[g], slab_area.at[g], refs[1].at[g]))
        copies.append(pair)
    for pair in copies:
        for copy in pair:
            copy.start()
    for g in range(count):
        for copy in copies[g]:
            copy.wait()
        for turn in range(owners):
            columns = pl.ds(pl.multiple_of(at_ref[1 + turn] * modes, LANES), modes)
            term = jnp.dot(slab_area[g], basis_area[g, :, columns], preferred_element_type=F32)
            sum_area[turn] = term if g == 0 else sum_area[turn] + term
    own_ref[...] = sum_area[0]
    for turn in range(1, owners):
        encode(sum_area[turn], coded_refs[turn - 1])


def project(slabs, basis, first, owners, modes, held=False):
    count, steps, cells = slabs.shape
    others = len(owners) - 1
    own, *coded = pl.pallas_call(
        functools.partial(project_kernel, held),
        in_specs=[
            pl.BlockSpec(memory_space=pltpu.SMEM),
            pl.BlockSpec(memory_space=pltpu.VMEM if held else pl.ANY),
            pl.BlockSpec(memory_space=pl.ANY),
        ],
        out_specs=[pl.BlockSpec(memory_space=pltpu.VMEM)] * (1 + others),
        out_shape=[jax.ShapeDtypeStruct((steps, modes), F32)]
        + [jax.ShapeDtypeStruct((steps + PAD, modes), jnp.int16)] * others,
        scratch_shapes=[
            pltpu.VMEM((count,) + basis.shape[1:], basis.dtype),
            pltpu.VMEM((1 + others, steps, modes), F32),
            pltpu.SemaphoreType.DMA((count,)),
        ]
        + ([] if held else [pltpu.VMEM(slabs.shape, slabs.dtype), pltpu.SemaphoreType.DMA((count,))]),
        compiler_params=pltpu.CompilerParams(vmem_limit_bytes=(36 if held else 60) * LIMIT // 16),
        cost_estimate=pl.CostEstimate(
            flops=2 * count * steps * cells * modes * (1 + others),
            bytes_accessed=2 * count * cells * (steps + modes * (1 + others)) + 4 * steps * modes,
            transcendentals=0,
        ),
    )(jnp.stack([first] + owners), slabs, basis)
    return own, coded


def add_kernel(own_ref, coded_ref, out_ref):
    out_ref[...] = own_ref[...] + decode(coded_ref)


def fold_kernel(own_ref, *refs):
    total = own_ref[...]
    for ref in refs[:-1]:
        total = total + decode(ref)
    encode(total, refs[-1])


def call(kernel, inputs, outputs, scratch, flops):
    smem = pl.BlockSpec(memory_space=pltpu.SMEM)
    vmem = pl.BlockSpec(memory_space=pltpu.VMEM)
    moved = sum(4 * x.size for x in inputs) + sum(4 * x.size for x in outputs)
    return pl.pallas_call(
        kernel,
        in_specs=[smem if x.dtype == jnp.int32 else vmem for x in inputs],
        out_specs=[vmem] * len(outputs),
        out_shape=outputs,
        scratch_shapes=scratch,
        compiler_params=pltpu.CompilerParams(vmem_limit_bytes=LIMIT),
        cost_estimate=pl.CostEstimate(flops=flops, bytes_accessed=moved, transcendentals=0),
    )(*inputs)


def swap_halves(block, axis):
    half = lax.axis_size(axis) // 2
    return lax.ppermute(block, axis, [(i, (i + half) % (2 * half)) for i in range(2 * half)])


def send_along(term, axis, turn):
    count = lax.axis_size(axis)
    return lax.ppermute(term, axis, [(i, (i + turn) % count) for i in range(count)])


def body(observations, pod_basis, decay, step_mask, process_var, obs_var, prior_mean, prior_var):
    tm_count = lax.axis_size("tm")
    space_count = lax.axis_size("space")
    steps, modes = decay.shape
    chunks = steps // CHUNK
    rank = lax.axis_index("tm").astype(jnp.int32)
    me = rank.reshape(1)
    side = lax.axis_index("space").astype(jnp.int32)
    shape = functools.partial(jax.ShapeDtypeStruct, dtype=F32)
    area = pltpu.VMEM
    group = tm_count // 2
    groups = [[half * group + i for i in range(group)] for half in range(2)]
    half = rank // group

    seen = jnp.broadcast_to(step_mask.astype(F32)[:, None], (steps, modes))
    q, r = process_var[None, :], obs_var[None, :]
    flat = (chunks, modes)
    deep = (CHUNK, chunks, modes)
    strips = area((modes // LANES, steps, LANES), F32)
    slabs = observations.reshape(2, group, steps, observations.shape[3])
    basis = pod_basis.reshape(tm_count, -1, pod_basis.shape[3])
    first = half * group
    owners = [lax.rem(side + turn, space_count) for turn in range(space_count)]
    far = lax.dynamic_index_in_dim(slabs, 1 - half, 0, keepdims=False)
    far, q = lax.optimization_barrier((far, q))
    far = lax.all_to_all(far, "tm", 0, 0, axis_index_groups=groups, tiled=True)
    chunk_totals, block_totals = call(
        totals_kernel, (me, decay, seen, q, r), [shape((3,) + flat), shape((3, modes))], [strips] * 2, 40 * steps * modes
    )
    block_totals, own_half = lax.optimization_barrier((block_totals, half))
    near = lax.dynamic_index_in_dim(slabs, own_half, 0, keepdims=False)
    blocks = jnp.stack(gather_near(block_totals, "tm"))
    far, near, blocks = lax.optimization_barrier((far, near, blocks))
    near = lax.all_to_all(near, "tm", 0, 0, axis_index_groups=groups, tiled=True)

    own, theirs = project(far, basis, first, owners, modes)
    arriving = [send_along(term, "space", turn + 1) for turn, term in enumerate(theirs)]
    coded = jax.ShapeDtypeStruct((steps + PAD, modes), jnp.int16)
    (crossing,) = call(fold_kernel, (own, *arriving), [coded], [], 8 * steps * modes)
    near, crossing = lax.optimization_barrier((near, crossing))
    crossing = swap_halves(crossing, "tm")
    rest = gather_far(blocks, "tm")

    own, theirs = project(near, basis, first, owners, modes, True)
    parts = [send_along(term, "space", turn + 1) for turn, term in enumerate(theirs)]
    own, chunk_totals, rest = lax.optimization_barrier((own, chunk_totals, rest))
    blocks = jnp.concatenate([blocks] + rest, 0)
    (own,) = call(add_kernel, (own, crossing), [shape((steps, modes))], [], EARLY)
    parts.insert(0, own)
    *maps, whole, carry, edge, log_variance = call(
        functools.partial(gains_kernel, tm_count),
        (me, decay, seen, q, r, prior_var[None, :], chunk_totals, blocks),
        [shape(deep)] * 6 + [shape((3,) + deep), shape((2,) + flat), shape((2, tm_count, modes)), shape((steps, modes))],
        [area((2,) + flat, F32), area(deep, F32), area(deep, F32), strips, strips],
        80 * steps * modes,
    )

    coefficients, mean, smooth, ends = call(
        functools.partial(means_kernel, len(parts)),
        (*parts, *maps, carry),
        [shape((steps, modes)), shape(deep), shape(deep), shape((2, modes))],
        [area((2,) + flat, F32), strips],
        12 * steps * modes,
    )
    ends = jnp.broadcast_to(ends[None], (tm_count,) + ends.shape)
    ends = lax.all_to_all(ends, "tm", 0, 0, tiled=True)
    filtered, smoothed = call(
        functools.partial(finish_kernel, tm_count),
        (me, prior_mean[None, :], whole, edge, ends, mean, smooth),
        [shape((steps, modes))] * 2,
        [strips, strips],
        8 * steps * modes,
    )
    return coefficients, filtered, smoothed, log_variance


def solution(mesh):
    return jax.shard_map(
        body,
        mesh=mesh,
        in_specs=(
            P(None, "tm", "space", None),
            P(None, "space", None, None),
            P("tm", "space"),
            P("tm"),
            P("space"),
            P("space"),
            P("space"),
            P("space"),
        ),
        out_specs=(P("tm", "space"), P("tm", "space"), P("tm", "space"), P("tm", "space")),
        check_vma=False,
    )
```

```python
import functools

import jax
import jax.numpy as jnp
from jax import lax
from jax.experimental import pallas as pl
from jax.experimental.pallas import tpu as pltpu
from jax.sharding import PartitionSpec as P

CHUNK = 16
LANES = 128
PAD = 16
STEPS16 = 32512.0
TINY = 1e-30
EARLY = 1 << 34
F32 = jnp.float32
LIMIT = 16 * 1024 * 1024


def swap(block, axis, turn):
    return lax.ppermute(block, axis, [(i, i ^ turn) for i in range(lax.axis_size(axis))])


def inner_size(count):
    group = 1
    while group * group < count:
        group *= 2
    return group if count % group == 0 else count


def gather_near(rows, axis):
    return [rows] + [swap(rows, axis, turn) for turn in range(1, inner_size(lax.axis_size(axis)))]


def gather_far(near, axis):
    count = lax.axis_size(axis)
    return [swap(near, axis, turn) for turn in range(near.shape[0], count, near.shape[0])]


def lanes(ref, strip_ref):
    for m in range(strip_ref.shape[0]):
        strip_ref[m] = ref[:, m * LANES : (m + 1) * LANES]


def unlanes(strip_ref, ref):
    for m in range(strip_ref.shape[0]):
        ref[:, m * LANES : (m + 1) * LANES] = strip_ref[m]


def chunk_rows(strip_ref, i, chunks):
    rows = pl.ds(i, chunks, stride=CHUNK)
    return jnp.concatenate([strip_ref[m, rows, :] for m in range(strip_ref.shape[0])], 1)


def put_rows(strip_ref, i, chunks, value):
    rows = pl.ds(i, chunks, stride=CHUNK)
    for m in range(strip_ref.shape[0]):
        strip_ref[m, rows, :] = value[:, m * LANES : (m + 1) * LANES]


def opened(me_ref, shape):
    rows = lax.broadcasted_iota(jnp.int32, shape, 0)
    return jnp.logical_and(rows == 0, me_ref[0] == 0)


def step_terms(i, chunks, first, q, r, decay_ref, seen_ref):
    d = chunk_rows(decay_ref, i, chunks)
    seen = chunk_rows(seen_ref, i, chunks) > 0.5
    base = q
    if i == 0:
        d = jnp.where(first, 1.0, d)
        base = jnp.where(first, 0.0, q)
    return d, seen, base


def element(d, seen, base, r):
    inverse = 1.0 / (base + r)
    retain = jnp.where(seen, r * inverse, 1.0)
    return retain * d, retain * base, jnp.where(seen, d * d * inverse, 0.0), inverse


def join(early, late):
    lead, spread, weight = early
    lead_late, spread_late, weight_late = late
    factor = 1.0 / (1.0 + spread * weight_late)
    return (
        lead_late * factor * lead,
        lead_late * lead_late * factor * spread + spread_late,
        lead * lead * factor * weight_late + weight,
    )


def totals_kernel(me_ref, decay_in, seen_in, q_ref, r_ref, chunk_ref, block_ref, decay_ref, seen_ref):
    steps, modes = decay_in.shape
    lanes(decay_in, decay_ref)
    lanes(seen_in, seen_ref)
    chunks = steps // CHUNK
    shape = (chunks, modes)
    q = jnp.broadcast_to(q_ref[...], shape)
    r = jnp.broadcast_to(r_ref[...], shape)
    first = opened(me_ref, shape)
    total = None
    for i in range(CHUNK):
        step = element(*step_terms(i, chunks, first, q, r, decay_ref, seen_ref), r)[:3]
        total = step if i == 0 else join(total, step)
    for k in range(3):
        chunk_ref[k] = total[k]
    total = tuple(chunk_ref[k, 0:1, :] for k in range(3))
    for c in range(1, chunks):
        total = join(total, tuple(chunk_ref[k, c : c + 1, :] for k in range(3)))
    for k in range(3):
        block_ref[k : k + 1, :] = total[k]


def gains_kernel(
    count, me_ref, decay_in, seen_in, q_ref, r_ref, prior_ref, chunk_ref, blocks_ref,
    a_ref, b_ref, alpha_ref, beta_ref, keep_ref, lift_ref, whole_ref, carry_ref, edge_ref, log_ref,
    enter_ref, var_ref, info_ref, decay_ref, seen_ref,
):
    steps, modes = decay_in.shape
    lanes(decay_in, decay_ref)
    lanes(seen_in, seen_ref)
    chunks = steps // CHUNK
    shape = (chunks, modes)
    me = me_ref[0]
    q = jnp.broadcast_to(q_ref[...], shape)
    r = jnp.broadcast_to(r_ref[...], shape)
    first = opened(me_ref, shape)

    v = prior_ref[...]
    mine = v
    for j in range(count):
        mine = jnp.where(j == me, v, mine)
        at = lax.bitwise_xor(me, j)
        lead, spread, weight = (blocks_ref[at, k : k + 1, :] for k in range(3))
        along = lead / (1.0 + weight * v)
        edge_ref[0, j : j + 1, :] = along
        v = spread + lead * along * v
    v = mine
    for c in range(chunks):
        enter_ref[0, c : c + 1, :] = v
        lead, spread, weight = (chunk_ref[k, c : c + 1, :] for k in range(3))
        v = spread + lead * lead * v / (1.0 + weight * v)

    info = jnp.zeros((1, modes), F32)
    mine = info
    for j in reversed(range(count)):
        mine = jnp.where(j == me, info, mine)
        at = lax.bitwise_xor(me, j)
        lead, spread, weight = (blocks_ref[at, k : k + 1, :] for k in range(3))
        along = lead / (1.0 + spread * info)
        edge_ref[1, j : j + 1, :] = along
        info = weight + lead * along * info
    info = mine
    for c in reversed(range(chunks)):
        enter_ref[1, c : c + 1, :] = info
        lead, spread, weight = (chunk_ref[k, c : c + 1, :] for k in range(3))
        info = weight + lead * lead * info / (1.0 + spread * info)

    v = enter_ref[0]
    run = None
    for i in range(CHUNK):
        d, seen, base = step_terms(i, chunks, first, q, r, decay_ref, seen_ref)
        ahead = d * d * v + base
        inverse = 1.0 / (ahead + r)
        retain = jnp.where(seen, r * inverse, 1.0)
        v = retain * ahead
        a = retain * d
        run = a if i == 0 else a * run
        a_ref[i] = a
        b_ref[i] = jnp.where(seen, ahead * inverse, 0.0)
        var_ref[i] = v
        whole_ref[0, i] = run
    carry_ref[0] = run

    info = enter_ref[1]
    run = jnp.ones(shape, F32)
    for i in reversed(range(CHUNK)):
        lead, spread, weight, inverse = element(*step_terms(i, chunks, first, q, r, decay_ref, seen_ref), r)
        d, seen, _ = step_terms(i, chunks, first, q, r, decay_ref, seen_ref)
        factor = 1.0 / (1.0 + spread * info)
        alpha = lead * factor
        info_ref[i] = info
        whole_ref[2, i] = run
        alpha_ref[i] = alpha
        beta_ref[i] = jnp.where(seen, d * inverse * factor, 0.0)
        info = weight + lead * alpha * info
        run = alpha * run
    carry_ref[1] = run

    along = jnp.ones((1, modes), F32)
    for c in range(chunks):
        enter_ref[0, c : c + 1, :] = along
        along = along * carry_ref[0, c : c + 1, :]
    along = jnp.ones((1, modes), F32)
    for c in reversed(range(chunks)):
        enter_ref[1, c : c + 1, :] = along
        along = along * carry_ref[1, c : c + 1, :]
    onward = enter_ref[0]
    back = enter_ref[1]
    for i in range(CHUNK):
        v = var_ref[i]
        keep = 1.0 / (1.0 + v * info_ref[i])
        lift = v * keep
        weight = whole_ref[0, i] * onward
        keep_ref[i] = keep
        lift_ref[i] = lift
        whole_ref[0, i] = weight
        whole_ref[1, i] = keep * weight
        whole_ref[2, i] = lift * (whole_ref[2, i] * back)
        put_rows(decay_ref, i, chunks, jnp.log(lift))
    unlanes(decay_ref, log_ref)


def means_kernel(parts, *refs):
    part_refs = refs[:parts]
    a_ref, b_ref, alpha_ref, beta_ref, keep_ref, lift_ref, carry_ref = refs[parts : parts + 7]
    coef_ref, mean_ref, smooth_ref, block_ref, enter_ref, strip_ref = refs[parts + 7 :]
    steps, modes = coef_ref.shape
    chunks = steps // CHUNK
    c = part_refs[0][...]
    for ref in part_refs[1:]:
        c = c + decode(ref)
    coef_ref[...] = c
    lanes(coef_ref, strip_ref)
    f = e = jnp.zeros((chunks, modes), F32)
    for i in range(CHUNK):
        f = a_ref[i] * f + b_ref[i] * chunk_rows(strip_ref, i, chunks)
        k = CHUNK - 1 - i
        e = alpha_ref[k] * e + beta_ref[k] * chunk_rows(strip_ref, k, chunks)
    mean_ref[0] = f
    mean_ref[1] = e
    f = e = jnp.zeros((1, modes), F32)
    for c in range(chunks):
        k = chunks - 1 - c
        enter_ref[0, c : c + 1, :] = f
        enter_ref[1, k : k + 1, :] = e
        f = mean_ref[0, c : c + 1, :] + carry_ref[0, c : c + 1, :] * f
        e = mean_ref[1, k : k + 1, :] + carry_ref[1, k : k + 1, :] * e
    block_ref[0:1, :] = f
    block_ref[1:2, :] = e
    f = enter_ref[0]
    e = enter_ref[1]
    for i in range(CHUNK):
        f = a_ref[i] * f + b_ref[i] * chunk_rows(strip_ref, i, chunks)
        mean_ref[i] = f
    for i in reversed(range(CHUNK)):
        smooth_ref[i] = keep_ref[i] * mean_ref[i] + lift_ref[i] * e
        e = alpha_ref[i] * e + beta_ref[i] * chunk_rows(strip_ref, i, chunks)


def finish_kernel(count, me_ref, prior_ref, whole_ref, edge_ref, blocks_ref, mean_ref, smooth_ref, out_mean_ref, out_smooth_ref, mean_strip_ref, smooth_strip_ref):
    steps, modes = out_mean_ref.shape
    chunks = steps // CHUNK
    me = me_ref[0]
    f = prior_ref[...]
    e = jnp.zeros((1, modes), F32)
    for j in range(count - 1):
        f = jnp.where(j < me, blocks_ref[j, 0:1, :] + edge_ref[0, j : j + 1, :] * f, f)
        k = count - 1 - j
        e = jnp.where(k > me, blocks_ref[k, 1:2, :] + edge_ref[1, k : k + 1, :] * e, e)
    f = jnp.broadcast_to(f, (chunks, modes))
    e = jnp.broadcast_to(e, (chunks, modes))
    for i in range(CHUNK):
        put_rows(mean_strip_ref, i, chunks, mean_ref[i] + whole_ref[0, i] * f)
        put_rows(smooth_strip_ref, i, chunks, smooth_ref[i] + whole_ref[1, i] * f + whole_ref[2, i] * e)
    unlanes(mean_strip_ref, out_mean_ref)
    unlanes(smooth_strip_ref, out_smooth_ref)


def encode(values, ref):
    steps = values.shape[0]
    top = jnp.max(jnp.abs(values), axis=0, keepdims=True)
    power = jnp.floor(jnp.log2(jnp.maximum(top, TINY))) + 1.0
    coded = jnp.floor(values * (jnp.exp2(-power) * STEPS16) + 0.5)
    ref[0:steps, :] = coded.astype(jnp.int32).astype(jnp.int16)
    power = jnp.broadcast_to(power, (PAD, power.shape[1]))
    ref[steps : steps + PAD, :] = power.astype(jnp.int32).astype(jnp.int16)


def decode(ref):
    steps = ref.shape[0] - PAD
    power = ref[steps : steps + PAD, :].astype(jnp.int32).astype(F32)[0:1, :]
    return ref[0:steps, :].astype(jnp.int32).astype(F32) * (jnp.exp2(power) * (1.0 / STEPS16))


def project_kernel(held, at_ref, slab_ref, basis_ref, own_ref, *refs):
    owners = at_ref.shape[0] - 1
    coded_refs = refs[: owners - 1]
    basis_area, sum_area, basis_sems, *refs = refs[owners - 1 :]
    slab_area = slab_ref if held else refs[0]
    count = slab_ref.shape[0]
    modes = own_ref.shape[1]
    copies = []
    for g in range(count):
        source = (g + count // 2) % count
        pair = [pltpu.make_async_copy(basis_ref.at[at_ref[0] + source], basis_area.at[g], basis_sems.at[g])]
        if not held:
            pair.append(pltpu.make_async_copy(slab_ref.at[g], slab_area.at[g], refs[1].at[g]))
        copies.append(pair)
    for pair in copies:
        for copy in pair:
            copy.start()
    for g in range(count):
        for copy in copies[g]:
            copy.wait()
        for turn in range(owners):
            columns = pl.ds(pl.multiple_of(at_ref[1 + turn] * modes, LANES), modes)
            term = jnp.dot(slab_area[g], basis_area[g, :, columns], preferred_element_type=F32)
            sum_area[turn] = term if g == 0 else sum_area[turn] + term
    own_ref[...] = sum_area[0]
    for turn in range(1, owners):
        encode(sum_area[turn], coded_refs[turn - 1])


def project(slabs, basis, first, owners, modes, held=False):
    count, steps, cells = slabs.shape
    others = len(owners) - 1
    own, *coded = pl.pallas_call(
        functools.partial(project_kernel, held),
        in_specs=[
            pl.BlockSpec(memory_space=pltpu.SMEM),
            pl.BlockSpec(memory_space=pltpu.VMEM if held else pl.ANY),
            pl.BlockSpec(memory_space=pl.ANY),
        ],
        out_specs=[pl.BlockSpec(memory_space=pltpu.VMEM)] * (1 + others),
        out_shape=[jax.ShapeDtypeStruct((steps, modes), F32)]
        + [jax.ShapeDtypeStruct((steps + PAD, modes), jnp.int16)] * others,
        scratch_shapes=[
            pltpu.VMEM((count,) + basis.shape[1:], basis.dtype),
            pltpu.VMEM((1 + others, steps, modes), F32),
            pltpu.SemaphoreType.DMA((count,)),
        ]
        + ([] if held else [pltpu.VMEM(slabs.shape, slabs.dtype), pltpu.SemaphoreType.DMA((count,))]),
        compiler_params=pltpu.CompilerParams(vmem_limit_bytes=(36 if held else 60) * LIMIT // 16),
        cost_estimate=pl.CostEstimate(
            flops=2 * count * steps * cells * modes * (1 + others),
            bytes_accessed=2 * count * cells * (steps + modes * (1 + others)) + 4 * steps * modes,
            transcendentals=0,
        ),
    )(jnp.stack([first] + owners), slabs, basis)
    return own, coded


def project_one_kernel(at_ref, slab_ref, basis_ref, out_ref, basis_area, sum_area, sems):
    count = slab_ref.shape[0]
    modes = out_ref.shape[1]
    columns = pl.ds(pl.multiple_of(at_ref[1] * modes, LANES), modes)
    copies = [
        pltpu.make_async_copy(basis_ref.at[at_ref[0] + g, :, columns], basis_area.at[g], sems.at[g])
        for g in range(count)
    ]
    for copy in copies:
        copy.start()
    for g in range(count):
        copies[g].wait()
        term = jnp.dot(slab_ref[g], basis_area[g], preferred_element_type=F32)
        sum_area[...] = term if g == 0 else sum_area[...] + term
    if out_ref.dtype == jnp.int16:
        encode(sum_area[...], out_ref)
    else:
        out_ref[...] = sum_area[...]


def project_one(slabs, basis, first, owner, modes, out):
    count, steps, cells = slabs.shape
    vmem = pl.BlockSpec(memory_space=pltpu.VMEM)
    return pl.pallas_call(
        project_one_kernel,
        in_specs=[pl.BlockSpec(memory_space=pltpu.SMEM), vmem, pl.BlockSpec(memory_space=pl.ANY)],
        out_specs=vmem,
        out_shape=out,
        scratch_shapes=[
            pltpu.VMEM((count, cells, modes), basis.dtype),
            pltpu.VMEM((steps, modes), F32),
            pltpu.SemaphoreType.DMA((count,)),
        ],
        compiler_params=pltpu.CompilerParams(vmem_limit_bytes=36 * LIMIT // 16),
        cost_estimate=pl.CostEstimate(
            flops=2 * count * steps * cells * modes,
            bytes_accessed=2 * count * cells * (steps + modes) + 4 * steps * modes,
            transcendentals=0,
        ),
    )(jnp.stack([first, owner]), slabs, basis)


def add_kernel(own_ref, early_ref, late_ref, out_ref):
    out_ref[...] = own_ref[...] + decode(early_ref) + decode(late_ref)


def fold_kernel(own_ref, *refs):
    total = own_ref[...]
    for ref in refs[:-1]:
        total = total + decode(ref)
    encode(total, refs[-1])


def call(kernel, inputs, outputs, scratch, flops):
    smem = pl.BlockSpec(memory_space=pltpu.SMEM)
    vmem = pl.BlockSpec(memory_space=pltpu.VMEM)
    moved = sum(4 * x.size for x in inputs) + sum(4 * x.size for x in outputs)
    return pl.pallas_call(
        kernel,
        in_specs=[smem if x.dtype == jnp.int32 else vmem for x in inputs],
        out_specs=[vmem] * len(outputs),
        out_shape=outputs,
        scratch_shapes=scratch,
        compiler_params=pltpu.CompilerParams(vmem_limit_bytes=LIMIT),
        cost_estimate=pl.CostEstimate(flops=flops, bytes_accessed=moved, transcendentals=0),
    )(*inputs)


def mirror(block, axis, inner):
    count = lax.axis_size(axis)
    quarter = count // 4
    places = [i for i in range(count) if (quarter <= i < 3 * quarter) == inner]
    return lax.ppermute(block, axis, [(i, i ^ (3 * quarter)) for i in places])


def send_along(term, axis, turn):
    count = lax.axis_size(axis)
    return lax.ppermute(term, axis, [(i, (i + turn) % count) for i in range(count)])


def body(observations, pod_basis, decay, step_mask, process_var, obs_var, prior_mean, prior_var):
    tm_count = lax.axis_size("tm")
    space_count = lax.axis_size("space")
    steps, modes = decay.shape
    chunks = steps // CHUNK
    rank = lax.axis_index("tm").astype(jnp.int32)
    me = rank.reshape(1)
    side = lax.axis_index("space").astype(jnp.int32)
    shape = functools.partial(jax.ShapeDtypeStruct, dtype=F32)
    area = pltpu.VMEM
    group = tm_count // 2
    groups = [[half * group + i for i in range(group)] for half in range(2)]
    half = rank // group

    seen = jnp.broadcast_to(step_mask.astype(F32)[:, None], (steps, modes))
    q, r = process_var[None, :], obs_var[None, :]
    flat = (chunks, modes)
    deep = (CHUNK, chunks, modes)
    strips = area((modes // LANES, steps, LANES), F32)
    slabs = observations.reshape(2, group, steps, observations.shape[3])
    basis = pod_basis.reshape(tm_count, -1, pod_basis.shape[3])
    first = half * group
    owners = [lax.rem(side + turn, space_count) for turn in range(space_count)]
    far = lax.dynamic_index_in_dim(slabs, 1 - half, 0, keepdims=False)
    far, q = lax.optimization_barrier((far, q))
    turned = [places[group // 2 :] + places[: group // 2] for places in groups]
    far = lax.all_to_all(far, "tm", 0, 0, axis_index_groups=turned, tiled=True)
    chunk_totals, block_totals = call(
        totals_kernel, (me, decay, seen, q, r), [shape((3,) + flat), shape((3, modes))], [strips] * 2, 40 * steps * modes
    )
    block_totals, own_half = lax.optimization_barrier((block_totals, half))
    near = lax.dynamic_index_in_dim(slabs, own_half, 0, keepdims=False)
    blocks = jnp.stack(gather_near(block_totals, "tm"))
    far, near, blocks = lax.optimization_barrier((far, near, blocks))
    near = lax.all_to_all(near, "tm", 0, 0, axis_index_groups=groups, tiled=True)

    own, theirs = project(far, basis, first, owners, modes)
    arriving = [send_along(term, "space", turn + 1) for turn, term in enumerate(theirs)]
    coded = jax.ShapeDtypeStruct((steps + PAD, modes), jnp.int16)
    (crossing,) = call(fold_kernel, (own, *arriving), [coded], [], 8 * steps * modes)
    early = mirror(crossing, "tm", True)
    near, crossing, early = lax.optimization_barrier((near, crossing, early))
    crossing = mirror(crossing, "tm", False)
    rest = gather_far(blocks, "tm")

    theirs = [project_one(near, basis, first, owner, modes, coded) for owner in owners[1:]]
    parts = [send_along(term, "space", turn + 1) for turn, term in enumerate(theirs)]
    own_near, _ = lax.optimization_barrier((near, theirs))
    own = project_one(own_near, basis, first, side, modes, shape((steps, modes)))
    own, chunk_totals, rest = lax.optimization_barrier((own, chunk_totals, rest))
    blocks = jnp.concatenate([blocks] + rest, 0)
    (own,) = call(add_kernel, (own, early, crossing), [shape((steps, modes))], [], EARLY)
    parts.insert(0, own)
    *maps, whole, carry, edge, log_variance = call(
        functools.partial(gains_kernel, tm_count),
        (me, decay, seen, q, r, prior_var[None, :], chunk_totals, blocks),
        [shape(deep)] * 6 + [shape((3,) + deep), shape((2,) + flat), shape((2, tm_count, modes)), shape((steps, modes))],
        [area((2,) + flat, F32), area(deep, F32), area(deep, F32), strips, strips],
        80 * steps * modes,
    )

    coefficients, mean, smooth, ends = call(
        functools.partial(means_kernel, len(parts)),
        (*parts, *maps, carry),
        [shape((steps, modes)), shape(deep), shape(deep), shape((2, modes))],
        [area((2,) + flat, F32), strips],
        12 * steps * modes,
    )
    ends = jnp.broadcast_to(ends[None], (tm_count,) + ends.shape)
    ends = lax.all_to_all(ends, "tm", 0, 0, tiled=True)
    filtered, smoothed = call(
        functools.partial(finish_kernel, tm_count),
        (me, prior_mean[None, :], whole, edge, ends, mean, smooth),
        [shape((steps, modes))] * 2,
        [strips, strips],
        8 * steps * modes,
    )
    return coefficients, filtered, smoothed, log_variance


def solution(mesh):
    return jax.shard_map(
        body,
        mesh=mesh,
        in_specs=(
            P(None, "tm", "space", None),
            P(None, "space", None, None),
            P("tm", "space"),
            P("tm"),
            P("space"),
            P("space"),
            P("space"),
            P("space"),
        ),
        out_specs=(P("tm", "space"), P("tm", "space"), P("tm", "space"), P("tm", "space")),
        check_vma=False,
    )
```

```python
import functools

import jax
import jax.numpy as jnp
from jax import lax
from jax.experimental import pallas as pl
from jax.experimental.pallas import tpu as pltpu
from jax.sharding import PartitionSpec as P

CHUNK = 16
LANES = 128
PAD = 16
STEPS16 = 32512.0
TINY = 1e-30
EARLY = 1 << 34
F32 = jnp.float32
LIMIT = 16 * 1024 * 1024


def swap(block, axis, turn):
    return lax.ppermute(block, axis, [(i, i ^ turn) for i in range(lax.axis_size(axis))])


def inner_size(count):
    group = 1
    while group * group < count:
        group *= 2
    return group if count % group == 0 else count


def gather_near(rows, axis):
    return [rows] + [swap(rows, axis, turn) for turn in range(1, inner_size(lax.axis_size(axis)))]


def gather_far(near, axis):
    count = lax.axis_size(axis)
    return [swap(near, axis, turn) for turn in range(near.shape[0], count, near.shape[0])]


def lanes(ref, strip_ref):
    for m in range(strip_ref.shape[0]):
        strip_ref[m] = ref[:, m * LANES : (m + 1) * LANES]


def unlanes(strip_ref, ref):
    for m in range(strip_ref.shape[0]):
        ref[:, m * LANES : (m + 1) * LANES] = strip_ref[m]


def chunk_rows(strip_ref, i, chunks):
    rows = pl.ds(i, chunks, stride=CHUNK)
    return jnp.concatenate([strip_ref[m, rows, :] for m in range(strip_ref.shape[0])], 1)


def put_rows(strip_ref, i, chunks, value):
    rows = pl.ds(i, chunks, stride=CHUNK)
    for m in range(strip_ref.shape[0]):
        strip_ref[m, rows, :] = value[:, m * LANES : (m + 1) * LANES]


def opened(me_ref, shape):
    rows = lax.broadcasted_iota(jnp.int32, shape, 0)
    return jnp.logical_and(rows == 0, me_ref[0] == 0)


def step_terms(i, chunks, first, q, r, decay_ref, seen_ref):
    d = chunk_rows(decay_ref, i, chunks)
    seen = chunk_rows(seen_ref, i, chunks) > 0.5
    base = q
    if i == 0:
        d = jnp.where(first, 1.0, d)
        base = jnp.where(first, 0.0, q)
    return d, seen, base


def element(d, seen, base, r):
    inverse = 1.0 / (base + r)
    retain = jnp.where(seen, r * inverse, 1.0)
    return retain * d, retain * base, jnp.where(seen, d * d * inverse, 0.0), inverse


def join(early, late):
    lead, spread, weight = early
    lead_late, spread_late, weight_late = late
    factor = 1.0 / (1.0 + spread * weight_late)
    return (
        lead_late * factor * lead,
        lead_late * lead_late * factor * spread + spread_late,
        lead * lead * factor * weight_late + weight,
    )


def totals_kernel(me_ref, decay_in, seen_in, q_ref, r_ref, chunk_ref, block_ref, decay_ref, seen_ref):
    steps, modes = decay_in.shape
    lanes(decay_in, decay_ref)
    lanes(seen_in, seen_ref)
    chunks = steps // CHUNK
    shape = (chunks, modes)
    q = jnp.broadcast_to(q_ref[...], shape)
    r = jnp.broadcast_to(r_ref[...], shape)
    first = opened(me_ref, shape)
    total = None
    for i in range(CHUNK):
        step = element(*step_terms(i, chunks, first, q, r, decay_ref, seen_ref), r)[:3]
        total = step if i == 0 else join(total, step)
    for k in range(3):
        chunk_ref[k] = total[k]
    total = tuple(chunk_ref[k, 0:1, :] for k in range(3))
    for c in range(1, chunks):
        total = join(total, tuple(chunk_ref[k, c : c + 1, :] for k in range(3)))
    for k in range(3):
        block_ref[k : k + 1, :] = total[k]


def gains_kernel(
    count, me_ref, decay_in, seen_in, q_ref, r_ref, prior_ref, chunk_ref, blocks_ref,
    a_ref, b_ref, alpha_ref, beta_ref, keep_ref, lift_ref, whole_ref, carry_ref, edge_ref, log_ref,
    enter_ref, var_ref, info_ref, decay_ref, seen_ref,
):
    steps, modes = decay_in.shape
    lanes(decay_in, decay_ref)
    lanes(seen_in, seen_ref)
    chunks = steps // CHUNK
    shape = (chunks, modes)
    me = me_ref[0]
    q = jnp.broadcast_to(q_ref[...], shape)
    r = jnp.broadcast_to(r_ref[...], shape)
    first = opened(me_ref, shape)

    v = prior_ref[...]
    mine = v
    for j in range(count):
        mine = jnp.where(j == me, v, mine)
        at = lax.bitwise_xor(me, j)
        lead, spread, weight = (blocks_ref[at, k : k + 1, :] for k in range(3))
        along = lead / (1.0 + weight * v)
        edge_ref[0, j : j + 1, :] = along
        v = spread + lead * along * v
    v = mine
    for c in range(chunks):
        enter_ref[0, c : c + 1, :] = v
        lead, spread, weight = (chunk_ref[k, c : c + 1, :] for k in range(3))
        v = spread + lead * lead * v / (1.0 + weight * v)

    info = jnp.zeros((1, modes), F32)
    mine = info
    for j in reversed(range(count)):
        mine = jnp.where(j == me, info, mine)
        at = lax.bitwise_xor(me, j)
        lead, spread, weight = (blocks_ref[at, k : k + 1, :] for k in range(3))
        along = lead / (1.0 + spread * info)
        edge_ref[1, j : j + 1, :] = along
        info = weight + lead * along * info
    info = mine
    for c in reversed(range(chunks)):
        enter_ref[1, c : c + 1, :] = info
        lead, spread, weight = (chunk_ref[k, c : c + 1, :] for k in range(3))
        info = weight + lead * lead * info / (1.0 + spread * info)

    v = enter_ref[0]
    run = None
    for i in range(CHUNK):
        d, seen, base = step_terms(i, chunks, first, q, r, decay_ref, seen_ref)
        ahead = d * d * v + base
        inverse = 1.0 / (ahead + r)
        retain = jnp.where(seen, r * inverse, 1.0)
        v = retain * ahead
        a = retain * d
        run = a if i == 0 else a * run
        a_ref[i] = a
        b_ref[i] = jnp.where(seen, ahead * inverse, 0.0)
        var_ref[i] = v
        whole_ref[0, i] = run
    carry_ref[0] = run

    info = enter_ref[1]
    run = jnp.ones(shape, F32)
    for i in reversed(range(CHUNK)):
        lead, spread, weight, inverse = element(*step_terms(i, chunks, first, q, r, decay_ref, seen_ref), r)
        d, seen, _ = step_terms(i, chunks, first, q, r, decay_ref, seen_ref)
        factor = 1.0 / (1.0 + spread * info)
        alpha = lead * factor
        info_ref[i] = info
        whole_ref[2, i] = run
        alpha_ref[i] = alpha
        beta_ref[i] = jnp.where(seen, d * inverse * factor, 0.0)
        info = weight + lead * alpha * info
        run = alpha * run
    carry_ref[1] = run

    along = jnp.ones((1, modes), F32)
    for c in range(chunks):
        enter_ref[0, c : c + 1, :] = along
        along = along * carry_ref[0, c : c + 1, :]
    along = jnp.ones((1, modes), F32)
    for c in reversed(range(chunks)):
        enter_ref[1, c : c + 1, :] = along
        along = along * carry_ref[1, c : c + 1, :]
    onward = enter_ref[0]
    back = enter_ref[1]
    for i in range(CHUNK):
        v = var_ref[i]
        keep = 1.0 / (1.0 + v * info_ref[i])
        lift = v * keep
        weight = whole_ref[0, i] * onward
        keep_ref[i] = keep
        lift_ref[i] = lift
        whole_ref[0, i] = weight
        whole_ref[1, i] = keep * weight
        whole_ref[2, i] = lift * (whole_ref[2, i] * back)
        put_rows(decay_ref, i, chunks, jnp.log(lift))
    unlanes(decay_ref, log_ref)


def means_kernel(parts, *refs):
    part_refs = refs[:parts]
    a_ref, b_ref, alpha_ref, beta_ref, keep_ref, lift_ref, carry_ref = refs[parts : parts + 7]
    coef_ref, mean_ref, smooth_ref, block_ref, enter_ref, strip_ref = refs[parts + 7 :]
    steps, modes = coef_ref.shape
    chunks = steps // CHUNK
    c = part_refs[0][...]
    for ref in part_refs[1:]:
        c = c + decode(ref)
    coef_ref[...] = c
    lanes(coef_ref, strip_ref)
    f = e = jnp.zeros((chunks, modes), F32)
    for i in range(CHUNK):
        f = a_ref[i] * f + b_ref[i] * chunk_rows(strip_ref, i, chunks)
        k = CHUNK - 1 - i
        e = alpha_ref[k] * e + beta_ref[k] * chunk_rows(strip_ref, k, chunks)
    mean_ref[0] = f
    mean_ref[1] = e
    f = e = jnp.zeros((1, modes), F32)
    for c in range(chunks):
        k = chunks - 1 - c
        enter_ref[0, c : c + 1, :] = f
        enter_ref[1, k : k + 1, :] = e
        f = mean_ref[0, c : c + 1, :] + carry_ref[0, c : c + 1, :] * f
        e = mean_ref[1, k : k + 1, :] + carry_ref[1, k : k + 1, :] * e
    block_ref[0:1, :] = f
    block_ref[1:2, :] = e
    f = enter_ref[0]
    e = enter_ref[1]
    for i in range(CHUNK):
        f = a_ref[i] * f + b_ref[i] * chunk_rows(strip_ref, i, chunks)
        mean_ref[i] = f
    for i in reversed(range(CHUNK)):
        smooth_ref[i] = keep_ref[i] * mean_ref[i] + lift_ref[i] * e
        e = alpha_ref[i] * e + beta_ref[i] * chunk_rows(strip_ref, i, chunks)


def finish_kernel(count, me_ref, prior_ref, whole_ref, edge_ref, blocks_ref, mean_ref, smooth_ref, out_mean_ref, out_smooth_ref, mean_strip_ref, smooth_strip_ref):
    steps, modes = out_mean_ref.shape
    chunks = steps // CHUNK
    me = me_ref[0]
    f = prior_ref[...]
    e = jnp.zeros((1, modes), F32)
    for j in range(count - 1):
        f = jnp.where(j < me, blocks_ref[j, 0:1, :] + edge_ref[0, j : j + 1, :] * f, f)
        k = count - 1 - j
        e = jnp.where(k > me, blocks_ref[k, 1:2, :] + edge_ref[1, k : k + 1, :] * e, e)
    f = jnp.broadcast_to(f, (chunks, modes))
    e = jnp.broadcast_to(e, (chunks, modes))
    for i in range(CHUNK):
        put_rows(mean_strip_ref, i, chunks, mean_ref[i] + whole_ref[0, i] * f)
        put_rows(smooth_strip_ref, i, chunks, smooth_ref[i] + whole_ref[1, i] * f + whole_ref[2, i] * e)
    unlanes(mean_strip_ref, out_mean_ref)
    unlanes(smooth_strip_ref, out_smooth_ref)


def encode(values, ref):
    steps = values.shape[0]
    top = jnp.max(jnp.abs(values), axis=0, keepdims=True)
    power = jnp.floor(jnp.log2(jnp.maximum(top, TINY))) + 1.0
    coded = jnp.floor(values * (jnp.exp2(-power) * STEPS16) + 0.5)
    ref[0:steps, :] = coded.astype(jnp.int32).astype(jnp.int16)
    power = jnp.broadcast_to(power, (PAD, power.shape[1]))
    ref[steps : steps + PAD, :] = power.astype(jnp.int32).astype(jnp.int16)


def decode(ref):
    steps = ref.shape[0] - PAD
    power = ref[steps : steps + PAD, :].astype(jnp.int32).astype(F32)[0:1, :]
    return ref[0:steps, :].astype(jnp.int32).astype(F32) * (jnp.exp2(power) * (1.0 / STEPS16))


def project_kernel(held, at_ref, slab_ref, basis_ref, own_ref, *refs):
    owners = at_ref.shape[0] - 1
    coded_refs = refs[: owners - 1]
    basis_area, sum_area, basis_sems, *refs = refs[owners - 1 :]
    slab_area = slab_ref if held else refs[0]
    count = slab_ref.shape[0]
    modes = own_ref.shape[1]
    copies = []
    for g in range(count):
        source = g if held else (g + count // 2) % count
        pair = [pltpu.make_async_copy(basis_ref.at[at_ref[0] + source], basis_area.at[g], basis_sems.at[g])]
        if not held:
            pair.append(pltpu.make_async_copy(slab_ref.at[g], slab_area.at[g], refs[1].at[g]))
        copies.append(pair)
    for pair in copies:
        for copy in pair:
            copy.start()
    for g in range(count):
        for copy in copies[g]:
            copy.wait()
        for turn in range(owners):
            columns = pl.ds(pl.multiple_of(at_ref[1 + turn] * modes, LANES), modes)
            term = jnp.dot(slab_area[g], basis_area[g, :, columns], preferred_element_type=F32)
            sum_area[turn] = term if g == 0 else sum_area[turn] + term
    own_ref[...] = sum_area[0]
    for turn in range(1, owners):
        encode(sum_area[turn], coded_refs[turn - 1])


def project(slabs, basis, first, owners, modes, held=False):
    count, steps, cells = slabs.shape
    others = len(owners) - 1
    own, *coded = pl.pallas_call(
        functools.partial(project_kernel, held),
        in_specs=[
            pl.BlockSpec(memory_space=pltpu.SMEM),
            pl.BlockSpec(memory_space=pltpu.VMEM if held else pl.ANY),
            pl.BlockSpec(memory_space=pl.ANY),
        ],
        out_specs=[pl.BlockSpec(memory_space=pltpu.VMEM)] * (1 + others),
        out_shape=[jax.ShapeDtypeStruct((steps, modes), F32)]
        + [jax.ShapeDtypeStruct((steps + PAD, modes), jnp.int16)] * others,
        scratch_shapes=[
            pltpu.VMEM((count,) + basis.shape[1:], basis.dtype),
            pltpu.VMEM((1 + others, steps, modes), F32),
            pltpu.SemaphoreType.DMA((count,)),
        ]
        + ([] if held else [pltpu.VMEM(slabs.shape, slabs.dtype), pltpu.SemaphoreType.DMA((count,))]),
        compiler_params=pltpu.CompilerParams(vmem_limit_bytes=(36 if held else 60) * LIMIT // 16),
        cost_estimate=pl.CostEstimate(
            flops=2 * count * steps * cells * modes * (1 + others),
            bytes_accessed=2 * count * cells * (steps + modes * (1 + others)) + 4 * steps * modes,
            transcendentals=0,
        ),
    )(jnp.stack([first] + owners), slabs, basis)
    return own, coded


def add_kernel(own_ref, early_ref, late_ref, out_ref):
    out_ref[...] = own_ref[...] + decode(early_ref) + decode(late_ref)


def fold_kernel(own_ref, *refs):
    total = own_ref[...]
    for ref in refs[:-1]:
        total = total + decode(ref)
    encode(total, refs[-1])


def call(kernel, inputs, outputs, scratch, flops):
    smem = pl.BlockSpec(memory_space=pltpu.SMEM)
    vmem = pl.BlockSpec(memory_space=pltpu.VMEM)
    moved = sum(4 * x.size for x in inputs) + sum(4 * x.size for x in outputs)
    return pl.pallas_call(
        kernel,
        in_specs=[smem if x.dtype == jnp.int32 else vmem for x in inputs],
        out_specs=[vmem] * len(outputs),
        out_shape=outputs,
        scratch_shapes=scratch,
        compiler_params=pltpu.CompilerParams(vmem_limit_bytes=LIMIT),
        cost_estimate=pl.CostEstimate(flops=flops, bytes_accessed=moved, transcendentals=0),
    )(*inputs)


def mirror(block, axis, inner):
    count = lax.axis_size(axis)
    quarter = count // 4
    places = [i for i in range(count) if (quarter <= i < 3 * quarter) == inner]
    return lax.ppermute(block, axis, [(i, i ^ (3 * quarter)) for i in places])


def send_along(term, axis, turn):
    count = lax.axis_size(axis)
    return lax.ppermute(term, axis, [(i, (i + turn) % count) for i in range(count)])


def body(observations, pod_basis, decay, step_mask, process_var, obs_var, prior_mean, prior_var):
    tm_count = lax.axis_size("tm")
    space_count = lax.axis_size("space")
    steps, modes = decay.shape
    chunks = steps // CHUNK
    rank = lax.axis_index("tm").astype(jnp.int32)
    me = rank.reshape(1)
    side = lax.axis_index("space").astype(jnp.int32)
    shape = functools.partial(jax.ShapeDtypeStruct, dtype=F32)
    area = pltpu.VMEM
    group = tm_count // 2
    groups = [[half * group + i for i in range(group)] for half in range(2)]
    half = rank // group

    seen = jnp.broadcast_to(step_mask.astype(F32)[:, None], (steps, modes))
    q, r = process_var[None, :], obs_var[None, :]
    flat = (chunks, modes)
    deep = (CHUNK, chunks, modes)
    strips = area((modes // LANES, steps, LANES), F32)
    slabs = observations.reshape(2, group, steps, observations.shape[3])
    basis = pod_basis.reshape(tm_count, -1, pod_basis.shape[3])
    first = half * group
    owners = [lax.rem(side + turn, space_count) for turn in range(space_count)]
    far = lax.dynamic_index_in_dim(slabs, 1 - half, 0, keepdims=False)
    far, q = lax.optimization_barrier((far, q))
    turned = [places[group // 2 :] + places[: group // 2] for places in groups]
    far = lax.all_to_all(far, "tm", 0, 0, axis_index_groups=turned, tiled=True)
    chunk_totals, block_totals = call(
        totals_kernel, (me, decay, seen, q, r), [shape((3,) + flat), shape((3, modes))], [strips] * 2, 40 * steps * modes
    )
    block_totals, own_half = lax.optimization_barrier((block_totals, half))
    near = lax.dynamic_index_in_dim(slabs, own_half, 0, keepdims=False)
    blocks = jnp.stack(gather_near(block_totals, "tm"))
    far, near, blocks = lax.optimization_barrier((far, near, blocks))
    near = lax.all_to_all(near, "tm", 0, 0, axis_index_groups=groups, tiled=True)

    own, theirs = project(far, basis, first, owners, modes)
    arriving = [send_along(term, "space", turn + 1) for turn, term in enumerate(theirs)]
    coded = jax.ShapeDtypeStruct((steps + PAD, modes), jnp.int16)
    (crossing,) = call(fold_kernel, (own, *arriving), [coded], [], 8 * steps * modes)
    early = mirror(crossing, "tm", True)
    near, crossing, early = lax.optimization_barrier((near, crossing, early))
    crossing = mirror(crossing, "tm", False)
    rest = gather_far(blocks, "tm")

    own, theirs = project(near, basis, first, owners, modes, True)
    parts = [send_along(term, "space", turn + 1) for turn, term in enumerate(theirs)]
    own, chunk_totals, rest = lax.optimization_barrier((own, chunk_totals, rest))
    blocks = jnp.concatenate([blocks] + rest, 0)
    (own,) = call(add_kernel, (own, early, crossing), [shape((steps, modes))], [], EARLY)
    parts.insert(0, own)
    *maps, whole, carry, edge, log_variance = call(
        functools.partial(gains_kernel, tm_count),
        (me, decay, seen, q, r, prior_var[None, :], chunk_totals, blocks),
        [shape(deep)] * 6 + [shape((3,) + deep), shape((2,) + flat), shape((2, tm_count, modes)), shape((steps, modes))],
        [area((2,) + flat, F32), area(deep, F32), area(deep, F32), strips, strips],
        80 * steps * modes,
    )

    coefficients, mean, smooth, ends = call(
        functools.partial(means_kernel, len(parts)),
        (*parts, *maps, carry),
        [shape((steps, modes)), shape(deep), shape(deep), shape((2, modes))],
        [area((2,) + flat, F32), strips],
        12 * steps * modes,
    )
    ends = jnp.broadcast_to(ends[None], (tm_count,) + ends.shape)
    ends = lax.all_to_all(ends, "tm", 0, 0, tiled=True)
    filtered, smoothed = call(
        functools.partial(finish_kernel, tm_count),
        (me, prior_mean[None, :], whole, edge, ends, mean, smooth),
        [shape((steps, modes))] * 2,
        [strips, strips],
        8 * steps * modes,
    )
    return coefficients, filtered, smoothed, log_variance


def solution(mesh):
    return jax.shard_map(
        body,
        mesh=mesh,
        in_specs=(
            P(None, "tm", "space", None),
            P(None, "space", None, None),
            P("tm", "space"),
            P("tm"),
            P("space"),
            P("space"),
            P("space"),
            P("space"),
        ),
        out_specs=(P("tm", "space"), P("tm", "space"), P("tm", "space"), P("tm", "space")),
        check_vma=False,
    )
```
